32 devices in a mesh: dp: 8 (over z, y), tensor: 4 (over x, core).
Axes of the slice: x: 2, y: 2, z: 4, core: 2. Of those that a mesh axis runs over, the one named last changes fastest.
Arguments:
- inputs: bfloat16 [65536, 1024], P(('dp', 'tensor')), may hold values from -6 to 6
- query_weight: bfloat16 [1024, 1024], P('tensor'), may hold values from -0.1875 to 0.1875
- key_weight: bfloat16 [1024, 1024], P('tensor'), may hold values from -0.1875 to 0.1875
- value_weight: bfloat16 [1024, 1024], P('tensor'), may hold values from -0.1875 to 0.1875
- output_weight: bfloat16 [1024, 1024], P('tensor'), may hold values from -3 to 3
- inner_weight: bfloat16 [1024, 4096], P(None, 'tensor'), may hold values from -0.1875 to 0.1875
- inner_bias: float32 [4096], P('tensor'), may hold values from -3 to 3
- outer_weight: bfloat16 [4096, 1024], P('tensor'), may hold values from -0.09375 to 0.09375
- outer_bias: float32 [1024], replicated, may hold values from -3 to 3
- first_gain: float32 [1024], replicated, may hold values from 0.1 to 1.9
- first_shift: float32 [1024], replicated, may hold values from -2 to 2
- second_gain: float32 [1024], replicated, may hold values from 0.1 to 1.9
- second_shift: float32 [1024], replicated, may hold values from -2 to 2
- item_lengths: int32 [16], P('dp'), may hold values from 1024 to 4096, as said below
- key_mask: int32 [65536], P('dp'), may hold values from 0 to 1, as said below
- random_blocks: int32 [16, 16, 64, 3], P('dp', 'tensor'), may hold values from 0 to 63
- cotangent: bfloat16 [65536, 1024], P(('dp', 'tensor')), may hold values from -6 to 6
Outputs:
- outputs: bfloat16 [65536, 1024], P(('dp', 'tensor'))
- input_grad: float32 [65536, 1024], P(('dp', 'tensor'))
- query_weight_grad: float32 [1024, 1024], P('tensor')
- key_weight_grad: float32 [1024, 1024], P('tensor')
- value_weight_grad: float32 [1024, 1024], P('tensor')
- output_weight_grad: float32 [1024, 1024], P('tensor')
- inner_weight_grad: float32 [1024, 4096], P(None, 'tensor')
- inner_bias_grad: float32 [4096], P('tensor')
- outer_weight_grad: float32 [4096, 1024], P('tensor')
- outer_bias_grad: float32 [1024], replicated
- first_gain_grad: float32 [1024], replicated
- first_shift_grad: float32 [1024], replicated
- second_gain_grad: float32 [1024], replicated
- second_shift_grad: float32 [1024], replicated
The draws below stay inside these ranges and needn't reach their ends.
Inputs may be any that keep to these rules, and one draw needn't show every extreme that they name: `item_lengths`: multiples of 64; in every draw some item uses all 4096 rows. `key_mask`: the first row of every item is 1.
All inputs are finite; a program needn't handle non-finite values.
Results may differ from the reference program's by a relative error of at most 0.012.
The reference program's roundings to bfloat16 on the way count: a program that leaves them out, or rounds other values in their place, can miss the bound.
Values may be sent and summed in bfloat16 or wider, within the bound.
No kernel may reach another device: no remote copies, remote signals or barrier semaphores. Data moves between devices by JAX's collectives and lax.ppermute only.
A program may use at most 384 MiB of HBM per device.

```python
import jax
import jax.numpy as jnp
from jax import lax

D = 1024
H = 16
FF = 4096
BLK = 64
RANDOM = 3
NB = 64
LOW_BLOCKS = 16
ITEMS = 16
TOKENS = 65536


def draw_item_lengths(key, part):
    key = jax.random.fold_in(key, 11)
    first_key, second_key = jax.random.split(key)
    attempts = jax.random.randint(first_key, (3, ITEMS), 0, NB - LOW_BLOCKS + 1)
    blocks = LOW_BLOCKS + jnp.min(attempts, axis=0)
    picked = jax.random.randint(second_key, (), 0, ITEMS)
    blocks = jnp.where(jnp.arange(ITEMS) == picked, NB, blocks)
    return (blocks * BLK).astype(jnp.int32)


def draw_key_mask(key, part):
    key = jax.random.fold_in(key, 23)
    levels = jax.random.randint(key, (TOKENS,), 0, 8)
    leading = jnp.arange(TOKENS) % (NB * BLK) == 0
    return jnp.where(leading | (levels != 0), 1, 0).astype(jnp.int32)


def touch_ends(values, key, smallest, top_value):
    dims = values.shape
    place = [jax.random.randint(jax.random.fold_in(key, axis), (), 0, dims[axis]) for axis in range(len(dims))]
    values = values.at[tuple(place)].set(smallest)
    longest = dims.index(max(dims))
    place[longest] = (place[longest] + 1) % dims[longest]
    return values.at[tuple(place)].set(top_value)


def level_of(key, dims, cuts, smallest, largest):
    factor_of = 1.0
    for axis_at, parts in cuts:
        heights = jax.random.uniform(jax.random.fold_in(jax.random.fold_in(key, 6), axis_at), (parts,), jnp.float32, smallest / len(cuts), largest / len(cuts))
        factor_of = factor_of * jnp.repeat(jnp.exp(heights), dims[axis_at] // parts).reshape((-1,) + (1,) * (len(dims) - 1 - axis_at))
    return factor_of


def scatter_about(stream_key, shape, scale, most, cuts=(), held_as=jnp.bfloat16):
    values = scale * jax.random.normal(stream_key, shape, jnp.float32)
    if cuts:
        values = values * level_of(stream_key, shape, cuts, -0.22, 0.18)
    return jnp.clip(values, -most, most).astype(held_as)


def setup_inputs(seed: int = 0) -> dict:
    streams_of = jax.random.split(jax.random.key(seed), 18)
    inputs = scatter_about(streams_of[0], (TOKENS, D), 1.0, 6.0, ((0, 32),))
    query_weight = scatter_about(streams_of[1], (D, D), D ** -0.5, 0.1875, ((0, 4),))
    key_weight = scatter_about(streams_of[2], (D, D), D ** -0.5, 0.1875, ((0, 4),))
    value_weight = scatter_about(streams_of[3], (D, D), D ** -0.5, 0.1875, ((0, 4),))
    output_weight = scatter_about(streams_of[4], (D, D), (max(D // 256, 1)) ** -0.5, 3.0, ((0, 4),))
    inner_weight = scatter_about(streams_of[5], (D, FF), D ** -0.5, 0.1875, ((1, 4),))
    inner_bias = scatter_about(streams_of[6], (FF,), 0.5, 3.0, ((0, 4),), jnp.float32)
    outer_weight = scatter_about(streams_of[7], (FF, D), FF ** -0.5, 0.09375, ((0, 4),))
    outer_bias = scatter_about(streams_of[8], (D,), 0.5, 3.0, (), jnp.float32)
    first_gain = jnp.clip(1.0 + 0.18 * jax.random.normal(streams_of[9], (D,), jnp.float32), 0.1, 1.9)
    first_shift = scatter_about(streams_of[10], (D,), 0.3, 2.0, (), jnp.float32)
    second_gain = jnp.clip(1.0 + 0.18 * jax.random.normal(streams_of[11], (D,), jnp.float32), 0.1, 1.9)
    second_shift = scatter_about(streams_of[12], (D,), 0.3, 2.0, (), jnp.float32)
    item_lengths = draw_item_lengths(jax.random.fold_in(streams_of[17], 71), 0)
    key_mask = draw_key_mask(jax.random.fold_in(streams_of[17], 71), 0)
    random_blocks = touch_ends(jax.random.randint(streams_of[15], (ITEMS, H, NB, RANDOM), 0, NB), jax.random.fold_in(streams_of[15], 1), 0, NB - 1).astype(jnp.int32)
    cotangent = scatter_about(streams_of[16], (TOKENS, D), 1.0, 6.0, ((0, 32),))
    return dict(inputs=inputs, query_weight=query_weight, key_weight=key_weight, value_weight=value_weight, output_weight=output_weight, inner_weight=inner_weight, inner_bias=inner_bias, outer_weight=outer_weight, outer_bias=outer_bias, first_gain=first_gain, first_shift=first_shift, second_gain=second_gain, second_shift=second_shift, item_lengths=item_lengths, key_mask=key_mask, random_blocks=random_blocks, cotangent=cotangent)


EPSILON = 1e-05
MASKED = -1e+30
HIGHEST = lax.Precision.HIGHEST

@jax.custom_vjp
def low(v):
    return lax.optimization_barrier(v.astype(jnp.bfloat16)).astype(jnp.float32)

@jax.custom_vjp
def low_back(v):
    return v

def low_keep(v):
    return (low(v), None)

def low_pass(kept, grad):
    return (grad,)

def back_keep(v):
    return (v, None)

def back_low(kept, grad):
    return (low(grad),)
low.defvjp(low_keep, low_pass)
low_back.defvjp(back_keep, back_low)

def matmul_high(left, right):
    return jnp.dot(left, right, precision=HIGHEST)

def layer_norm(resid, gain, shift):
    center = lax.optimization_barrier(jnp.mean(resid, axis=-1, keepdims=True))
    deviation = resid - center
    spread = lax.optimization_barrier(jnp.mean(deviation * deviation, axis=-1, keepdims=True))
    return deviation * lax.rsqrt(spread + EPSILON) * gain + shift

def softmax_rows(scores):
    row_max = lax.optimization_barrier(jnp.max(scores, axis=-1, keepdims=True))
    shifted = jnp.exp(scores - row_max)
    return shifted / lax.optimization_barrier(jnp.sum(shifted, axis=-1, keepdims=True))

def block_lists(blocks_used, random_pick):
    block_count = random_pick.shape[0]
    places = jnp.arange(block_count, dtype=jnp.int32)[:, None]
    fixed_cols = jnp.zeros_like(places)
    chosen = jnp.concatenate([places - 1, places, places + 1, fixed_cols, fixed_cols + blocks_used - 1, random_pick % blocks_used], axis=1)
    inside = (chosen >= 0) & (chosen < blocks_used)
    slot_count = chosen.shape[1]
    before = jnp.arange(slot_count)[:, None] < jnp.arange(slot_count)[None, :]
    repeated = jnp.any((chosen[:, :, None] == chosen[:, None, :]) & inside[:, :, None] & before[None], axis=1)
    return (jnp.clip(chosen, 0, block_count - 1), inside & jnp.logical_not(repeated))

def head_attention(query_rows, key_rows, value_rows, random_pick, blocks_used, key_ok):
    block_count = random_pick.shape[0]
    item_span, head_size = query_rows.shape
    block_len = item_span // block_count
    factor = head_size ** (-0.5)
    chosen, usable = block_lists(blocks_used, random_pick)
    query_blocks = query_rows.reshape(block_count, block_len, head_size)
    key_blocks = key_rows.reshape(block_count, block_len, head_size)[chosen].reshape(block_count, -1, head_size)
    value_blocks = value_rows.reshape(block_count, block_len, head_size)[chosen].reshape(block_count, -1, head_size)
    allowed = (usable[:, :, None] & key_ok.reshape(block_count, block_len)[chosen]).reshape(block_count, 1, -1)
    scores = low_back(jnp.einsum('nqd,nkd->nqk', query_blocks, key_blocks, precision=HIGHEST) * factor)
    probs = softmax_rows(jnp.where(allowed, scores, MASKED))
    attended = jnp.einsum('nqk,nkd->nqd', low(probs), value_blocks, precision=HIGHEST).reshape(item_span, head_size)
    offset = (blocks_used - 1) * block_len
    global_rows = jnp.concatenate([query_rows[:block_len], lax.dynamic_slice_in_dim(query_rows, offset, block_len, 0)], axis=0)
    global_scores = low_back(matmul_high(global_rows, key_rows.T) * factor)
    global_probs = softmax_rows(jnp.where(key_ok[None, :], global_scores, MASKED))
    global_out = matmul_high(low(global_probs), value_rows)
    attended = attended.at[:block_len].set(global_out[:block_len])
    return lax.dynamic_update_slice_in_dim(attended, global_out[block_len:], offset, 0)

def layer(resid, params, length, key_flags, random_pick):
    query_weight, key_weight, value_weight, output_weight, inner_weight, inner_bias, outer_weight, outer_bias, first_gain, first_shift, second_gain, second_shift = params
    item_span = resid.shape[0]
    head_count = random_pick.shape[0]
    places = jnp.arange(item_span, dtype=jnp.int32)
    item_live = places < length
    key_ok = item_live & (key_flags == 1)
    blocks_used = length // (item_span // random_pick.shape[1])
    first_normed = low(layer_norm(resid, first_gain, first_shift))

    def project(weight):
        projected = low_back(low(matmul_high(first_normed, weight.T)))
        return projected.reshape(item_span, head_count, -1).transpose(1, 0, 2)
    per_head = jax.checkpoint(lambda group_rows: head_attention(group_rows[0], group_rows[1], group_rows[2], group_rows[3], blocks_used, key_ok))
    attended = lax.map(per_head, (project(query_weight), project(key_weight), project(value_weight), random_pick))
    merged = attended.transpose(1, 0, 2).reshape(item_span, -1)
    merged = low_back(low(jnp.where(item_live[:, None], merged, jnp.zeros_like(merged))))
    middle = resid + low_back(matmul_high(merged, output_weight))
    second_normed = low(layer_norm(middle, second_gain, second_shift))
    inner_pre = low_back(matmul_high(second_normed, inner_weight) + inner_bias)
    hidden_act = low(jax.nn.gelu(inner_pre, approximate=True))
    return middle + matmul_high(hidden_act, outer_weight) + outer_bias

def reference(inputs, query_weight, key_weight, value_weight, output_weight, inner_weight, inner_bias, outer_weight, outer_bias, first_gain, first_shift, second_gain, second_shift, item_lengths, key_mask, random_blocks, cotangent):
    params = tuple((weight.astype(jnp.float32) for weight in (query_weight, key_weight, value_weight, output_weight, inner_weight, inner_bias, outer_weight, outer_bias, first_gain, first_shift, second_gain, second_shift)))
    item_count = item_lengths.shape[0]
    item_span = inputs.shape[0] // item_count
    model_width = inputs.shape[1]
    resid_items = inputs.astype(jnp.float32).reshape(item_count, item_span, model_width)
    grad_items = cotangent.astype(jnp.float32).reshape(item_count, item_span, model_width)
    flag_items = key_mask.reshape(item_count, item_span)

    def one_step(totals, one_item):
        resid, grad_out, length, key_flags, random_pick = one_item
        result, pullback = jax.vjp(lambda here, weights: layer(here, weights, length, key_flags, random_pick), resid, params)
        resid_grad, weight_grads = pullback(grad_out)
        return (jax.tree.map(jnp.add, totals, weight_grads), (result.astype(jnp.bfloat16), resid_grad))
    zero_grads = jax.tree.map(jnp.zeros_like, params)
    totals, (results, resid_grads) = lax.scan(one_step, zero_grads, (resid_items, grad_items, item_lengths, flag_items, random_blocks))
    return (results.reshape(inputs.shape), resid_grads.reshape(inputs.shape), totals[0], totals[1], totals[2], totals[3], totals[4], totals[5], totals[6], totals[7], totals[8], totals[9], totals[10], totals[11])
```

```python
import functools

import jax
import jax.numpy as jnp
from jax import lax
from jax.experimental import pallas as pl
from jax.experimental.pallas import tpu as pltpu
from jax.sharding import PartitionSpec as P

EPSILON = 1e-05
MASKED = -1e30
LOG2E = 1.4426950408889634
SHARED = 5
KEY_CHUNK = 512
MEGA = 2**20


def contract_rows(left, right):
    return lax.dot_general(
        left, right, (((0,), (0,)), ((), ())), preferred_element_type=jnp.float32
    )


def contract_cols(left, right):
    return lax.dot_general(
        left, right, (((1,), (1,)), ((), ())), preferred_element_type=jnp.float32
    )


def matmul(left, right):
    return lax.dot_general(
        left, right, (((1,), (0,)), ((), ())), preferred_element_type=jnp.float32
    )


def block_lists(blocks_used, random_pick):
    block_count = random_pick.shape[0]
    places = jnp.arange(block_count, dtype=jnp.int32)[:, None]
    fixed_cols = jnp.zeros_like(places)
    chosen = jnp.concatenate(
        [
            places - 1,
            places,
            places + 1,
            fixed_cols,
            fixed_cols + blocks_used - 1,
            random_pick % blocks_used,
        ],
        axis=1,
    )
    inside = (chosen >= 0) & (chosen < blocks_used)
    slot_count = chosen.shape[1]
    before = jnp.arange(slot_count)[:, None] < jnp.arange(slot_count)[None, :]
    repeated = jnp.any(
        (chosen[:, :, None] == chosen[:, None, :]) & inside[:, :, None] & before[None], axis=1
    )
    return (jnp.clip(chosen, 0, block_count - 1), inside & jnp.logical_not(repeated))


def norm_rows(resid, gain, shift):
    center = jnp.mean(resid, axis=1, keepdims=True)
    deviation = resid - center
    inverse = lax.rsqrt(jnp.mean(deviation * deviation, axis=1, keepdims=True) + EPSILON)
    unit_rows = deviation * inverse
    normed = (unit_rows * gain + shift).astype(jnp.bfloat16)
    return (normed, unit_rows, inverse)


def norm_back(grad_normed, unit_rows, inverse, gain):
    scaled = grad_normed * gain
    plain_mean = jnp.mean(scaled, axis=1, keepdims=True)
    cross_mean = jnp.mean(scaled * unit_rows, axis=1, keepdims=True)
    resid_grad = inverse * (scaled - plain_mean - unit_rows * cross_mean)
    return (resid_grad, jnp.sum(grad_normed * unit_rows, axis=0), jnp.sum(grad_normed, axis=0))


class Shape:
    def __init__(self, span, heads, head_size, blocks, slots):
        self.span, self.heads, self.head_size, self.blocks, self.slots = (
            span,
            heads,
            head_size,
            blocks,
            slots,
        )
        self.length = span // blocks
        self.lanes = heads * head_size
        self.columns = heads * self.length
        self.wide = max(1, min(heads, 128 // head_size))
        self.tile = self.wide * head_size
        self.chunk = min(KEY_CHUNK, span)
        self.bias_lanes = min(128, self.columns)


def rows_of(index, length):
    return pl.ds(pl.multiple_of(index * length, length), length)


def spread_heads(block, sh):
    lane = lax.broadcasted_iota(jnp.int32, block.shape, 1) // sh.head_size
    zero = jnp.zeros_like(block)
    return jnp.concatenate([jnp.where(lane == h, block, zero) for h in range(sh.heads)], axis=0)


def pick_heads(stacked, sh):
    lane = lax.broadcasted_iota(jnp.int32, (sh.length, sh.lanes), 1) // sh.head_size
    out = stacked[: sh.length]
    for h in range(1, sh.heads):
        out = jnp.where(lane == h, stacked[h * sh.length : (h + 1) * sh.length], out)
    return out


def mixed_slot(load, idx, j, s, sh):
    cols = []
    for t in range(sh.heads // sh.wide):
        out = None
        for i in range(sh.wide):
            at = idx[((t * sh.wide + i) * sh.blocks + j) * sh.slots + s]
            piece = load(rows_of(at, sh.length), t)
            if i == 0:
                out = piece
            else:
                lane = lax.broadcasted_iota(jnp.int32, piece.shape, 1) // sh.head_size
                out = jnp.where(lane == i, piece, out)
        cols.append(out)
    return cols[0] if len(cols) == 1 else jnp.concatenate(cols, axis=1)


def gather_rows(ref, first, idx, j, sh):
    parts = [
        ref[rows_of(idx[j * sh.slots + s], sh.length), first : first + sh.lanes]
        for s in range(SHARED)
    ]

    def load(rows, t):
        return ref[rows, first + t * sh.tile : first + (t + 1) * sh.tile]

    for s in range(SHARED, sh.slots):
        parts.append(mixed_slot(load, idx, j, s, sh))
    return jnp.concatenate(parts, axis=0)


def widen(bias, sh):
    reps = sh.columns // sh.bias_lanes
    return bias if reps == 1 else jnp.concatenate([bias] * reps, axis=1)


def gather_bias(ref, idx, j, sh):
    parts = [
        widen(ref[rows_of(idx[j * sh.slots + s], sh.length), : sh.bias_lanes], sh)
        for s in range(SHARED)
    ]

    def load(rows, t):
        return ref[rows, : sh.bias_lanes]

    for s in range(SHARED, sh.slots):
        parts.append(mixed_slot(load, idx, j, s, sh))
    return jnp.concatenate(parts, axis=0)


def scatter_rows(ref, value, idx, j, sh):
    length, tile = sh.length, sh.tile
    for s in range(SHARED):
        ref[rows_of(idx[j * sh.slots + s], length), :] += value[s * length : (s + 1) * length]
    for s in range(SHARED, sh.slots):
        for h in range(sh.heads):
            t, i = h // sh.wide, h % sh.wide
            at = rows_of(idx[(h * sh.blocks + j) * sh.slots + s], length)
            piece = value[s * length : (s + 1) * length, t * tile : (t + 1) * tile]
            if sh.wide > 1:
                lane = lax.broadcasted_iota(jnp.int32, piece.shape, 1) // sh.head_size
                piece = jnp.where(lane == i, piece, 0.0)
            ref[at, t * tile : (t + 1) * tile] += piece


def each_block(count, unroll, block):
    def many(i, carry):
        for u in range(unroll):
            block(1 + i * unroll + u)
        return carry

    lax.fori_loop(0, count // unroll, many, 0)

    def one(j, carry):
        block(j)
        return carry

    lax.fori_loop(1 + count // unroll * unroll, 1 + count, one, 0)


def forward_kernel(sh, pieces, unroll, used, member, idx, bidx, *refs):
    packed, bias_ref = refs[:pieces], refs[pieces]
    outs = refs[pieces + 1 : 2 * pieces + 1]
    rows, o_scr, s_scr, sems = refs[2 * pieces + 1 :]
    c = used[0]
    scale = sh.head_size ** (-0.5) * LOG2E
    rows_each = sh.span // pieces
    query, key, value = 0, sh.lanes, 2 * sh.lanes

    def place(r):
        return rows_of(lax.rem(member[0] + r, pieces), rows_each)

    loads = [pltpu.make_async_copy(packed[r], rows.at[place(r)], sems.at[r]) for r in range(pieces)]
    for copy in loads:
        copy.start()
    o_scr[...] = jnp.zeros_like(o_scr)
    for copy in loads:
        copy.wait()

    def block(j):
        at = rows_of(j, sh.length)
        q_all = spread_heads(rows[at, query : query + sh.lanes], sh)
        scores = contract_cols(gather_rows(rows, key, idx, j, sh), q_all) * scale
        scores = scores + gather_bias(bias_ref, bidx, j, sh)
        shifted = jnp.exp2(scores - jnp.max(scores, axis=0, keepdims=True))
        inverse = 1.0 / jnp.sum(shifted, axis=0, keepdims=True)
        probs = (shifted * inverse).astype(jnp.bfloat16)
        out = pick_heads(contract_rows(probs, gather_rows(rows, value, idx, j, sh)), sh)
        o_scr[at, :] = out.astype(o_scr.dtype)

    each_block(c - 2, unroll, block)

    chunks = pl.cdiv(c * sh.length, sh.chunk)
    line = (1, sh.columns)
    for j in (0, c - 1):
        at = rows_of(j, sh.length)
        q_all = spread_heads(rows[at, query : query + sh.lanes], sh)

        def first(i, top):
            keys = rows_of(i, sh.chunk)
            scores = contract_cols(rows[keys, key : key + sh.lanes], q_all) * scale
            scores = scores + widen(bias_ref[keys, : sh.bias_lanes], sh)
            s_scr[keys, :] = scores
            return jnp.maximum(top, jnp.max(scores, axis=0, keepdims=True))

        top = lax.fori_loop(0, chunks, first, jnp.full(line, MASKED, jnp.float32))

        def second(i, total):
            keys = rows_of(i, sh.chunk)
            shifted = jnp.exp2(s_scr[keys, :] - top)
            s_scr[keys, :] = shifted
            return total + jnp.sum(shifted, axis=0, keepdims=True)

        inverse = 1.0 / lax.fori_loop(0, chunks, second, jnp.zeros(line, jnp.float32))

        def third(i, total):
            keys = rows_of(i, sh.chunk)
            probs = (s_scr[keys, :] * inverse).astype(jnp.bfloat16)
            return total + contract_rows(probs, rows[keys, value : value + sh.lanes])

        total = lax.fori_loop(0, chunks, third, jnp.zeros((sh.columns, sh.lanes), jnp.float32))
        o_scr[at, :] = pick_heads(total, sh).astype(o_scr.dtype)

    stores = [
        pltpu.make_async_copy(o_scr.at[place(r)], outs[r], sems.at[pieces + r])
        for r in range(pieces)
    ]
    for copy in stores:
        copy.start()
    for copy in stores:
        copy.wait()


def backward_kernel(sh, pieces, unroll, used, member, idx, bidx, *refs):
    packed, tops, bias_ref = refs[:pieces], refs[pieces : 2 * pieces], refs[2 * pieces]
    outs = refs[2 * pieces + 1 : 3 * pieces + 1]
    rows, grads, d_scr, ka_scr, va_scr, s_scr, p_scr, sems = refs[3 * pieces + 1 :]
    c = used[0]
    factor = sh.head_size ** (-0.5)
    scale = factor * LOG2E
    rows_each = sh.span // pieces
    query, key, value = 0, sh.lanes, 2 * sh.lanes

    def place(r):
        return rows_of(lax.rem(member[0] + r, pieces), rows_each)

    loads = [pltpu.make_async_copy(packed[r], rows.at[place(r)], sems.at[r]) for r in range(pieces)]
    loads += [
        pltpu.make_async_copy(tops[r], grads.at[place(r)], sems.at[pieces + r])
        for r in range(pieces)
    ]
    for copy in loads:
        copy.start()
    d_scr[:, : sh.lanes] = jnp.zeros((sh.span, sh.lanes), d_scr.dtype)
    ka_scr[...] = jnp.zeros_like(ka_scr)
    va_scr[...] = jnp.zeros_like(va_scr)
    for copy in loads:
        copy.wait()

    def block(j):
        at = rows_of(j, sh.length)
        q_all = spread_heads(rows[at, query : query + sh.lanes], sh)
        g_all = spread_heads(grads[at, :], sh)
        k_all = gather_rows(rows, key, idx, j, sh)
        scores = contract_cols(k_all, q_all) * scale + gather_bias(bias_ref, bidx, j, sh)
        prob_grad = contract_cols(gather_rows(rows, value, idx, j, sh), g_all)
        shifted = jnp.exp2(scores - jnp.max(scores, axis=0, keepdims=True))
        probs = shifted * (1.0 / jnp.sum(shifted, axis=0, keepdims=True))
        delta = jnp.sum(probs * prob_grad, axis=0, keepdims=True)
        score_grad = (probs * (prob_grad - delta)).astype(jnp.bfloat16)
        query_grad = pick_heads(contract_rows(score_grad, k_all), sh) * factor
        d_scr[at, : sh.lanes] = query_grad.astype(d_scr.dtype)
        scatter_rows(ka_scr, matmul(score_grad, q_all), idx, j, sh)
        scatter_rows(va_scr, matmul(probs.astype(jnp.bfloat16), g_all), idx, j, sh)

    each_block(c - 2, unroll, block)

    chunks = pl.cdiv(c * sh.length, sh.chunk)
    line = (1, sh.columns)
    for j in (0, c - 1):
        at = rows_of(j, sh.length)
        q_all = spread_heads(rows[at, query : query + sh.lanes], sh)
        g_all = spread_heads(grads[at, :], sh)

        def first(i, carry):
            top, total, cross = carry
            keys = rows_of(i, sh.chunk)
            scores = contract_cols(rows[keys, key : key + sh.lanes], q_all) * scale
            scores = scores + widen(bias_ref[keys, : sh.bias_lanes], sh)
            prob_grad = contract_cols(rows[keys, value : value + sh.lanes], g_all)
            s_scr[keys, :] = scores
            p_scr[keys, :] = prob_grad
            higher = jnp.maximum(top, jnp.max(scores, axis=0, keepdims=True))
            shifted = jnp.exp2(scores - higher)
            fade = jnp.exp2(top - higher)
            return (
                higher,
                total * fade + jnp.sum(shifted, axis=0, keepdims=True),
                cross * fade + jnp.sum(shifted * prob_grad, axis=0, keepdims=True),
            )

        zero = jnp.zeros(line, jnp.float32)
        top, total, cross = lax.fori_loop(
            0, chunks, first, (jnp.full(line, MASKED, jnp.float32), zero, zero)
        )
        inverse = 1.0 / total
        delta = cross * inverse

        def second(i, total):
            keys = rows_of(i, sh.chunk)
            probs = jnp.exp2(s_scr[keys, :] - top) * inverse
            score_grad = (probs * (p_scr[keys, :] - delta)).astype(jnp.bfloat16)
            ka_scr[keys, :] += matmul(score_grad, q_all)
            va_scr[keys, :] += matmul(probs.astype(jnp.bfloat16), g_all)
            return total + contract_rows(score_grad, rows[keys, key : key + sh.lanes])

        total = lax.fori_loop(0, chunks, second, jnp.zeros((sh.columns, sh.lanes), jnp.float32))
        d_scr[at, : sh.lanes] = (pick_heads(total, sh) * factor).astype(d_scr.dtype)

    d_scr[:, key : key + sh.lanes] = (ka_scr[...] * factor).astype(d_scr.dtype)
    d_scr[:, value : value + sh.lanes] = va_scr[...].astype(d_scr.dtype)
    stores = [
        pltpu.make_async_copy(d_scr.at[place(r)], outs[r], sems.at[2 * pieces + r])
        for r in range(pieces)
    ]
    for copy in stores:
        copy.start()
    for copy in stores:
        copy.wait()


ANYWHERE = pl.BlockSpec(memory_space=pl.ANY)
ON_CHIP = pl.BlockSpec(memory_space=pltpu.VMEM)
SCALARS = pl.BlockSpec(memory_space=pltpu.SMEM)


def attend_cost(sh, products):
    flops = products * 2 * (sh.blocks + 2 * sh.blocks // sh.slots) * sh.length * sh.slots
    flops *= sh.length * sh.head_size * sh.heads * 4
    return pl.CostEstimate(flops=flops, bytes_accessed=16 * sh.span * sh.lanes, transcendentals=0)


def attend_forward(sh, packed, lists, unroll=4):
    pieces = len(packed)
    used, member, idx, bidx, bias = lists
    rows_each = sh.span // pieces
    return pl.pallas_call(
        functools.partial(forward_kernel, sh, pieces, unroll),
        in_specs=[SCALARS] * 4 + [ANYWHERE] * pieces + [ON_CHIP],
        out_specs=[ANYWHERE] * pieces,
        out_shape=[jax.ShapeDtypeStruct((rows_each, sh.lanes), jnp.bfloat16)] * pieces,
        scratch_shapes=[
            pltpu.VMEM((sh.span, 3 * sh.lanes), jnp.bfloat16),
            pltpu.VMEM((sh.span, sh.lanes), jnp.bfloat16),
            pltpu.VMEM((sh.span, sh.columns), jnp.float32),
            pltpu.SemaphoreType.DMA((2 * pieces,)),
        ],
        compiler_params=pltpu.CompilerParams(vmem_limit_bytes=40 * MEGA),
        cost_estimate=attend_cost(sh, 2),
        name="attend_forward",
    )(used, member, idx, bidx, *packed, bias)


def attend_backward(sh, packed, tops, lists, unroll=2):
    pieces = len(packed)
    used, member, idx, bidx, bias = lists
    rows_each = sh.span // pieces
    return pl.pallas_call(
        functools.partial(backward_kernel, sh, pieces, unroll),
        in_specs=[SCALARS] * 4 + [ANYWHERE] * (2 * pieces) + [ON_CHIP],
        out_specs=[ANYWHERE] * pieces,
        out_shape=[jax.ShapeDtypeStruct((rows_each, 3 * sh.lanes), jnp.bfloat16)] * pieces,
        scratch_shapes=[
            pltpu.VMEM((sh.span, 3 * sh.lanes), jnp.bfloat16),
            pltpu.VMEM((sh.span, sh.lanes), jnp.bfloat16),
            pltpu.VMEM((sh.span, 3 * sh.lanes), jnp.bfloat16),
            pltpu.VMEM((sh.span, sh.lanes), jnp.float32),
            pltpu.VMEM((sh.span, sh.lanes), jnp.float32),
            pltpu.VMEM((sh.span, sh.columns), jnp.float32),
            pltpu.VMEM((sh.span, sh.columns), jnp.float32),
            pltpu.SemaphoreType.DMA((3 * pieces,)),
        ],
        compiler_params=pltpu.CompilerParams(vmem_limit_bytes=56 * MEGA),
        cost_estimate=attend_cost(sh, 5),
        name="attend_backward",
    )(used, member, idx, bidx, *packed, *tops, bias)


def low(values):
    return values.astype(jnp.bfloat16)


def full(values):
    return values.astype(jnp.float32)


def swap(values, bit):
    size = lax.axis_size("dp")
    return lax.ppermute(values, "dp", [(i, i ^ bit) for i in range(size)])


def halve(values, bit):
    half = values.shape[0] // 2
    upper = (lax.axis_index("dp") // bit) % 2
    mine = lax.dynamic_slice_in_dim(values, upper * half, half, 0)
    theirs = lax.dynamic_slice_in_dim(values, (1 - upper) * half, half, 0)
    return low(full(mine) + full(swap(theirs, bit)))


def double(values, bit):
    upper = (lax.axis_index("dp") // bit) % 2
    other = swap(values, bit)
    return jnp.where(
        upper == 0,
        jnp.concatenate([values, other], axis=0),
        jnp.concatenate([other, values], axis=0),
    )


def sum_groups(values):
    bits = [1 << i for i in range(lax.axis_size("dp").bit_length() - 1)]
    orders = [bits, bits[1:2] + bits[:1] + bits[2:]]
    part = values.shape[0] // len(orders)
    sums = []
    for i, order in enumerate(orders):
        total = low(values[i * part : (i + 1) * part])
        for bit in order:
            total = halve(total, bit)
        for bit in order[::-1]:
            total = double(total, bit)
        sums.append(total)
    return jnp.concatenate(sums, axis=0).astype(jnp.float32)


def per_device(
    inputs,
    query_weight,
    key_weight,
    value_weight,
    output_weight,
    inner_weight,
    inner_bias,
    outer_weight,
    outer_bias,
    first_gain,
    first_shift,
    second_gain,
    second_shift,
    item_lengths,
    key_mask,
    random_blocks,
    cotangent,
):
    tensor = lax.axis_size("tensor")
    items = item_lengths.shape[0]
    local_rows, model = inputs.shape
    span = local_rows * tensor // items
    members = tensor // items
    place = lax.axis_index("tensor")
    item, member = place // members, place % members
    heads, blocks = random_blocks.shape[1], random_blocks.shape[2]
    lanes = query_weight.shape[0]
    length = span // blocks
    sh = Shape(span, heads, lanes // heads, blocks, SHARED + random_blocks.shape[3])

    def from_item(values, step):
        if step % items == 0:
            return values
        pairs = [
            (t, (t // members - step) % items * members + t % members) for t in range(tensor)
        ]
        return lax.ppermute(values, "tensor", pairs)

    def from_member(values, step):
        if step % members == 0:
            return values
        pairs = [
            (t, t // members * members + (t % members - step) % members) for t in range(tensor)
        ]
        return lax.ppermute(values, "tensor", pairs)

    joint = jnp.concatenate([query_weight, key_weight, value_weight], axis=0)
    joint_item = [from_item(joint, s) for s in range(items)]
    out_item = [from_item(output_weight, s) for s in range(items)]
    inner_item = [from_item(inner_weight, s) for s in range(items)]
    outer_item = [from_item(outer_weight, s) for s in range(items)]
    order = [(s, r) for s in range(items) for r in range(members)]

    def gather(parts):
        return [from_member(parts[s], -r) for s, r in order]

    resid = inputs.astype(jnp.float32)
    grad_top = cotangent.astype(jnp.float32)
    first_own, first_unit, first_inverse = norm_rows(resid, first_gain, first_shift)
    first_all = [from_member(first_own, r) for r in range(members)]
    packed = [
        [low(contract_cols(first_all[r], joint_item[s])) for r in range(members)]
        for s in range(items)
    ]

    used = lax.dynamic_index_in_dim(item_lengths, item, 0, False) // length
    flags = lax.dynamic_index_in_dim(key_mask.reshape(items, span), item, 0, False)
    key_ok = (jnp.arange(span, dtype=jnp.int32) < used * length) & (flags == 1)
    bias = jnp.where(jnp.concatenate([key_ok, jnp.zeros((length,), bool)]), 0.0, MASKED)
    bias = jnp.broadcast_to(bias.astype(jnp.float32)[:, None], (span + length, 128))

    def lists_of(s):
        picks = from_item(
            lax.dynamic_index_in_dim(random_blocks, (item - s) % items, 0, False), s
        )
        chosen, usable = jax.vmap(lambda pick: block_lists(used, pick))(picks)
        marked = jnp.where(usable, chosen, blocks)
        return (used.reshape(1), member.reshape(1), chosen.reshape(-1), marked.reshape(-1), bias)

    lists = [lists_of(s) for s in range(items)]

    merged = []
    for s in range(items):
        outs = attend_forward(sh, packed[s], lists[s])
        merged += [from_member(outs[r], -r) for r in range(members)]
    merged = jnp.concatenate(merged, axis=1)

    out_full = jnp.concatenate(gather(out_item), axis=0)
    inner_full = jnp.concatenate(gather(inner_item), axis=1)
    outer_full = jnp.concatenate(gather(outer_item), axis=0)
    biases = lax.all_gather(inner_bias, "tensor", axis=0)
    spots = jnp.stack([(item + s) % items * members + (member - r) % members for s, r in order])
    bias_full = jnp.concatenate(
        [lax.dynamic_index_in_dim(biases, spots[i], 0, False) for i in range(tensor)]
    )

    middle = resid + matmul(merged, out_full)
    second_own, second_unit, second_inverse = norm_rows(middle, second_gain, second_shift)
    inner_pre = matmul(second_own, inner_full) + bias_full
    hidden_act = low(jax.nn.gelu(inner_pre, approximate=True))
    outputs = low(middle + matmul(hidden_act, outer_full) + outer_bias)

    outer_part = contract_rows(hidden_act, cotangent)
    hidden_grad = contract_cols(cotangent, outer_full)
    gelu_pull = jax.vjp(lambda pre_act: jax.nn.gelu(pre_act, approximate=True), inner_pre)[1]
    inner_grad = low(gelu_pull(hidden_grad)[0])
    inner_part = contract_rows(inner_grad, second_own)
    bias_part = jnp.sum(inner_grad.astype(jnp.float32), axis=0)
    second_grad = contract_cols(inner_grad, inner_full)
    second_resid, second_gain_grad, second_shift_grad = norm_back(
        second_grad, second_unit, second_inverse, second_gain
    )
    middle_grad = grad_top + second_resid
    branch = low(middle_grad)
    output_part = contract_rows(merged, branch)
    merged_grad = low(contract_cols(branch, out_full))

    tops = [[None] * members for _ in range(items)]
    for i, (s, r) in enumerate(order):
        tops[s][r] = from_member(merged_grad[:, i * lanes : (i + 1) * lanes], r)
    packed_grad = [None] * items
    for s in range(items - 1, -1, -1):
        packed_grad[s] = attend_backward(sh, packed[s], tops[s], lists[s])

    def collect(parts):
        totals = []
        for s in range(items):
            total = parts[s * members]
            for r in range(1, members):
                total = total + full(from_member(low(parts[s * members + r]), r))
            totals.append(total)
        return collect_items(totals)

    def collect_items(totals):
        total = totals[0]
        for s in range(1, items):
            total = total + full(from_item(low(totals[s]), -s))
        return total

    def split(values):
        return [values[i * lanes_of : (i + 1) * lanes_of] for i in range(tensor)]

    lanes_of = outer_weight.shape[0]
    outer_grad = sum_groups(collect(split(outer_part)))
    inner_grad_sum = sum_groups(collect(split(inner_part))).T
    lanes_of = lanes
    output_grad = collect(split(output_part))

    joint_parts = []
    for s in range(items):
        total = contract_rows(packed_grad[s][0], first_all[0])
        for r in range(1, members):
            total = total + contract_rows(packed_grad[s][r], first_all[r])
        joint_parts.append(total)
    joint_grad = collect_items(joint_parts)
    attention_grad = sum_groups(jnp.concatenate([joint_grad, output_grad], axis=0))

    back = [from_member(packed_grad[s][r], -r) for s, r in order]
    joint_full = jnp.concatenate(gather(joint_item), axis=0)
    first_grad = matmul(jnp.concatenate(back, axis=1), joint_full)
    first_resid, first_gain_grad, first_shift_grad = norm_back(
        first_grad, first_unit, first_inverse, first_gain
    )
    input_grad = middle_grad + first_resid

    bias_parts = bias_part.reshape(tensor, -1)
    bias_own = jnp.zeros_like(bias_parts)
    for i in range(tensor):
        bias_own = lax.dynamic_update_index_in_dim(bias_own, bias_parts[i], spots[i], 0)
    vectors = lax.psum(
        jnp.concatenate(
            [
                jnp.stack(
                    [
                        jnp.sum(grad_top, axis=0),
                        first_gain_grad,
                        first_shift_grad,
                        second_gain_grad,
                        second_shift_grad,
                    ]
                ).reshape(-1),
                bias_own.reshape(-1),
            ]
        ),
        ("dp", "tensor"),
    )
    small = vectors[: 5 * model].reshape(5, model)
    bias_sum = lax.dynamic_index_in_dim(vectors[5 * model :].reshape(tensor, -1), place, 0, False)
    return (
        outputs,
        input_grad,
        attention_grad[:lanes],
        attention_grad[lanes : 2 * lanes],
        attention_grad[2 * lanes : 3 * lanes],
        attention_grad[3 * lanes :],
        inner_grad_sum,
        bias_sum,
        outer_grad,
        small[0],
        small[1],
        small[2],
        small[3],
        small[4],
    )


def solution(mesh):
    placed = (
        P(("dp", "tensor"), None),
        P("tensor", None),
        P("tensor", None),
        P("tensor", None),
        P("tensor", None),
        P(None, "tensor"),
        P("tensor"),
        P("tensor", None),
        P(),
        P(),
        P(),
        P(),
        P(),
        P("dp"),
        P("dp"),
        P("dp", "tensor", None, None),
        P(("dp", "tensor"), None),
    )
    return jax.shard_map(
        per_device,
        mesh=mesh,
        in_specs=placed,
        out_specs=(
            P(("dp", "tensor"), None),
            P(("dp", "tensor"), None),
            P("tensor", None),
            P("tensor", None),
            P("tensor", None),
            P("tensor", None),
            P(None, "tensor"),
            P("tensor"),
            P("tensor", None),
            P(),
            P(),
            P(),
            P(),
            P(),
        ),
        check_vma=False,
    )
```

```python
import functools

import jax
import jax.numpy as jnp
from jax import lax
from jax.experimental import pallas as pl
from jax.experimental.pallas import tpu as pltpu
from jax.sharding import PartitionSpec as P

EPSILON = 1e-05
MASKED = -1e30
LOG2E = 1.4426950408889634
SHARED = 5
KEY_CHUNK = 512
MEGA = 2**20
ROW_TILE = 256
LAST_PARTS = 2
BACK_PARTS = 2


def contract_rows(left, right):
    return lax.dot_general(
        left, right, (((0,), (0,)), ((), ())), preferred_element_type=jnp.float32
    )


def contract_cols(left, right):
    return lax.dot_general(
        left, right, (((1,), (1,)), ((), ())), preferred_element_type=jnp.float32
    )


def matmul(left, right):
    return lax.dot_general(
        left, right, (((1,), (0,)), ((), ())), preferred_element_type=jnp.float32
    )


def block_lists(blocks_used, random_pick):
    block_count = random_pick.shape[0]
    places = jnp.arange(block_count, dtype=jnp.int32)[:, None]
    fixed_cols = jnp.zeros_like(places)
    chosen = jnp.concatenate(
        [
            places - 1,
            places,
            places + 1,
            fixed_cols,
            fixed_cols + blocks_used - 1,
            random_pick % blocks_used,
        ],
        axis=1,
    )
    inside = (chosen >= 0) & (chosen < blocks_used)
    slot_count = chosen.shape[1]
    before = jnp.arange(slot_count)[:, None] < jnp.arange(slot_count)[None, :]
    repeated = jnp.any(
        (chosen[:, :, None] == chosen[:, None, :]) & inside[:, :, None] & before[None], axis=1
    )
    return (jnp.clip(chosen, 0, block_count - 1), inside & jnp.logical_not(repeated))


def low(values):
    return values.astype(jnp.bfloat16)


def full(values):
    return values.astype(jnp.float32)


class Shape:
    def __init__(self, span, heads, head_size, blocks, slots):
        self.span, self.heads, self.head_size, self.blocks, self.slots = (
            span,
            heads,
            head_size,
            blocks,
            slots,
        )
        self.length = span // blocks
        self.lanes = heads * head_size
        self.columns = heads * self.length
        self.wide = max(1, min(heads, 128 // head_size))
        self.tile = self.wide * head_size
        self.chunk = min(KEY_CHUNK, span)
        self.bias_lanes = min(128, self.columns)


def rows_of(index, length):
    return pl.ds(pl.multiple_of(index * length, length), length)


def spread_heads(block, sh):
    lane = lax.broadcasted_iota(jnp.int32, block.shape, 1) // sh.head_size
    zero = jnp.zeros_like(block)
    return jnp.concatenate([jnp.where(lane == h, block, zero) for h in range(sh.heads)], axis=0)


def pick_heads(stacked, sh):
    lane = lax.broadcasted_iota(jnp.int32, (sh.length, sh.lanes), 1) // sh.head_size
    out = stacked[: sh.length]
    for h in range(1, sh.heads):
        out = jnp.where(lane == h, stacked[h * sh.length : (h + 1) * sh.length], out)
    return out


def mixed_slot(load, idx, j, s, sh):
    cols = []
    for t in range(sh.heads // sh.wide):
        out = None
        for i in range(sh.wide):
            at = idx[((t * sh.wide + i) * sh.blocks + j) * sh.slots + s]
            piece = load(rows_of(at, sh.length), t)
            if i == 0:
                out = piece
            else:
                lane = lax.broadcasted_iota(jnp.int32, piece.shape, 1) // sh.head_size
                out = jnp.where(lane == i, piece, out)
        cols.append(out)
    return cols[0] if len(cols) == 1 else jnp.concatenate(cols, axis=1)


def gather_rows(ref, first, idx, j, sh):
    parts = [
        ref[rows_of(idx[j * sh.slots + s], sh.length), first : first + sh.lanes]
        for s in range(SHARED)
    ]

    def load(rows, t):
        return ref[rows, first + t * sh.tile : first + (t + 1) * sh.tile]

    for s in range(SHARED, sh.slots):
        parts.append(mixed_slot(load, idx, j, s, sh))
    return jnp.concatenate(parts, axis=0)


def widen(bias, sh):
    reps = sh.columns // sh.bias_lanes
    return bias if reps == 1 else jnp.concatenate([bias] * reps, axis=1)


def gather_bias(ref, idx, j, sh):
    parts = [
        widen(ref[rows_of(idx[j * sh.slots + s], sh.length), : sh.bias_lanes], sh)
        for s in range(SHARED)
    ]

    def load(rows, t):
        return ref[rows, : sh.bias_lanes]

    for s in range(SHARED, sh.slots):
        parts.append(mixed_slot(load, idx, j, s, sh))
    return jnp.concatenate(parts, axis=0)


def split_rows(dot, left, right, cuts):
    edges = [0, *cuts, left.shape[0]]
    return jnp.concatenate([dot(left[a:b], right) for a, b in zip(edges, edges[1:])], axis=0)


def each_block(first, count, unroll, blocks_from):
    def many(i, carry):
        blocks_from(first + i * unroll, unroll)
        return carry

    lax.fori_loop(0, count // unroll, many, 0)

    def one(j, carry):
        blocks_from(j, 1)
        return carry

    lax.fori_loop(first + count // unroll * unroll, first + count, one, 0)


def forward_kernel(sh, pieces, unroll, used, member, idx, bidx, *refs):
    packed, bias_ref = refs[:pieces], refs[pieces]
    outs, log_ref = refs[pieces + 1 : 2 * pieces + 1], refs[2 * pieces + 1]
    rows, o_scr, s_scr, sems = refs[2 * pieces + 2 :]
    c = used[0]
    scale = sh.head_size ** (-0.5) * LOG2E
    rows_each = sh.span // pieces
    query, key, value = 0, sh.lanes, 2 * sh.lanes

    def place(r):
        return rows_of(lax.rem(member[0] + r, pieces), rows_each)

    loads = [pltpu.make_async_copy(packed[r], rows.at[place(r)], sems.at[r]) for r in range(pieces)]
    for copy in loads:
        copy.start()
    o_scr[...] = jnp.zeros_like(o_scr)
    log_ref[...] = jnp.zeros_like(log_ref)
    for copy in loads:
        copy.wait()

    def block(j):
        at = rows_of(j, sh.length)
        q_all = spread_heads(rows[at, query : query + sh.lanes], sh)
        scores = contract_cols(gather_rows(rows, key, idx, j, sh), q_all) * scale
        scores = scores + gather_bias(bias_ref, bidx, j, sh)
        top = jnp.max(scores, axis=0, keepdims=True)
        shifted = jnp.exp2(scores - top)
        total = jnp.sum(shifted, axis=0, keepdims=True)
        log_ref[pl.ds(j, 1), :] = top + jnp.log2(total)
        probs = low(shifted * (1.0 / total))
        out = pick_heads(contract_rows(probs, gather_rows(rows, value, idx, j, sh)), sh)
        o_scr[at, :] = low(out)

    def blocks_from(j, count):
        for u in range(count):
            block(j + u)

    each_block(1, c - 2, unroll, blocks_from)

    chunks = pl.cdiv(c * sh.length, sh.chunk)
    row = (1, sh.columns)
    for j in (0, c - 1):
        at = rows_of(j, sh.length)
        q_all = spread_heads(rows[at, query : query + sh.lanes], sh)

        def first(i, top):
            keys = rows_of(i, sh.chunk)
            scores = contract_cols(rows[keys, key : key + sh.lanes], q_all) * scale
            scores = scores + widen(bias_ref[keys, : sh.bias_lanes], sh)
            s_scr[keys, :] = scores
            return jnp.maximum(top, jnp.max(scores, axis=0, keepdims=True))

        top = lax.fori_loop(0, chunks, first, jnp.full(row, MASKED, jnp.float32))

        def second(i, total):
            keys = rows_of(i, sh.chunk)
            shifted = jnp.exp2(s_scr[keys, :] - top)
            s_scr[keys, :] = shifted
            return total + jnp.sum(shifted, axis=0, keepdims=True)

        total = lax.fori_loop(0, chunks, second, jnp.zeros(row, jnp.float32))
        log_ref[pl.ds(j, 1), :] = top + jnp.log2(total)
        inverse = 1.0 / total

        def third(i, out):
            keys = rows_of(i, sh.chunk)
            probs = low(s_scr[keys, :] * inverse)
            return out + contract_rows(probs, rows[keys, value : value + sh.lanes])

        out = lax.fori_loop(0, chunks, third, jnp.zeros((sh.columns, sh.lanes), jnp.float32))
        o_scr[at, :] = low(pick_heads(out, sh))

    stores = [
        pltpu.make_async_copy(o_scr.at[place(r)], outs[r], sems.at[pieces + r])
        for r in range(pieces)
    ]
    for copy in stores:
        copy.start()
    for copy in stores:
        copy.wait()


def backward_kernel(sh, pieces, unroll, part, used, member, idx, bidx, *refs):
    part, parts = part
    packed, tops, made = refs[:pieces], refs[pieces : 2 * pieces], refs[2 * pieces : 3 * pieces]
    refs = refs[3 * pieces :]
    (bias_ref, log_ref), refs = refs[:2], refs[2:]
    carried, refs = refs[: pieces * (part > 0)], refs[pieces * (part > 0) :]
    outs, refs = refs[:pieces], refs[pieces:]
    rows, grads, merged, d_scr, ka_scr, va_scr, sems = refs
    c = used[0]
    factor = sh.head_size ** (-0.5)
    scale = factor * LOG2E
    rows_each = sh.span // pieces
    query, key, value = 0, sh.lanes, 2 * sh.lanes
    length, slots = sh.length, sh.slots
    keys_each = slots * length

    def place(r):
        return rows_of(lax.rem(member[0] + r, pieces), rows_each)

    loads = []
    for n, (sources, target) in enumerate(((packed, rows), (tops, grads), (made, merged))):
        for r in range(pieces):
            copy = pltpu.make_async_copy(
                sources[r], target.at[place(r)], sems.at[n * pieces + r]
            )
            loads.append(copy)
            copy.start()
    for r in range(pieces if part else 0):
        copy = pltpu.make_async_copy(
            carried[r], d_scr.at[place(r)], sems.at[4 * pieces + r]
        )
        loads.append(copy)
        copy.start()
    if not part:
        d_scr[:, : sh.lanes] = jnp.zeros((sh.span, sh.lanes), d_scr.dtype)
        ka_scr[...] = jnp.zeros_like(ka_scr)
        va_scr[...] = jnp.zeros_like(va_scr)
    for copy in loads:
        copy.wait()
    if part:
        ka_scr[...] = full(d_scr[:, key : key + sh.lanes]) * (1.0 / factor)
        va_scr[...] = full(d_scr[:, value : value + sh.lanes])

    def equal_rows(products):
        row = lax.broadcasted_iota(jnp.int32, products.shape, 0)
        column = lax.broadcasted_iota(jnp.int32, products.shape, 1)
        return jnp.sum(
            jnp.where(column % length == row, products, 0.0), axis=0, keepdims=True
        )

    def block(j):
        at = rows_of(j, length)
        q_all = spread_heads(rows[at, query : query + sh.lanes], sh)
        g_all = spread_heads(grads[at, :], sh)
        k_all = gather_rows(rows, key, idx, j, sh)
        v_all = jnp.concatenate([gather_rows(rows, value, idx, j, sh), merged[at, :]], axis=0)
        cuts = [keys_each // 2]
        scores = split_rows(contract_cols, k_all, q_all, cuts) * scale
        prob_grad = split_rows(contract_cols, v_all, g_all, cuts)
        delta = equal_rows(prob_grad[keys_each:])
        scores = scores + gather_bias(bias_ref, bidx, j, sh)
        probs = jnp.exp2(scores - log_ref[pl.ds(j, 1), :])
        score_grad = low(probs * (prob_grad[:keys_each] - delta))
        query_grad = pick_heads(contract_rows(score_grad, k_all), sh) * factor
        d_scr[at, : sh.lanes] = low(query_grad)
        return (
            split_rows(matmul, score_grad, q_all, cuts),
            split_rows(matmul, low(probs), g_all, cuts),
        )

    def random_add(ref, j, value):
        tile = sh.tile
        for s in range(SHARED, slots):
            for h in range(sh.heads):
                t, i = h // sh.wide, h % sh.wide
                at = rows_of(idx[(h * sh.blocks + j) * slots + s], length)
                piece = value[s * length : (s + 1) * length, t * tile : (t + 1) * tile]
                if sh.wide > 1:
                    lane = lax.broadcasted_iota(jnp.int32, piece.shape, 1) // sh.head_size
                    piece = jnp.where(lane == i, piece, 0.0)
                ref[at, t * tile : (t + 1) * tile] += piece

    def blocks_from(j, count):
        gained = [block(j + u) for u in range(count)]
        for which, ref in ((0, ka_scr), (1, va_scr)):

            def slot(u, s):
                return gained[u][which][s * length : (s + 1) * length]

            for n in range(count + 2):
                total = None
                for u in range(count):
                    if 0 <= n - u <= 2:
                        total = slot(u, n - u) if total is None else total + slot(u, n - u)
                ref[rows_of(j - 1 + n, length), :] += total
            for s, target in ((3, 0), (4, c - 1)):
                total = slot(0, s)
                for u in range(1, count):
                    total = total + slot(u, s)
                ref[rows_of(target, length), :] += total
            for u in range(count):
                random_add(ref, j + u, gained[u][which])

    steps = (c - 2) // unroll
    begin, end = steps * part // parts * unroll, steps * (part + 1) // parts * unroll
    if part == parts - 1:
        end = c - 2
    each_block(1 + begin, end - begin, unroll, blocks_from)

    chunks = pl.cdiv(c * length, sh.chunk)
    for j in (0, c - 1)[2 * part // parts : 2 * (part + 1) // parts]:
        at = rows_of(j, length)
        q_all = spread_heads(rows[at, query : query + sh.lanes], sh)
        g_all = spread_heads(grads[at, :], sh)
        delta = equal_rows(contract_cols(merged[at, :], g_all))
        log_row = log_ref[pl.ds(j, 1), :]

        def chunk(i, total):
            keys = rows_of(i, sh.chunk)
            k_all = rows[keys, key : key + sh.lanes]
            scores = contract_cols(k_all, q_all) * scale
            scores = scores + widen(bias_ref[keys, : sh.bias_lanes], sh)
            probs = jnp.exp2(scores - log_row)
            prob_grad = contract_cols(rows[keys, value : value + sh.lanes], g_all)
            score_grad = low(probs * (prob_grad - delta))
            ka_scr[keys, :] += matmul(score_grad, q_all)
            va_scr[keys, :] += matmul(low(probs), g_all)
            return total + contract_rows(score_grad, k_all)

        total = lax.fori_loop(0, chunks, chunk, jnp.zeros((sh.columns, sh.lanes), jnp.float32))
        d_scr[at, : sh.lanes] = low(pick_heads(total, sh) * factor)

    d_scr[:, key : key + sh.lanes] = low(ka_scr[...] * factor)
    d_scr[:, value : value + sh.lanes] = low(va_scr[...])
    stores = [
        pltpu.make_async_copy(d_scr.at[place(r)], outs[r], sems.at[3 * pieces + r])
        for r in range(pieces)
    ]
    for copy in stores:
        copy.start()
    for copy in stores:
        copy.wait()


ANYWHERE = pl.BlockSpec(memory_space=pl.ANY)
ON_CHIP = pl.BlockSpec(memory_space=pltpu.VMEM)
SCALARS = pl.BlockSpec(memory_space=pltpu.SMEM)


def cost(flops, accessed=10**6):
    return pl.CostEstimate(flops=int(flops), bytes_accessed=int(accessed), transcendentals=0)


def attend_cost(sh, weight):
    return cost(weight * sh.blocks * sh.slots * sh.length * sh.columns * sh.lanes)


def attend_forward(sh, packed, lists, weight=16, unroll=6):
    pieces = len(packed)
    used, member, idx, bidx, bias = lists
    rows_each = sh.span // pieces
    outs = pl.pallas_call(
        functools.partial(forward_kernel, sh, pieces, unroll),
        in_specs=[SCALARS] * 4 + [ANYWHERE] * pieces + [ON_CHIP],
        out_specs=[ANYWHERE] * pieces + [ON_CHIP],
        out_shape=[jax.ShapeDtypeStruct((rows_each, sh.lanes), jnp.bfloat16)] * pieces
        + [jax.ShapeDtypeStruct((sh.blocks, sh.columns), jnp.float32)],
        scratch_shapes=[
            pltpu.VMEM((sh.span, 3 * sh.lanes), jnp.bfloat16),
            pltpu.VMEM((sh.span, sh.lanes), jnp.bfloat16),
            pltpu.VMEM((sh.span, sh.columns), jnp.float32),
            pltpu.SemaphoreType.DMA((2 * pieces,)),
        ],
        compiler_params=pltpu.CompilerParams(vmem_limit_bytes=40 * MEGA),
        cost_estimate=attend_cost(sh, weight),
        name="attend_forward",
    )(used, member, idx, bidx, *packed, bias)
    return outs[:pieces], outs[pieces]


def attend_backward(sh, packed, tops, made, log_rows, lists, part=(0, 1), carried=(), unroll=2):
    pieces = len(packed)
    used, member, idx, bidx, bias = lists
    rows_each = sh.span // pieces
    return pl.pallas_call(
        functools.partial(backward_kernel, sh, pieces, unroll, part),
        in_specs=[SCALARS] * 4
        + [ANYWHERE] * (3 * pieces)
        + [ON_CHIP] * 2
        + [ANYWHERE] * len(carried),
        out_specs=[ANYWHERE] * pieces,
        out_shape=[jax.ShapeDtypeStruct((rows_each, 3 * sh.lanes), jnp.bfloat16)] * pieces,
        scratch_shapes=[
            pltpu.VMEM((sh.span, 3 * sh.lanes), jnp.bfloat16),
            pltpu.VMEM((sh.span, sh.lanes), jnp.bfloat16),
            pltpu.VMEM((sh.span, sh.lanes), jnp.bfloat16),
            pltpu.VMEM((sh.span, 3 * sh.lanes), jnp.bfloat16),
            pltpu.VMEM((sh.span, sh.lanes), jnp.float32),
            pltpu.VMEM((sh.span, sh.lanes), jnp.float32),
            pltpu.SemaphoreType.DMA((5 * pieces,)),
        ],
        compiler_params=pltpu.CompilerParams(vmem_limit_bytes=36 * MEGA),
        cost_estimate=attend_cost(sh, 32 // part[1]),
        name="attend_backward",
    )(used, member, idx, bidx, *packed, *tops, *made, bias, log_rows, *carried)


GELU_A = (2 / 3.141592653589793) ** 0.5
GELU_B = GELU_A * 0.044715
ONES = 16


def gelu_both(pre):
    square = pre * pre
    turn = jnp.tanh(pre * (GELU_A + GELU_B * square))
    half = 0.5 + 0.5 * turn
    act = pre * half
    slope = half + act * (1.0 - turn) * (GELU_A + 3.0 * GELU_B * square)
    return act, slope


def unit_of(rows):
    center = jnp.mean(rows, axis=1, keepdims=True)
    deviation = rows - center
    inverse = lax.rsqrt(jnp.mean(deviation * deviation, axis=1, keepdims=True) + EPSILON)
    return deviation * inverse, inverse


def norm_grad(grad_normed, unit, inverse, gain):
    scaled = grad_normed * gain
    plain_mean = jnp.mean(scaled, axis=1, keepdims=True)
    cross_mean = jnp.mean(scaled * unit, axis=1, keepdims=True)
    return inverse * (scaled - plain_mean - unit * cross_mean)


def column_sum(values):
    return jnp.sum(values, axis=0, keepdims=True)


def take(refs, count):
    return refs[:count], refs[count:]


def tiled(tile, cols, first=0):
    return pl.BlockSpec((tile, cols), lambda i: (first + i, 0))


def line(cols):
    return pl.BlockSpec((1, cols), lambda i: (0, 0))


def line_out(cols):
    return jax.ShapeDtypeStruct((1, cols), jnp.float32)


def rows_out(rows, cols, dtype=jnp.bfloat16):
    return jax.ShapeDtypeStruct((rows, cols), dtype)


def middle_kernel(count, outs_count, head, tail, offsets, *refs):
    (cot_ref, bias_ref), refs = take(refs, 2)
    if head:
        (resid_ref, outer_bias_ref, gain_ref, shift_ref), refs = take(refs, 4)
        merged, refs = take(refs, outs_count)
    else:
        (second_in, total_in, back_in), refs = take(refs, 3)
    if tail:
        (middle_in, gain_in), refs = take(refs, 2)
    out_w, refs = take(refs, outs_count if head or tail else 0)
    inner_w, refs = take(refs, count)
    outer_w, refs = take(refs, count)
    if head:
        (second_ref, middle_ref), refs = take(refs, 2)
    if tail:
        (outputs_ref, grad_ref, branch_ref, gain_sum, shift_sum, cot_sum), refs = take(refs, 6)
        tops, refs = take(refs, outs_count)
    else:
        (total_ref, back_ref), refs = take(refs, 2)
    acts, refs = take(refs, count)
    inner_grads, refs = take(refs, count)
    out_scr, inner_scr, outer_scr, total_scr, back_scr, sems = refs
    step = pl.program_id(0)
    model, width = inner_scr.shape[1:]
    out_copies = []
    for i, ref in enumerate(out_w):
        lanes = out_scr.shape[0] // outs_count
        out_copies.append(
            pltpu.make_async_copy(
                ref.at[pl.ds(offsets[0][i], lanes)], out_scr.at[pl.ds(i * lanes, lanes)], sems.at[i]
            )
        )
    copies = []
    for i in range(count):
        n = outs_count + 2 * i
        inner = inner_w[i].at[pl.ds(offsets[1][i], model)]
        outer = outer_w[i].at[pl.ds(offsets[2][i], width)]
        copies.append(
            [
                pltpu.make_async_copy(inner, inner_scr.at[i], sems.at[n]),
                pltpu.make_async_copy(outer, outer_scr.at[i], sems.at[n + 1]),
            ]
        )

    @pl.when(step == 0)
    def _():
        for copy in out_copies if head else []:
            copy.start()
        for pair in copies:
            for copy in pair:
                copy.start()
        for copy in [] if head else out_copies:
            copy.start()
        if tail:
            for ref in (gain_sum, shift_sum, cot_sum):
                ref[...] = jnp.zeros_like(ref)

    def body(first_step):
        def ready(group):
            if first_step:
                for copy in group:
                    copy.wait()

        cot = cot_ref[...]
        if head:
            ready(out_copies)
            joined = jnp.concatenate([ref[...] for ref in merged], axis=1)
            middle = full(resid_ref[...]) + matmul(joined, out_scr[...])
            middle_ref[...] = middle
            unit, _ = unit_of(middle)
            second = low(unit * gain_ref[...] + shift_ref[...])
            second_ref[:, :model] = second
            second_ref[:, model:] = jnp.ones((second.shape[0], ONES), jnp.bfloat16)
            total_scr[...] = middle + outer_bias_ref[...]
        else:
            second = second_in[:, :model]
            total_scr[...] = total_in[...]
            back_scr[...] = back_in[...]
        for i in range(count):
            ready(copies[i])
            pre = matmul(second, inner_scr[i]) + bias_ref[:, i * width : (i + 1) * width]
            grad = contract_cols(cot, outer_scr[i])
            act, slope = gelu_both(pre)
            act = low(act)
            acts[i][...] = act
            grad = low(grad * slope)
            inner_grads[i][...] = grad
            total_scr[...] += matmul(act, outer_scr[i])
            back = contract_cols(grad, inner_scr[i])
            if head and i == 0:
                back_scr[...] = back
            else:
                back_scr[...] += back
        if not tail:
            total_ref[...] = total_scr[...]
            back_ref[...] = back_scr[...]
            return
        outputs_ref[...] = low(total_scr[...])
        second_grad = back_scr[...]
        unit, inverse = unit_of(middle_in[...])
        cot_wide = full(cot)
        middle_grad = cot_wide + norm_grad(second_grad, unit, inverse, gain_in[...])
        gain_sum[...] += column_sum(second_grad * unit)
        shift_sum[...] += column_sum(second_grad)
        cot_sum[...] += column_sum(cot_wide)
        grad_ref[...] = middle_grad
        branch = low(middle_grad)
        branch_ref[...] = branch
        ready([] if head else out_copies)
        top = low(contract_cols(branch, out_scr[...]))
        at = 0
        for ref in tops:
            ref[...] = top[:, at : at + ref.shape[1]]
            at += ref.shape[1]

    @pl.when(step == 0)
    def _():
        body(True)

    @pl.when(step > 0)
    def _():
        body(False)


def run_middle(cot, bias, inner_w, outer_w, out_w, head=None, carried=None, tail=None):
    rows, model = cot.shape
    count, outs_count = len(inner_w), len(out_w)
    tile = min(ROW_TILE, rows)
    width = bias.shape[1] // count
    lanes = model // outs_count
    args, in_specs = [cot, bias], [tiled(tile, model), line(count * width)]
    if head is not None:
        resid, lines, merged = head
        args += [resid, *lines, *merged]
        in_specs += [tiled(tile, model)] + [line(model)] * 3 + [tiled(tile, lanes)] * outs_count
    else:
        args += carried
        in_specs += [tiled(tile, model + ONES)] + [tiled(tile, model)] * 2
    if tail is not None:
        args += tail
        in_specs += [tiled(tile, model), line(model)]
    used_out = out_w if head is not None or tail is not None else []
    weights = [*used_out, *inner_w, *outer_w]
    args += [array for array, _ in weights]
    in_specs += [ANYWHERE] * len(weights)
    offsets = [[first for _, first in group] for group in (used_out, inner_w, outer_w)]
    out_specs, out_shape = [], []

    def result(cols, dtype=jnp.bfloat16):
        out_specs.append(tiled(tile, cols))
        out_shape.append(rows_out(rows, cols, dtype))

    if head is not None:
        result(model + ONES)
        result(model, jnp.float32)
    if tail is not None:
        result(model)
        result(model, jnp.float32)
        result(model)
        for _ in range(3):
            out_specs.append(line(model))
            out_shape.append(line_out(model))
        for _ in range(outs_count):
            result(lanes)
    else:
        result(model, jnp.float32)
        result(model, jnp.float32)
    for _ in range(2 * count):
        result(width)
    outs = pl.pallas_call(
        functools.partial(
            middle_kernel, count, outs_count, head is not None, tail is not None, offsets
        ),
        grid=(rows // tile,),
        in_specs=in_specs,
        out_specs=out_specs,
        out_shape=out_shape,
        scratch_shapes=[
            pltpu.VMEM((model, model), jnp.bfloat16),
            pltpu.VMEM((count, model, width), jnp.bfloat16),
            pltpu.VMEM((count, width, model), jnp.bfloat16),
            pltpu.VMEM((tile, model), jnp.float32),
            pltpu.VMEM((tile, model), jnp.float32),
            pltpu.SemaphoreType.DMA((outs_count + 2 * count,)),
        ],
        compiler_params=pltpu.CompilerParams(vmem_limit_bytes=58 * MEGA),
        cost_estimate=cost(rows * model),
        name="middle",
    )(*args)
    plain = outs[: -2 * count]
    return plain, outs[-2 * count : -count], outs[-count:]


def bundle_kernel(count, *refs):
    sources, target, (held, sems) = refs[:count], refs[count], refs[count + 1 :]
    loads, stores, at = [], [], 0
    for i, source in enumerate(sources):
        rows = pl.ds(at, source.shape[0])
        at += source.shape[0]
        loads.append(pltpu.make_async_copy(source, held.at[rows], sems.at[i]))
        stores.append(pltpu.make_async_copy(held.at[rows], target.at[rows], sems.at[count + i]))
    for copy in loads:
        copy.start()
    for load, store in zip(loads, stores):
        load.wait()
        store.start()
    for copy in stores:
        copy.wait()


def run_bundle(arrays):
    rows, cols = sum(array.shape[0] for array in arrays), arrays[0].shape[1]
    return pl.pallas_call(
        functools.partial(bundle_kernel, len(arrays)),
        in_specs=[ANYWHERE] * len(arrays),
        out_specs=ANYWHERE,
        out_shape=rows_out(rows, cols),
        scratch_shapes=[
            pltpu.VMEM((rows, cols), jnp.bfloat16),
            pltpu.SemaphoreType.DMA((2 * len(arrays),)),
        ],
        compiler_params=pltpu.CompilerParams(vmem_limit_bytes=58 * MEGA),
        cost_estimate=cost(rows * cols),
        name="bundle",
    )(*arrays)


def add_kernel(count, tall, *refs):
    firsts, seconds, (out_ref, row_ref) = refs[:count], refs[count : 2 * count], refs[2 * count :]

    def total(arrays, rows):
        value = full(arrays[0][rows, :])
        for ref in arrays[1:]:
            value = value + full(ref[rows, :])
        return value

    rest = total(firsts, slice(tall, firsts[0].shape[0]))
    row_ref[...] = rest[:1]
    out_ref[:tall, :] = low(total(firsts, slice(0, tall)))
    out_ref[tall:, :] = low(total(seconds, slice(0, seconds[0].shape[0])))


def run_add(firsts, seconds, tall):
    count, cols = len(firsts), firsts[0].shape[1]
    return pl.pallas_call(
        functools.partial(add_kernel, count, tall),
        in_specs=[ON_CHIP] * (2 * count),
        out_specs=[ON_CHIP] * 2,
        out_shape=[rows_out(tall + seconds[0].shape[0], cols), line_out(cols)],
        compiler_params=pltpu.CompilerParams(vmem_limit_bytes=32 * MEGA),
        cost_estimate=cost(10**6, 8 * firsts[0].shape[0] * cols),
        name="add",
    )(*firsts, *seconds)


def first_kernel(resid_ref, gain_ref, shift_ref, weight_ref, normed_ref, packed_ref):
    unit, _ = unit_of(full(resid_ref[...]))
    normed = low(unit * gain_ref[...] + shift_ref[...])
    normed_ref[...] = normed
    packed_ref[...] = low(contract_cols(normed, weight_ref[...]))


def run_first(resid, gain, shift, weight):
    rows, model = resid.shape
    tile = min(ROW_TILE, rows)
    cols = weight.shape[0]
    return pl.pallas_call(
        first_kernel,
        grid=(rows // tile,),
        in_specs=[
            tiled(tile, model),
            line(model),
            line(model),
            pl.BlockSpec((cols, model), lambda i: (0, 0), pipeline_mode=pl.Buffered(1)),
        ],
        out_specs=[tiled(tile, model), tiled(tile, cols)],
        out_shape=[rows_out(rows, model), rows_out(rows, cols)],
        compiler_params=pltpu.CompilerParams(vmem_limit_bytes=32 * MEGA),
        cost_estimate=cost(rows * model),
        name="first",
    )(resid, gain, shift, weight)


def project_kernel(rows_ref, weight_ref, packed_ref):
    packed_ref[...] = low(contract_cols(rows_ref[...], weight_ref[...]))


def run_project(rows_in, weight):
    rows, model = rows_in.shape
    tile = min(2 * ROW_TILE, rows)
    cols = weight.shape[0]
    return pl.pallas_call(
        project_kernel,
        grid=(rows // tile,),
        in_specs=[
            tiled(tile, model),
            pl.BlockSpec((cols, model), lambda i: (0, 0), pipeline_mode=pl.Buffered(1)),
        ],
        out_specs=tiled(tile, cols),
        out_shape=rows_out(rows, cols),
        compiler_params=pltpu.CompilerParams(vmem_limit_bytes=32 * MEGA),
        cost_estimate=cost(rows * model),
        name="project",
    )(rows_in, weight)


def last_kernel(parts, *refs):
    (resid_ref, grad_ref, gain_ref), refs = take(refs, 3)
    packed, refs = take(refs, parts)
    joint_w, refs = take(refs, parts)
    out_ref, gain_sum, shift_sum, joint_scr, sems = refs[-5:]
    step = pl.program_id(0)
    copies = [
        pltpu.make_async_copy(joint_w[i], joint_scr.at[i], sems.at[i]) for i in range(parts)
    ]

    @pl.when(step == 0)
    def _():
        for copy in copies:
            copy.start()
        gain_sum[...] = jnp.zeros_like(gain_sum)
        shift_sum[...] = jnp.zeros_like(shift_sum)
        for copy in copies:
            copy.wait()

    unit, inverse = unit_of(full(resid_ref[...]))
    joined = jnp.concatenate([ref[...] for ref in packed], axis=1)
    first_grad = matmul(joined, joint_scr[...].reshape(joined.shape[1], joint_scr.shape[2]))
    out_ref[...] = grad_ref[...] + norm_grad(first_grad, unit, inverse, gain_ref[...])
    gain_sum[...] += column_sum(first_grad * unit)
    shift_sum[...] += column_sum(first_grad)


def run_last(part, part_rows, resid, middle_grad, gain, packed, joint_w, made):
    parts = len(packed)
    rows, model = resid.shape
    tile = min(ROW_TILE, part_rows)
    depth = packed[0].shape[1]
    first = part * part_rows // tile
    return pl.pallas_call(
        functools.partial(last_kernel, parts),
        grid=(part_rows // tile,),
        in_specs=[tiled(tile, model, first)] * 2
        + [line(model)]
        + [tiled(tile, depth, first)] * parts
        + [ANYWHERE] * parts
        + [ANYWHERE] * (made is not None),
        out_specs=[tiled(tile, model, first)] + [line(model)] * 2,
        out_shape=[rows_out(rows, model, jnp.float32)] + [line_out(model)] * 2,
        scratch_shapes=[
            pltpu.VMEM((parts, depth, model), jnp.bfloat16),
            pltpu.SemaphoreType.DMA((parts,)),
        ],
        input_output_aliases={} if made is None else {3 + 2 * parts: 0},
        compiler_params=pltpu.CompilerParams(vmem_limit_bytes=40 * MEGA),
        cost_estimate=cost(2 * part_rows * model * parts * depth, part_rows * model * 20),
        name="last",
    )(resid, middle_grad, gain, *packed, *joint_w, *([] if made is None else [made]))


def swap(values, axis, bit):
    size = lax.axis_size(axis)
    return lax.ppermute(values, axis, [(i, i ^ bit) for i in range(size)])


def after(values, *earlier):
    return lax.optimization_barrier((values, earlier))[0]


def put_halves(upper, mine, other):
    return jnp.where(
        upper == 0,
        jnp.concatenate([mine, other], axis=0),
        jnp.concatenate([other, mine], axis=0),
    )


def half(values, upper):
    rows = values.shape[0] // 2
    return lax.dynamic_slice_in_dim(values, upper * rows, rows, 0)


class GroupSum:
    def __init__(self, values, which=(0, 1)):
        bits = [1 << i for i in range(lax.axis_size("dp").bit_length() - 1)]
        orders = []
        for order in (bits, bits[1:2] + bits[:1] + bits[2:]):
            odd = len(order) % 2
            groups = [order[:odd]] + [order[i : i + 2] for i in range(odd, len(order), 2)]
            orders.append([tuple(group) for group in groups if group])
        orders = [orders[n] for n in which]
        part = values.shape[0] // len(orders)
        self.parts = [values[n * part : (n + 1) * part] for n in range(len(orders))]
        self.steps = [
            [(True, group) for group in order] + [(False, group) for group in order[::-1]]
            for order in orders
        ]
        self.pending = None

    def start(self):
        self.pending, sent = [], []
        if not self.steps[0]:
            return tuple(self.parts)
        for values, steps in zip(self.parts, self.steps):
            halving, group = steps.pop(0)
            uppers = [(lax.axis_index("dp") // bit) % 2 for bit in group]
            others = []
            for k in range(1, 1 << len(group)):
                flips = [k >> i & 1 for i in range(len(group))]
                leaving = values
                if halving:
                    for upper, flip in zip(uppers[::-1], flips[::-1]):
                        leaving = half(leaving, 1 - upper if flip else upper)
                sent.append(leaving)
                bit = sum(bit for bit, flip in zip(group, flips) if flip)
                others.append(swap(leaving, "dp", bit))
            if halving:
                for upper in uppers[::-1]:
                    values = half(values, upper)
            self.pending.append((halving, uppers, values, others))
        return tuple(sent)

    def finish(self, *earlier):
        if not self.pending:
            return
        self.parts = []
        for halving, uppers, mine, others in self.pending:
            if earlier:
                others = after(others, *earlier)
            if halving:
                total = full(mine)
                for other in others:
                    total = total + full(other)
                self.parts.append(low(total))
            else:
                pieces = [mine, *others]
                for upper in uppers:
                    pieces = [
                        put_halves(upper, pieces[n], pieces[n + 1])
                        for n in range(0, len(pieces), 2)
                    ]
                self.parts += pieces
        self.pending = None

    def step(self, *earlier):
        self.finish(*earlier)
        return self.start()

    def result(self):
        while self.steps[0] or self.pending:
            self.step()
        return full(jnp.concatenate(self.parts, axis=0))


def sum_all(values):
    for axis in ("tensor", "dp"):
        size, bit = lax.axis_size(axis), 1
        while bit < size:
            if 2 * bit < size:
                others = [swap(values, axis, bit * n) for n in (1, 2, 3)]
                values = (values + others[0]) + (others[1] + others[2])
                bit *= 4
            else:
                values = values + swap(values, axis, bit)
                bit *= 2
    return values


def split_exact(values):
    terms = []
    for _ in range(3):
        term = lax.reduce_precision(values, 8, 7)
        terms.append(low(term))
        values = values - term
    return terms


def per_device(
    inputs,
    query_weight,
    key_weight,
    value_weight,
    output_weight,
    inner_weight,
    inner_bias,
    outer_weight,
    outer_bias,
    first_gain,
    first_shift,
    second_gain,
    second_shift,
    item_lengths,
    key_mask,
    random_blocks,
    cotangent,
):
    tensor = lax.axis_size("tensor")
    items = item_lengths.shape[0]
    local_rows, model = inputs.shape
    span = local_rows * tensor // items
    members = tensor // items
    place = lax.axis_index("tensor")
    item, member = place // members, place % members
    heads, blocks = random_blocks.shape[1], random_blocks.shape[2]
    lanes = query_weight.shape[0]
    length = span // blocks
    sh = Shape(span, heads, lanes // heads, blocks, SHARED + random_blocks.shape[3])

    def from_item(values, step):
        if step % items == 0:
            return values
        pairs = [
            (t, (t // members - step) % items * members + t % members) for t in range(tensor)
        ]
        return lax.ppermute(values, "tensor", pairs)

    def from_member(values, step):
        if step % members == 0:
            return values
        pairs = [
            (t, t // members * members + (t % members - step) % members) for t in range(tensor)
        ]
        return lax.ppermute(values, "tensor", pairs)

    order = [(s, r) for s in range(items) for r in range(members)]
    away = range(1, items)
    joint = run_bundle([query_weight, key_weight, value_weight])
    upper = lax.axis_index("dp") % 2
    joint_halves = [from_item(half(joint, upper), s) for s in away]

    lines = (first_gain.reshape(1, -1), first_shift.reshape(1, -1))
    firsts = [run_first(from_member(inputs, r), *lines, joint) for r in range(members)]
    first_all = [normed for normed, _ in firsts]

    width = inner_weight.shape[1]
    bias_rows = jnp.stack(split_exact(inner_bias))
    bias_rows = jnp.concatenate([bias_rows, jnp.zeros((13, width), jnp.bfloat16)], axis=0)
    own_weights = [output_weight, inner_weight, outer_weight, bias_rows]
    if width == model:
        sent = [run_bundle([output_weight, outer_weight, bias_rows]), inner_weight]
        views = [(0, 0), (1, 0), (0, lanes), (0, lanes + width)]
    else:
        sent = own_weights
        views = [(n, 0) for n in range(len(own_weights))]

    used = lax.dynamic_index_in_dim(item_lengths, item, 0, False) // length
    flags = lax.dynamic_index_in_dim(key_mask.reshape(items, span), item, 0, False)
    key_ok = (jnp.arange(span, dtype=jnp.int32) < used * length) & (flags == 1)
    bias = jnp.where(jnp.concatenate([key_ok, jnp.zeros((length,), bool)]), 0.0, MASKED)
    bias = jnp.broadcast_to(full(bias)[:, None], (span + length, 128))
    def lists_of(s):
        picks = lax.dynamic_index_in_dim(random_blocks, (item - s) % items, 0, False)
        if s:
            picks = from_item(after(picks, joint_halves), s)
        chosen, usable = jax.vmap(lambda pick: block_lists(used, pick))(picks)
        marked = jnp.where(usable, chosen, blocks)
        return (used.reshape(1), member.reshape(1), chosen.reshape(-1), marked.reshape(-1), bias)

    lists = [lists_of(s) for s in range(items)]

    packed, made, merged, logs, joint_item = [], [], [], [], [joint]
    rows_in = first_all
    for s in range(items):
        if s == 0:
            group = [packed_rows for _, packed_rows in firsts]
            sent = after(sent, joint_halves)
            joint_others = [swap(rows, "dp", 1) for rows in joint_halves]
            own_sent = after(sent, group[-1])
            own_parts = {
                r: [from_member(array, -r) for array in own_sent] for r in range(1, members)
            }
            item_sent = [own_sent] + [[from_item(array, t) for array in sent] for t in away]
        else:
            halves = after((joint_halves[s - 1], joint_others[s - 1]), made[s - 1][0])
            weight = put_halves(upper, *halves)
            joint_item.append(weight)
            group = [run_project(rows, weight) for rows in rows_in]
        packed.append(group)
        outs, log_rows = attend_forward(sh, after(group, sent, joint_halves), lists[s], 0 if s else 64)
        made.append(outs)
        logs.append(log_rows)
        merged += [from_member(outs[r], -r) for r in range(members)]
        rows_in = after(first_all, outs[0], [arrays[0] for arrays in own_parts.values()])

    part_weights = {}
    for s, r in order:
        if (s, r) == (0, 0):
            part_weights[s, r] = [(array, 0) for array in own_weights]
        else:
            arrays = own_parts[r] if s == 0 else None
            if s:
                early = item_sent[s][:1] if width == model else item_sent[s]
                arrays = [from_member(array, -r) for array in after(early, packed[s])]
                arrays += item_sent[s][len(early) :]
            part_weights[s, r] = [(arrays[n], row) for n, row in views]

    def part_bias(part):
        if part == (0, 0):
            return inner_bias.reshape(1, -1)
        array, row = part_weights[part][3]
        terms = full(array[row : row + 3])
        return (terms[0] + terms[1] + terms[2]).reshape(1, -1)

    groups = [
        [(0, 0)],
        [part for part in order if part[0] > 0],
        [(0, r) for r in range(1, members)],
    ]
    groups = [group for group in groups if group]
    out_full = [part_weights[part][0] for part in order]
    acts, inner_grads = {}, {}

    def outer_product(part):
        return contract_rows(acts[part], cotangent)

    def inner_product(part):
        return contract_rows(second_own, inner_grads[part])

    def output_product(part):
        return contract_rows(merged[order.index(part)], branch)

    def send_members(product, s):
        return [from_member(low(product((s, r))), r) for r in range(members - 1, 0, -1)]

    def add_members(product, s, others):
        total = product((s, 0))
        for other in others:
            total = total + full(other)
        return low(total)

    totals = {}
    carried, waits = None, ()
    for n, group in enumerate(groups):
        head = tail = None
        if n == 0:
            lines = [row.reshape(1, -1) for row in (outer_bias, second_gain, second_shift)]
            head = (inputs, lines, merged)
        if n == len(groups) - 1:
            tail = [middle, second_gain.reshape(1, -1)]
        inner_parts = [part_weights[part][1] for part in group]
        if n == 1 and width == model:
            late = after([item_sent[s][1] for s in range(items)], acts[0, 0])
            inner_parts = [(from_member(late[s], -r), 0) for s, r in group]
        plain, group_acts, group_grads = run_middle(
            cotangent,
            jnp.concatenate([part_bias(part) for part in group], axis=1),
            inner_parts,
            [part_weights[part][2] for part in group],
            out_full,
            head,
            after(carried, waits) if carried else None,
            tail,
        )
        for part, act, grad in zip(group, group_acts, group_grads):
            acts[part], inner_grads[part] = act, grad
        if n == 0:
            second_own, middle = plain[:2]
            plain = plain[2:]
        if n < len(groups) - 1:
            carried = [second_own, *plain]
        waits = []
        for s in sorted({s for s, _ in group if s > 0}, reverse=True):
            for name, product in (("outer", outer_product), ("inner", inner_product)):
                totals[name, s] = add_members(product, s, send_members(product, s))
                waits.append(totals[name, s])
    outputs, middle_grad, branch, second_gain_sum, second_shift_sum, cot_sum = plain[:6]
    tops = plain[6:]

    top_rows = [[None] * members for _ in range(items)]
    for i, (s, r) in enumerate(order):
        top_rows[s][r] = from_member(tops[i], r)
    products = {"outer": outer_product, "inner": inner_product, "output": output_product}
    item_sent = {
        name: [from_item(totals[name, s], -s) for s in away] for name in ("outer", "inner")
    }
    member_sent = {name: send_members(product, 0) for name, product in products.items()}
    totals["outer", 0] = add_members(outer_product, 0, member_sent["outer"])
    for s in range(items - 1, -1, -1):
        others = send_members(output_product, s) if s else member_sent["output"]
        totals["output", s] = add_members(output_product, s, others)
    item_sent["output"] = [from_item(totals["output", s], -s) for s in away]

    def add_items(total, others):
        total = full(total)
        for other in others:
            total = total + full(other)
        return low(total)

    packed_grad, joint_totals = [None] * items, [None] * items
    outer_sum = GroupSum(
        add_items(totals["outer", 0], after(item_sent["outer"], branch)), (0,)
    )
    waits = (outer_sum.start(), member_sent, totals["output", 0])
    inner_sum = None
    back, joint_sent = {}, []
    for s in range(items - 1, -1, -1):
        grads = ()
        for part in range(BACK_PARTS):
            if part:
                waits = outer_sum.step(grads[0])
                if inner_sum is None:
                    others, second_own = after((item_sent, second_own), grads[0], waits)
                    totals["inner", 0] = add_members(inner_product, 0, member_sent["inner"])
                    inner_terms = [totals["inner", 0], *others["inner"]]
                    output_terms = [totals["output", 0], *others["output"]]
                    if width == model:
                        inner_total, bias_total = run_add(inner_terms, output_terms, model)
                    else:
                        inner_total = add_items(inner_terms[0], inner_terms[1:])
                        bias_total = full(inner_total[model : model + 1])
                        inner_total = inner_total[:model]
                        output_sum = GroupSum(add_items(output_terms[0], output_terms[1:]), (0,))
                    inner_sum = GroupSum(inner_total, (1,))
                    waits = (waits, inner_sum.start(), outer_sum.step(inner_total))
                else:
                    waits = (waits, inner_sum.step(grads[0]), joint_sent)
            grads = attend_backward(
                sh,
                packed[s],
                after(top_rows[s], waits),
                made[s],
                logs[s],
                lists[s],
                (part, BACK_PARTS),
                grads,
            )
        packed_grad[s] = grads
        waits = inner_sum.step(grads[0])
        rows = after(grads, waits, outer_sum.step(grads[0]) if s else ())
        total = contract_rows(rows[0], first_all[0])
        for r in range(1, members):
            total = total + contract_rows(rows[r], first_all[r])
        joint_totals[s] = low(total) if s else total
        grads = after(grads, waits)
        waits = joint_totals[s]
        if s:
            grads = after(grads, waits)
            joint_sent.append(from_item(joint_totals[s], -s))
        for r in range(members):
            back[s, r] = from_member(grads[r], -r)

    back = [back[part] for part in order]
    joint_full = [from_member(joint_item[s], -r) for s, r in order]
    end_sum = GroupSum(add_items(joint_totals[0], joint_sent), (0,))
    waits = end_sum.start()
    pieces = []
    cut = local_rows // LAST_PARTS
    for n in range(LAST_PARTS):
        outs = run_last(
            n,
            cut,
            inputs,
            middle_grad,
            first_gain.reshape(1, -1),
            after(back, waits),
            joint_full,
            pieces[-1][0] if pieces else None,
        )
        pieces.append(outs)
        if n == 0:
            waits = end_sum.step(outs[1])
    input_grad = pieces[-1][0]
    vectors = [
        sum(piece[1] for piece in pieces),
        sum(piece[2] for piece in pieces),
        second_gain_sum,
        second_shift_sum,
        cot_sum,
        lax.dynamic_update_slice(jnp.zeros((tensor, width), jnp.float32), bias_total, (place, 0)),
    ]
    vectors = after(vectors, end_sum.step(), inner_sum.step(pieces[-1][1]))
    small = sum_all(jnp.concatenate([vector.reshape(-1) for vector in vectors]))
    bias_grad = lax.dynamic_slice_in_dim(small, 5 * model + place * width, width, 0)
    small = small[: 5 * model].reshape(5, model)
    end_grad = end_sum.result()
    outer_grad, inner_grad = outer_sum.result(), inner_sum.result()
    if width == model:
        inner_grad, output_grad = inner_grad[:model], inner_grad[model:]
    else:
        output_grad = output_sum.result()
    return (
        outputs,
        input_grad,
        end_grad[:lanes],
        end_grad[lanes : 2 * lanes],
        end_grad[2 * lanes :],
        output_grad,
        inner_grad,
        bias_grad,
        outer_grad,
        small[4],
        small[0],
        small[1],
        small[2],
        small[3],
    )


def solution(mesh):
    placed = (
        P(("dp", "tensor"), None),
        P("tensor", None),
        P("tensor", None),
        P("tensor", None),
        P("tensor", None),
        P(None, "tensor"),
        P("tensor"),
        P("tensor", None),
        P(),
        P(),
        P(),
        P(),
        P(),
        P("dp"),
        P("dp"),
        P("dp", "tensor", None, None),
        P(("dp", "tensor"), None),
    )
    return jax.shard_map(
        per_device,
        mesh=mesh,
        in_specs=placed,
        out_specs=(
            P(("dp", "tensor"), None),
            P(("dp", "tensor"), None),
            P("tensor", None),
            P("tensor", None),
            P("tensor", None),
            P("tensor", None),
            P(None, "tensor"),
            P("tensor"),
            P("tensor", None),
            P(),
            P(),
            P(),
            P(),
            P(),
        ),
        check_vma=False,
    )
```

```python
import functools

import jax
import jax.numpy as jnp
from jax import lax
from jax.experimental import pallas as pl
from jax.experimental.pallas import tpu as pltpu
from jax.sharding import PartitionSpec as P

EPSILON = 1e-05
MASKED = -1e30
LOG2E = 1.4426950408889634
SHARED = 5
KEY_CHUNK = 512
MEGA = 2**20
ROW_TILE = 256
LAST_PARTS = 2
BACK_PARTS = 2


def contract_rows(left, right):
    return lax.dot_general(
        left, right, (((0,), (0,)), ((), ())), preferred_element_type=jnp.float32
    )


def contract_cols(left, right):
    return lax.dot_general(
        left, right, (((1,), (1,)), ((), ())), preferred_element_type=jnp.float32
    )


def matmul(left, right):
    return lax.dot_general(
        left, right, (((1,), (0,)), ((), ())), preferred_element_type=jnp.float32
    )


def block_lists(blocks_used, random_pick):
    block_count = random_pick.shape[0]
    places = jnp.arange(block_count, dtype=jnp.int32)[:, None]
    fixed_cols = jnp.zeros_like(places)
    chosen = jnp.concatenate(
        [
            places - 1,
            places,
            places + 1,
            fixed_cols,
            fixed_cols + blocks_used - 1,
            random_pick % blocks_used,
        ],
        axis=1,
    )
    inside = (chosen >= 0) & (chosen < blocks_used)
    slot_count = chosen.shape[1]
    before = jnp.arange(slot_count)[:, None] < jnp.arange(slot_count)[None, :]
    repeated = jnp.any(
        (chosen[:, :, None] == chosen[:, None, :]) & inside[:, :, None] & before[None], axis=1
    )
    return (jnp.clip(chosen, 0, block_count - 1), inside & jnp.logical_not(repeated))


def low(values):
    return values.astype(jnp.bfloat16)


def full(values):
    return values.astype(jnp.float32)


class Shape:
    def __init__(self, span, heads, head_size, blocks, slots):
        self.span, self.heads, self.head_size, self.blocks, self.slots = (
            span,
            heads,
            head_size,
            blocks,
            slots,
        )
        self.length = span // blocks
        self.lanes = heads * head_size
        self.columns = heads * self.length
        self.wide = max(1, min(heads, 128 // head_size))
        self.tile = self.wide * head_size
        self.chunk = min(KEY_CHUNK, span)
        self.bias_lanes = min(128, self.columns)


def rows_of(index, length):
    return pl.ds(pl.multiple_of(index * length, length), length)


def spread_heads(block, sh):
    lane = lax.broadcasted_iota(jnp.int32, block.shape, 1) // sh.head_size
    zero = jnp.zeros_like(block)
    return jnp.concatenate([jnp.where(lane == h, block, zero) for h in range(sh.heads)], axis=0)


def pick_heads(stacked, sh):
    lane = lax.broadcasted_iota(jnp.int32, (sh.length, sh.lanes), 1) // sh.head_size
    out = stacked[: sh.length]
    for h in range(1, sh.heads):
        out = jnp.where(lane == h, stacked[h * sh.length : (h + 1) * sh.length], out)
    return out


def mixed_slot(load, idx, j, s, sh):
    cols = []
    for t in range(sh.heads // sh.wide):
        out = None
        for i in range(sh.wide):
            at = idx[((t * sh.wide + i) * sh.blocks + j) * sh.slots + s]
            piece = load(rows_of(at, sh.length), t)
            if i == 0:
                out = piece
            else:
                lane = lax.broadcasted_iota(jnp.int32, piece.shape, 1) // sh.head_size
                out = jnp.where(lane == i, piece, out)
        cols.append(out)
    return cols[0] if len(cols) == 1 else jnp.concatenate(cols, axis=1)


def gather_rows(ref, first, idx, j, sh):
    parts = [
        ref[rows_of(idx[j * sh.slots + s], sh.length), first : first + sh.lanes]
        for s in range(SHARED)
    ]

    def load(rows, t):
        return ref[rows, first + t * sh.tile : first + (t + 1) * sh.tile]

    for s in range(SHARED, sh.slots):
        parts.append(mixed_slot(load, idx, j, s, sh))
    return jnp.concatenate(parts, axis=0)


def widen(bias, sh):
    reps = sh.columns // sh.bias_lanes
    return bias if reps == 1 else jnp.concatenate([bias] * reps, axis=1)


def gather_bias(ref, idx, j, sh):
    parts = [
        widen(ref[rows_of(idx[j * sh.slots + s], sh.length), : sh.bias_lanes], sh)
        for s in range(SHARED)
    ]

    def load(rows, t):
        return ref[rows, : sh.bias_lanes]

    for s in range(SHARED, sh.slots):
        parts.append(mixed_slot(load, idx, j, s, sh))
    return jnp.concatenate(parts, axis=0)


def split_rows(dot, left, right, cuts):
    edges = [0, *cuts, left.shape[0]]
    return jnp.concatenate([dot(left[a:b], right) for a, b in zip(edges, edges[1:])], axis=0)


def each_block(first, count, unroll, blocks_from):
    def many(i, carry):
        blocks_from(first + i * unroll, unroll)
        return carry

    lax.fori_loop(0, count // unroll, many, 0)

    def one(j, carry):
        blocks_from(j, 1)
        return carry

    lax.fori_loop(first + count // unroll * unroll, first + count, one, 0)


def forward_kernel(sh, pieces, unroll, used, member, idx, bidx, *refs):
    packed, bias_ref = refs[:pieces], refs[pieces]
    outs, log_ref = refs[pieces + 1 : 2 * pieces + 1], refs[2 * pieces + 1]
    rows, o_scr, s_scr, sems = refs[2 * pieces + 2 :]
    c = used[0]
    scale = sh.head_size ** (-0.5) * LOG2E
    rows_each = sh.span // pieces
    query, key, value = 0, sh.lanes, 2 * sh.lanes

    def place(r):
        return rows_of(lax.rem(member[0] + r, pieces), rows_each)

    loads = [pltpu.make_async_copy(packed[r], rows.at[place(r)], sems.at[r]) for r in range(pieces)]
    for copy in loads:
        copy.start()
    o_scr[...] = jnp.zeros_like(o_scr)
    log_ref[...] = jnp.zeros_like(log_ref)
    for copy in loads:
        copy.wait()

    def block(j):
        at = rows_of(j, sh.length)
        q_all = spread_heads(rows[at, query : query + sh.lanes], sh)
        scores = contract_cols(gather_rows(rows, key, idx, j, sh), q_all) * scale
        scores = scores + gather_bias(bias_ref, bidx, j, sh)
        top = jnp.max(scores, axis=0, keepdims=True)
        shifted = jnp.exp2(scores - top)
        total = jnp.sum(shifted, axis=0, keepdims=True)
        log_ref[pl.ds(j, 1), :] = top + jnp.log2(total)
        probs = low(shifted * (1.0 / total))
        out = pick_heads(contract_rows(probs, gather_rows(rows, value, idx, j, sh)), sh)
        o_scr[at, :] = low(out)

    def blocks_from(j, count):
        for u in range(count):
            block(j + u)

    each_block(1, c - 2, unroll, blocks_from)

    chunks = pl.cdiv(c * sh.length, sh.chunk)
    row = (1, sh.columns)
    for j in (0, c - 1):
        at = rows_of(j, sh.length)
        q_all = spread_heads(rows[at, query : query + sh.lanes], sh)

        def first(i, top):
            keys = rows_of(i, sh.chunk)
            scores = contract_cols(rows[keys, key : key + sh.lanes], q_all) * scale
            scores = scores + widen(bias_ref[keys, : sh.bias_lanes], sh)
            s_scr[keys, :] = scores
            return jnp.maximum(top, jnp.max(scores, axis=0, keepdims=True))

        top = lax.fori_loop(0, chunks, first, jnp.full(row, MASKED, jnp.float32))

        def second(i, total):
            keys = rows_of(i, sh.chunk)
            shifted = jnp.exp2(s_scr[keys, :] - top)
            s_scr[keys, :] = shifted
            return total + jnp.sum(shifted, axis=0, keepdims=True)

        total = lax.fori_loop(0, chunks, second, jnp.zeros(row, jnp.float32))
        log_ref[pl.ds(j, 1), :] = top + jnp.log2(total)
        inverse = 1.0 / total

        def third(i, out):
            keys = rows_of(i, sh.chunk)
            probs = low(s_scr[keys, :] * inverse)
            return out + contract_rows(probs, rows[keys, value : value + sh.lanes])

        out = lax.fori_loop(0, chunks, third, jnp.zeros((sh.columns, sh.lanes), jnp.float32))
        o_scr[at, :] = low(pick_heads(out, sh))

    stores = [
        pltpu.make_async_copy(o_scr.at[place(r)], outs[r], sems.at[pieces + r])
        for r in range(pieces)
    ]
    for copy in stores:
        copy.start()
    for copy in stores:
        copy.wait()


def backward_kernel(sh, pieces, unroll, part, used, member, idx, bidx, *refs):
    part, parts = part
    packed, tops, made = refs[:pieces], refs[pieces : 2 * pieces], refs[2 * pieces : 3 * pieces]
    refs = refs[3 * pieces :]
    (bias_ref, log_ref), refs = refs[:2], refs[2:]
    carried, refs = refs[: pieces * (part > 0)], refs[pieces * (part > 0) :]
    outs, refs = refs[:pieces], refs[pieces:]
    rows, grads, merged, d_scr, ka_scr, va_scr, sems = refs[:7]
    c = used[0]
    factor = sh.head_size ** (-0.5)
    scale = factor * LOG2E
    rows_each = sh.span // pieces
    query, key, value = 0, sh.lanes, 2 * sh.lanes
    length, slots = sh.length, sh.slots
    keys_each = slots * length

    def place(r):
        return rows_of(lax.rem(member[0] + r, pieces), rows_each)

    loads = []
    for n, (sources, target) in enumerate(((packed, rows), (tops, grads), (made, merged))):
        for r in range(pieces):
            copy = pltpu.make_async_copy(
                sources[r], target.at[place(r)], sems.at[n * pieces + r]
            )
            loads.append(copy)
            copy.start()
    carries = []
    for r in range(pieces if part else 0):
        copy = pltpu.make_async_copy(carried[r], refs[7].at[place(r)], sems.at[4 * pieces + r])
        carries.append(copy)
        copy.start()
    d_scr[:, : sh.lanes] = jnp.zeros((sh.span, sh.lanes), d_scr.dtype)
    ka_scr[...] = jnp.zeros_like(ka_scr)
    va_scr[...] = jnp.zeros_like(va_scr)
    for copy in loads:
        copy.wait()

    def equal_rows(products):
        row = lax.broadcasted_iota(jnp.int32, products.shape, 0)
        column = lax.broadcasted_iota(jnp.int32, products.shape, 1)
        return jnp.sum(
            jnp.where(column % length == row, products, 0.0), axis=0, keepdims=True
        )

    def block(j):
        at = rows_of(j, length)
        q_all = spread_heads(rows[at, query : query + sh.lanes], sh)
        g_all = spread_heads(grads[at, :], sh)
        k_all = gather_rows(rows, key, idx, j, sh)
        v_all = jnp.concatenate([gather_rows(rows, value, idx, j, sh), merged[at, :]], axis=0)
        cuts = [keys_each // 2]
        scores = split_rows(contract_cols, k_all, q_all, cuts) * scale
        prob_grad = split_rows(contract_cols, v_all, g_all, cuts)
        delta = equal_rows(prob_grad[keys_each:])
        scores = scores + gather_bias(bias_ref, bidx, j, sh)
        probs = jnp.exp2(scores - log_ref[pl.ds(j, 1), :])
        score_grad = low(probs * (prob_grad[:keys_each] - delta))
        query_grad = pick_heads(contract_rows(score_grad, k_all), sh) * factor
        d_scr[at, : sh.lanes] = low(query_grad)
        return (
            split_rows(matmul, score_grad, q_all, cuts),
            split_rows(matmul, low(probs), g_all, cuts),
        )

    def random_add(ref, j, value):
        tile = sh.tile
        for s in range(SHARED, slots):
            for h in range(sh.heads):
                t, i = h // sh.wide, h % sh.wide
                at = rows_of(idx[(h * sh.blocks + j) * slots + s], length)
                piece = value[s * length : (s + 1) * length, t * tile : (t + 1) * tile]
                if sh.wide > 1:
                    lane = lax.broadcasted_iota(jnp.int32, piece.shape, 1) // sh.head_size
                    piece = jnp.where(lane == i, piece, 0.0)
                ref[at, t * tile : (t + 1) * tile] += piece

    def blocks_from(j, count):
        gained = [block(j + u) for u in range(count)]
        for which, ref in ((0, ka_scr), (1, va_scr)):

            def slot(u, s):
                return gained[u][which][s * length : (s + 1) * length]

            for n in range(count + 2):
                total = None
                for u in range(count):
                    if 0 <= n - u <= 2:
                        total = slot(u, n - u) if total is None else total + slot(u, n - u)
                ref[rows_of(j - 1 + n, length), :] += total
            for s, target in ((3, 0), (4, c - 1)):
                total = slot(0, s)
                for u in range(1, count):
                    total = total + slot(u, s)
                ref[rows_of(target, length), :] += total
            for u in range(count):
                random_add(ref, j + u, gained[u][which])

    steps = (c - 2) // unroll
    begin, end = steps * part // parts * unroll, steps * (part + 1) // parts * unroll
    if part == parts - 1:
        end = c - 2
    each_block(1 + begin, end - begin, unroll, blocks_from)

    chunks = pl.cdiv(c * length, sh.chunk)
    for j in (0, c - 1)[2 * part // parts : 2 * (part + 1) // parts]:
        at = rows_of(j, length)
        q_all = spread_heads(rows[at, query : query + sh.lanes], sh)
        g_all = spread_heads(grads[at, :], sh)
        delta = equal_rows(contract_cols(merged[at, :], g_all))
        log_row = log_ref[pl.ds(j, 1), :]

        def chunk(i, total):
            keys = rows_of(i, sh.chunk)
            k_all = rows[keys, key : key + sh.lanes]
            scores = contract_cols(k_all, q_all) * scale
            scores = scores + widen(bias_ref[keys, : sh.bias_lanes], sh)
            probs = jnp.exp2(scores - log_row)
            prob_grad = contract_cols(rows[keys, value : value + sh.lanes], g_all)
            score_grad = low(probs * (prob_grad - delta))
            ka_scr[keys, :] += matmul(score_grad, q_all)
            va_scr[keys, :] += matmul(low(probs), g_all)
            return total + contract_rows(score_grad, k_all)

        total = lax.fori_loop(0, chunks, chunk, jnp.zeros((sh.columns, sh.lanes), jnp.float32))
        d_scr[at, : sh.lanes] = low(pick_heads(total, sh) * factor)

    for copy in carries:
        copy.wait()

    def with_carried(first, values):
        return values + full(refs[7][:, first : first + sh.lanes]) if part else values

    if part:
        d_scr[:, : sh.lanes] = d_scr[:, : sh.lanes] + refs[7][:, : sh.lanes]
    d_scr[:, key : key + sh.lanes] = low(with_carried(key, ka_scr[...] * factor))
    d_scr[:, value : value + sh.lanes] = low(with_carried(value, va_scr[...]))
    stores = [
        pltpu.make_async_copy(d_scr.at[place(r)], outs[r], sems.at[3 * pieces + r])
        for r in range(pieces)
    ]
    for copy in stores:
        copy.start()
    for copy in stores:
        copy.wait()


ANYWHERE = pl.BlockSpec(memory_space=pl.ANY)
ON_CHIP = pl.BlockSpec(memory_space=pltpu.VMEM)
SCALARS = pl.BlockSpec(memory_space=pltpu.SMEM)


def cost(flops, accessed=10**6):
    return pl.CostEstimate(flops=int(flops), bytes_accessed=int(accessed), transcendentals=0)


def attend_cost(sh, weight):
    return cost(weight * sh.blocks * sh.slots * sh.length * sh.columns * sh.lanes)


def attend_forward(sh, packed, lists, weight=16, unroll=6):
    pieces = len(packed)
    used, member, idx, bidx, bias = lists
    rows_each = sh.span // pieces
    outs = pl.pallas_call(
        functools.partial(forward_kernel, sh, pieces, unroll),
        in_specs=[SCALARS] * 4 + [ANYWHERE] * pieces + [ON_CHIP],
        out_specs=[ANYWHERE] * pieces + [ON_CHIP],
        out_shape=[jax.ShapeDtypeStruct((rows_each, sh.lanes), jnp.bfloat16)] * pieces
        + [jax.ShapeDtypeStruct((sh.blocks, sh.columns), jnp.float32)],
        scratch_shapes=[
            pltpu.VMEM((sh.span, 3 * sh.lanes), jnp.bfloat16),
            pltpu.VMEM((sh.span, sh.lanes), jnp.bfloat16),
            pltpu.VMEM((sh.span, sh.columns), jnp.float32),
            pltpu.SemaphoreType.DMA((2 * pieces,)),
        ],
        compiler_params=pltpu.CompilerParams(vmem_limit_bytes=34 * MEGA),
        cost_estimate=attend_cost(sh, weight),
        name="attend_forward",
    )(used, member, idx, bidx, *packed, bias)
    return outs[:pieces], outs[pieces]


def attend_backward(sh, packed, tops, made, log_rows, lists, part=(0, 1), carried=(), weight=32, unroll=2):
    pieces = len(packed)
    used, member, idx, bidx, bias = lists
    rows_each = sh.span // pieces
    return pl.pallas_call(
        functools.partial(backward_kernel, sh, pieces, unroll, part),
        in_specs=[SCALARS] * 4
        + [ANYWHERE] * (3 * pieces)
        + [ON_CHIP] * 2
        + [ANYWHERE] * len(carried),
        out_specs=[ANYWHERE] * pieces,
        out_shape=[jax.ShapeDtypeStruct((rows_each, 3 * sh.lanes), jnp.bfloat16)] * pieces,
        scratch_shapes=[
            pltpu.VMEM((sh.span, 3 * sh.lanes), jnp.bfloat16),
            pltpu.VMEM((sh.span, sh.lanes), jnp.bfloat16),
            pltpu.VMEM((sh.span, sh.lanes), jnp.bfloat16),
            pltpu.VMEM((sh.span, 3 * sh.lanes), jnp.bfloat16),
            pltpu.VMEM((sh.span, sh.lanes), jnp.float32),
            pltpu.VMEM((sh.span, sh.lanes), jnp.float32),
            pltpu.SemaphoreType.DMA((5 * pieces,)),
        ]
        + [pltpu.VMEM((sh.span, 3 * sh.lanes), jnp.bfloat16)] * (len(carried) > 0),
        compiler_params=pltpu.CompilerParams(
            vmem_limit_bytes=(40 if carried else 34) * MEGA
        ),
        cost_estimate=attend_cost(sh, weight // part[1]),
        name="attend_backward",
    )(used, member, idx, bidx, *packed, *tops, *made, bias, log_rows, *carried)


GELU_A = (2 / 3.141592653589793) ** 0.5
GELU_B = GELU_A * 0.044715


def gelu_both(pre):
    square = pre * pre
    turn = jnp.tanh(pre * (GELU_A + GELU_B * square))
    half = 0.5 + 0.5 * turn
    act = pre * half
    slope = half + act * (1.0 - turn) * (GELU_A + 3.0 * GELU_B * square)
    return act, slope


def unit_of(rows):
    center = jnp.mean(rows, axis=1, keepdims=True)
    deviation = rows - center
    inverse = lax.rsqrt(jnp.mean(deviation * deviation, axis=1, keepdims=True) + EPSILON)
    return deviation * inverse, inverse


def norm_grad(grad_normed, unit, inverse, gain):
    scaled = grad_normed * gain
    plain_mean = jnp.mean(scaled, axis=1, keepdims=True)
    cross_mean = jnp.mean(scaled * unit, axis=1, keepdims=True)
    return inverse * (scaled - plain_mean - unit * cross_mean)


def column_sum(values):
    return jnp.sum(values, axis=0, keepdims=True)


def take(refs, count):
    return refs[:count], refs[count:]


def tiled(tile, cols, first=0):
    return pl.BlockSpec((tile, cols), lambda i: (first + i, 0))


def line(cols):
    return pl.BlockSpec((1, cols), lambda i: (0, 0))


def line_out(cols):
    return jax.ShapeDtypeStruct((1, cols), jnp.float32)


def rows_out(rows, cols, dtype=jnp.bfloat16):
    return jax.ShapeDtypeStruct((rows, cols), dtype)


def middle_kernel(count, outs_count, head, tail, offsets, *refs):
    (cot_ref, bias_ref), refs = take(refs, 2)
    if head:
        (resid_ref, outer_bias_ref, gain_ref, shift_ref), refs = take(refs, 4)
        merged, refs = take(refs, outs_count)
    else:
        (second_in, total_in, back_in), refs = take(refs, 3)
    if tail:
        (middle_in, gain_in), refs = take(refs, 2)
    out_w, refs = take(refs, outs_count if head or tail else 0)
    inner_w, refs = take(refs, count)
    outer_w, refs = take(refs, count)
    if head:
        (second_ref, middle_ref, joined_ref), refs = take(refs, 3)
    if tail:
        (outputs_ref, grad_ref, branch_ref, gain_sum, shift_sum, cot_sum), refs = take(refs, 6)
        tops, refs = take(refs, outs_count)
    else:
        (total_ref, back_ref), refs = take(refs, 2)
    (bias_sum,), refs = take(refs, 1)
    acts, refs = take(refs, count)
    inner_grads, refs = take(refs, count)
    out_scr, inner_scr, outer_scr, total_scr, back_scr, sems = refs
    step = pl.program_id(0)
    model, width = inner_scr.shape[1:]
    out_copies = []
    for i, ref in enumerate(out_w):
        lanes = out_scr.shape[0] // outs_count
        out_copies.append(
            pltpu.make_async_copy(
                ref.at[pl.ds(offsets[0][i], lanes)], out_scr.at[pl.ds(i * lanes, lanes)], sems.at[i]
            )
        )
    copies = []
    for i in range(count):
        n = outs_count + 2 * i
        inner = inner_w[i].at[pl.ds(offsets[1][i], model)]
        outer = outer_w[i].at[pl.ds(offsets[2][i], width)]
        copies.append(
            [
                pltpu.make_async_copy(inner, inner_scr.at[i], sems.at[n]),
                pltpu.make_async_copy(outer, outer_scr.at[i], sems.at[n + 1]),
            ]
        )

    @pl.when(step == 0)
    def _():
        for copy in out_copies if head else []:
            copy.start()
        for pair in copies:
            for copy in pair:
                copy.start()
        for copy in [] if head else out_copies:
            copy.start()
        for ref in (bias_sum, gain_sum, shift_sum, cot_sum) if tail else (bias_sum,):
            ref[...] = jnp.zeros_like(ref)

    def body(first_step):
        def ready(group):
            if first_step:
                for copy in group:
                    copy.wait()

        cot = cot_ref[...]
        if head:
            ready(out_copies)
            joined = jnp.concatenate([ref[...] for ref in merged], axis=1)
            joined_ref[...] = joined
            middle = full(resid_ref[...]) + matmul(joined, out_scr[...])
            middle_ref[...] = middle
            unit, _ = unit_of(middle)
            second = low(unit * gain_ref[...] + shift_ref[...])
            second_ref[...] = second
            total_scr[...] = middle + outer_bias_ref[...]
        else:
            second = second_in[...]
            total_scr[...] = total_in[...]
            back_scr[...] = back_in[...]
        for i in range(count):
            ready(copies[i])
            pre = matmul(second, inner_scr[i]) + bias_ref[:, i * width : (i + 1) * width]
            grad = contract_cols(cot, outer_scr[i])
            act, slope = gelu_both(pre)
            act = low(act)
            acts[i][...] = act
            grad = grad * slope
            bias_sum[:, i * width : (i + 1) * width] += column_sum(grad)
            grad = low(grad)
            inner_grads[i][...] = grad
            total_scr[...] += matmul(act, outer_scr[i])
            back = contract_cols(grad, inner_scr[i])
            if head and i == 0:
                back_scr[...] = back
            else:
                back_scr[...] += back
        if not tail:
            total_ref[...] = total_scr[...]
            back_ref[...] = back_scr[...]
            return
        outputs_ref[...] = low(total_scr[...])
        second_grad = back_scr[...]
        unit, inverse = unit_of(middle_in[...])
        cot_wide = full(cot)
        middle_grad = cot_wide + norm_grad(second_grad, unit, inverse, gain_in[...])
        gain_sum[...] += column_sum(second_grad * unit)
        shift_sum[...] += column_sum(second_grad)
        cot_sum[...] += column_sum(cot_wide)
        grad_ref[...] = middle_grad
        branch = low(middle_grad)
        branch_ref[...] = branch
        ready([] if head else out_copies)
        top = low(contract_cols(branch, out_scr[...]))
        at = 0
        for ref in tops:
            ref[...] = top[:, at : at + ref.shape[1]]
            at += ref.shape[1]

    @pl.when(step == 0)
    def _():
        body(True)

    @pl.when(step > 0)
    def _():
        body(False)


def run_middle(cot, bias, inner_w, outer_w, out_w, head=None, carried=None, tail=None):
    rows, model = cot.shape
    count, outs_count = len(inner_w), len(out_w)
    tile = min(ROW_TILE, rows)
    width = bias.shape[1] // count
    lanes = model // outs_count
    args, in_specs = [cot, bias], [tiled(tile, model), line(count * width)]
    if head is not None:
        resid, lines, merged = head
        args += [resid, *lines, *merged]
        in_specs += [tiled(tile, model)] + [line(model)] * 3 + [tiled(tile, lanes)] * outs_count
    else:
        args += carried
        in_specs += [tiled(tile, model)] * 3
    if tail is not None:
        args += tail
        in_specs += [tiled(tile, model), line(model)]
    used_out = out_w if head is not None or tail is not None else []
    weights = [*used_out, *inner_w, *outer_w]
    args += [array for array, _ in weights]
    in_specs += [ANYWHERE] * len(weights)
    offsets = [[first for _, first in group] for group in (used_out, inner_w, outer_w)]
    out_specs, out_shape = [], []

    def result(cols, dtype=jnp.bfloat16):
        out_specs.append(tiled(tile, cols))
        out_shape.append(rows_out(rows, cols, dtype))

    if head is not None:
        result(model)
        result(model, jnp.float32)
        result(model)
    if tail is not None:
        result(model)
        result(model, jnp.float32)
        result(model)
        for _ in range(3):
            out_specs.append(line(model))
            out_shape.append(line_out(model))
        for _ in range(outs_count):
            result(lanes)
    else:
        result(model, jnp.float32)
        result(model, jnp.float32)
    out_specs.append(line(count * width))
    out_shape.append(line_out(count * width))
    for _ in range(2 * count):
        result(width)
    outs = pl.pallas_call(
        functools.partial(
            middle_kernel, count, outs_count, head is not None, tail is not None, offsets
        ),
        grid=(rows // tile,),
        in_specs=in_specs,
        out_specs=out_specs,
        out_shape=out_shape,
        scratch_shapes=[
            pltpu.VMEM((model, model), jnp.bfloat16),
            pltpu.VMEM((count, model, width), jnp.bfloat16),
            pltpu.VMEM((count, width, model), jnp.bfloat16),
            pltpu.VMEM((tile, model), jnp.float32),
            pltpu.VMEM((tile, model), jnp.float32),
            pltpu.SemaphoreType.DMA((outs_count + 2 * count,)),
        ],
        compiler_params=pltpu.CompilerParams(vmem_limit_bytes=31 * MEGA),
        cost_estimate=cost(rows * model),
        name="middle",
    )(*args)
    plain, bias_sums = outs[: -2 * count - 1], outs[-2 * count - 1]
    return plain, bias_sums, outs[-2 * count : -count], outs[-count:]


def bundle_kernel(count, *refs):
    sources, target, (held, sems) = refs[:count], refs[count], refs[count + 1 :]
    loads, stores, at = [], [], 0
    for i, source in enumerate(sources):
        rows = pl.ds(at, source.shape[0])
        at += source.shape[0]
        loads.append(pltpu.make_async_copy(source, held.at[rows], sems.at[i]))
        stores.append(pltpu.make_async_copy(held.at[rows], target.at[rows], sems.at[count + i]))
    for copy in loads:
        copy.start()
    for load, store in zip(loads, stores):
        load.wait()
        store.start()
    for copy in stores:
        copy.wait()


def run_bundle(arrays):
    rows, cols = sum(array.shape[0] for array in arrays), arrays[0].shape[1]
    return pl.pallas_call(
        functools.partial(bundle_kernel, len(arrays)),
        in_specs=[ANYWHERE] * len(arrays),
        out_specs=ANYWHERE,
        out_shape=rows_out(rows, cols),
        scratch_shapes=[
            pltpu.VMEM((rows, cols), jnp.bfloat16),
            pltpu.SemaphoreType.DMA((2 * len(arrays),)),
        ],
        compiler_params=pltpu.CompilerParams(vmem_limit_bytes=58 * MEGA),
        cost_estimate=cost(rows * cols),
        name="bundle",
    )(*arrays)


def add_kernel(count, *refs):
    at = 0
    for group in (refs[:count], refs[count : 2 * count]):
        total = full(group[0][...])
        for ref in group[1:]:
            total = total + full(ref[...])
        refs[-1][at : at + total.shape[0], :] = low(total)
        at += total.shape[0]


def run_add(firsts, seconds):
    count, cols = len(firsts), firsts[0].shape[1]
    return pl.pallas_call(
        functools.partial(add_kernel, count),
        in_specs=[ON_CHIP] * (2 * count),
        out_specs=ON_CHIP,
        out_shape=rows_out(firsts[0].shape[0] + seconds[0].shape[0], cols),
        compiler_params=pltpu.CompilerParams(vmem_limit_bytes=14 * MEGA),
        cost_estimate=cost(10**6, 8 * firsts[0].shape[0] * cols),
        name="add",
    )(*firsts, *seconds)


def first_kernel(resid_ref, gain_ref, shift_ref, weight_ref, normed_ref, packed_ref):
    unit, _ = unit_of(full(resid_ref[...]))
    normed = low(unit * gain_ref[...] + shift_ref[...])
    normed_ref[...] = normed
    packed_ref[...] = low(contract_cols(normed, weight_ref[...]))


def run_first(resid, gain, shift, weight):
    rows, model = resid.shape
    tile = min(ROW_TILE, rows)
    cols = weight.shape[0]
    return pl.pallas_call(
        first_kernel,
        grid=(rows // tile,),
        in_specs=[
            tiled(tile, model),
            line(model),
            line(model),
            pl.BlockSpec((cols, model), lambda i: (0, 0), pipeline_mode=pl.Buffered(1)),
        ],
        out_specs=[tiled(tile, model), tiled(tile, cols)],
        out_shape=[rows_out(rows, model), rows_out(rows, cols)],
        compiler_params=pltpu.CompilerParams(vmem_limit_bytes=14 * MEGA),
        cost_estimate=cost(rows * model),
        name="first",
    )(resid, gain, shift, weight)


def project_kernel(rows_ref, weight_ref, packed_ref):
    packed_ref[...] = low(contract_cols(rows_ref[...], weight_ref[...]))


def run_project(rows_in, weight):
    rows, model = rows_in.shape
    tile = min(2 * ROW_TILE, rows)
    cols = weight.shape[0]
    return pl.pallas_call(
        project_kernel,
        grid=(rows // tile,),
        in_specs=[
            tiled(tile, model),
            pl.BlockSpec((cols, model), lambda i: (0, 0), pipeline_mode=pl.Buffered(1)),
        ],
        out_specs=tiled(tile, cols),
        out_shape=rows_out(rows, cols),
        compiler_params=pltpu.CompilerParams(vmem_limit_bytes=12 * MEGA),
        cost_estimate=cost(rows * model),
        name="project",
    )(rows_in, weight)


def last_kernel(parts, *refs):
    (resid_ref, grad_ref, gain_ref), refs = take(refs, 3)
    packed, refs = take(refs, parts)
    joint_w, refs = take(refs, parts)
    out_ref, gain_sum, shift_sum, joint_scr, sems = refs[-5:]
    step = pl.program_id(0)
    copies = [
        pltpu.make_async_copy(joint_w[i], joint_scr.at[i], sems.at[i]) for i in range(parts)
    ]

    @pl.when(step == 0)
    def _():
        for copy in copies:
            copy.start()
        gain_sum[...] = jnp.zeros_like(gain_sum)
        shift_sum[...] = jnp.zeros_like(shift_sum)
        for copy in copies:
            copy.wait()

    unit, inverse = unit_of(full(resid_ref[...]))
    joined = jnp.concatenate([ref[...] for ref in packed], axis=1)
    first_grad = matmul(joined, joint_scr[...].reshape(joined.shape[1], joint_scr.shape[2]))
    out_ref[...] = grad_ref[...] + norm_grad(first_grad, unit, inverse, gain_ref[...])
    gain_sum[...] += column_sum(first_grad * unit)
    shift_sum[...] += column_sum(first_grad)


def run_last(part, part_rows, resid, middle_grad, gain, packed, joint_w, made):
    parts = len(packed)
    rows, model = resid.shape
    tile = min(ROW_TILE, part_rows)
    depth = packed[0].shape[1]
    first = part * part_rows // tile
    return pl.pallas_call(
        functools.partial(last_kernel, parts),
        grid=(part_rows // tile,),
        in_specs=[tiled(tile, model, first)] * 2
        + [line(model)]
        + [tiled(tile, depth, first)] * parts
        + [ANYWHERE] * parts
        + [ANYWHERE] * (made is not None),
        out_specs=[tiled(tile, model, first)] + [line(model)] * 2,
        out_shape=[rows_out(rows, model, jnp.float32)] + [line_out(model)] * 2,
        scratch_shapes=[
            pltpu.VMEM((parts, depth, model), jnp.bfloat16),
            pltpu.SemaphoreType.DMA((parts,)),
        ],
        input_output_aliases={} if made is None else {3 + 2 * parts: 0},
        compiler_params=pltpu.CompilerParams(vmem_limit_bytes=20 * MEGA),
        cost_estimate=cost(2 * part_rows * model * parts * depth, part_rows * model * 20),
        name="last",
    )(resid, middle_grad, gain, *packed, *joint_w, *([] if made is None else [made]))


def swap(values, axis, bit):
    size = lax.axis_size(axis)
    return lax.ppermute(values, axis, [(i, i ^ bit) for i in range(size)])


def after(values, *earlier):
    return lax.optimization_barrier((values, earlier))[0]


def put_halves(upper, mine, other):
    return jnp.where(
        upper == 0,
        jnp.concatenate([mine, other], axis=0),
        jnp.concatenate([other, mine], axis=0),
    )


def half(values, upper):
    rows = values.shape[0] // 2
    return lax.dynamic_slice_in_dim(values, upper * rows, rows, 0)


class GroupSum:
    def __init__(self, values, which=(0, 1), pairs=True):
        bits = [1 << i for i in range(lax.axis_size("dp").bit_length() - 1)]
        orders = []
        for order in (bits, bits[1:2] + bits[:1] + bits[2:]):
            if not pairs:
                orders.append([(bit,) for bit in order])
                continue
            odd = len(order) % 2
            groups = [order[:odd]] + [order[i : i + 2] for i in range(odd, len(order), 2)]
            orders.append([tuple(group) for group in groups if group])
        orders = [orders[n] for n in which]
        part = values.shape[0] // len(orders)
        self.parts = [values[n * part : (n + 1) * part] for n in range(len(orders))]
        self.steps = [
            [(True, group) for group in order] + [(False, group) for group in order[::-1]]
            for order in orders
        ]
        self.pending = None

    def start(self):
        self.pending, sent = [], []
        if not self.steps[0]:
            return tuple(self.parts)
        for values, steps in zip(self.parts, self.steps):
            halving, group = steps.pop(0)
            uppers = [(lax.axis_index("dp") // bit) % 2 for bit in group]
            others = []
            for k in range(1, 1 << len(group)):
                flips = [k >> i & 1 for i in range(len(group))]
                leaving = values
                if halving:
                    for upper, flip in zip(uppers[::-1], flips[::-1]):
                        leaving = half(leaving, 1 - upper if flip else upper)
                sent.append(leaving)
                bit = sum(bit for bit, flip in zip(group, flips) if flip)
                others.append(swap(leaving, "dp", bit))
            if halving:
                for upper in uppers[::-1]:
                    values = half(values, upper)
            self.pending.append((halving, uppers, values, others))
        return tuple(sent)

    def finish(self, *earlier):
        if not self.pending:
            return
        self.parts = []
        for halving, uppers, mine, others in self.pending:
            if earlier:
                others = after(others, *earlier)
            if halving:
                total = full(mine)
                for other in others:
                    total = total + full(other)
                self.parts.append(low(total))
            else:
                pieces = [mine, *others]
                for upper in uppers:
                    pieces = [
                        put_halves(upper, pieces[n], pieces[n + 1])
                        for n in range(0, len(pieces), 2)
                    ]
                self.parts += pieces
        self.pending = None

    def step(self, *earlier):
        self.finish(*earlier)
        return self.start()

    def result(self, cuts=()):
        while self.steps[0] or (self.pending and not cuts):
            self.step()
        if not cuts:
            return full(jnp.concatenate(self.parts, axis=0))
        ((_, uppers, mine, others),) = self.pending
        if len(uppers) > 1:
            self.finish()
            halves = self.parts
        else:
            halves = [
                jnp.where(uppers[0] == 0, mine, others[0]),
                jnp.where(uppers[0] == 0, others[0], mine),
            ]
        edges, outs = [0, *cuts, sum(half.shape[0] for half in halves)], []
        for low_at, high_at in zip(edges, edges[1:]):
            pieces, first = [], 0
            for rows in halves:
                a, b = max(low_at - first, 0), min(high_at - first, rows.shape[0])
                if a < b:
                    pieces.append(rows[a:b])
                first += rows.shape[0]
            outs.append(full(jnp.concatenate(pieces, axis=0)))
        return outs


def sum_all(values):
    for axis in ("tensor", "dp"):
        bits = [1 << i for i in range(lax.axis_size(axis).bit_length() - 1)]
        bits = bits[len(bits) % 2 :] + bits[: len(bits) % 2]
        for i in range(0, len(bits) - 1, 2):
            others = [
                swap(values, axis, bit) for bit in (bits[i], bits[i + 1], bits[i] ^ bits[i + 1])
            ]
            values = (values + others[0]) + (others[1] + others[2])
        if len(bits) % 2:
            values = values + swap(values, axis, bits[-1])
    return values


def split_exact(values):
    terms = []
    for _ in range(3):
        term = lax.reduce_precision(values, 8, 7)
        terms.append(low(term))
        values = values - term
    return terms


def per_device(
    inputs,
    query_weight,
    key_weight,
    value_weight,
    output_weight,
    inner_weight,
    inner_bias,
    outer_weight,
    outer_bias,
    first_gain,
    first_shift,
    second_gain,
    second_shift,
    item_lengths,
    key_mask,
    random_blocks,
    cotangent,
):
    tensor = lax.axis_size("tensor")
    items = item_lengths.shape[0]
    local_rows, model = inputs.shape
    span = local_rows * tensor // items
    members = tensor // items
    place = lax.axis_index("tensor")
    item, member = place // members, place % members
    heads, blocks = random_blocks.shape[1], random_blocks.shape[2]
    lanes = query_weight.shape[0]
    length = span // blocks
    sh = Shape(span, heads, lanes // heads, blocks, SHARED + random_blocks.shape[3])

    def from_item(values, step):
        if step % items == 0:
            return values
        pairs = [
            (t, (t // members - step) % items * members + t % members) for t in range(tensor)
        ]
        return lax.ppermute(values, "tensor", pairs)

    def from_member(values, step):
        if step % members == 0:
            return values
        pairs = [
            (t, t // members * members + (t % members - step) % members) for t in range(tensor)
        ]
        return lax.ppermute(values, "tensor", pairs)

    order = [(s, r) for s in range(items) for r in range(members)]
    away = range(1, items)
    joint = run_bundle([query_weight, key_weight, value_weight])
    upper = lax.axis_index("dp") % 2
    joint_halves = [from_item(half(joint, upper), s) for s in away]

    lines = (first_gain.reshape(1, -1), first_shift.reshape(1, -1))
    firsts = [run_first(from_member(inputs, r), *lines, joint) for r in range(members)]
    first_all = [normed for normed, _ in firsts]

    width = inner_weight.shape[1]
    bias_rows = jnp.stack(split_exact(inner_bias))
    bias_rows = jnp.concatenate([bias_rows, jnp.zeros((13, width), jnp.bfloat16)], axis=0)
    own_weights = [output_weight, inner_weight, outer_weight, bias_rows]
    if width == model:
        sent = [run_bundle([output_weight, outer_weight, bias_rows]), inner_weight]
        views = [(0, 0), (1, 0), (0, lanes), (0, lanes + width)]
    else:
        sent = own_weights
        views = [(n, 0) for n in range(len(own_weights))]

    used = lax.dynamic_index_in_dim(item_lengths, item, 0, False) // length
    flags = lax.dynamic_index_in_dim(key_mask.reshape(items, span), item, 0, False)
    key_ok = (jnp.arange(span, dtype=jnp.int32) < used * length) & (flags == 1)
    bias = jnp.where(jnp.concatenate([key_ok, jnp.zeros((length,), bool)]), 0.0, MASKED)
    bias = jnp.broadcast_to(full(bias)[:, None], (span + length, 128))
    picks = [
        from_item(lax.dynamic_index_in_dim(random_blocks, (item - s) % items, 0, False), s)
        for s in range(items)
    ]
    chosen, usable = jax.vmap(lambda pick: block_lists(used, pick))(jnp.concatenate(picks))
    marked = jnp.where(usable, chosen, blocks)
    chosen, marked = chosen.reshape(items, -1), marked.reshape(items, -1)
    lists = [
        (used.reshape(1), member.reshape(1), chosen[s], marked[s], bias) for s in range(items)
    ]

    packed, made, merged, logs, joint_item = [], [], [], [], [joint]
    rows_in = first_all
    for s in range(items):
        if s == 0:
            group = [packed_rows for _, packed_rows in firsts]
            sent = after(sent, joint_halves)
            joint_others = [swap(rows, "dp", 1) for rows in joint_halves]
            own_sent = after(sent, group[-1])
            own_parts = {
                r: [from_member(array, -r) for array in own_sent] for r in range(1, members)
            }
            item_sent = [own_sent] + [[from_item(array, t) for array in sent] for t in away]
        else:
            halves = after((joint_halves[s - 1], joint_others[s - 1]), made[s - 1][0])
            weight = put_halves(upper, *halves)
            joint_item.append(weight)
            group = [run_project(rows, weight) for rows in rows_in]
        packed.append(group)
        outs, log_rows = attend_forward(sh, after(group, sent, joint_halves), lists[s], 0 if s else 64)
        made.append(outs)
        logs.append(log_rows)
        merged += [from_member(outs[r], -r) for r in range(members)]
        rows_in = after(first_all, outs[0], [arrays[0] for arrays in own_parts.values()])

    part_weights = {}
    for s, r in order:
        if (s, r) == (0, 0):
            part_weights[s, r] = [(array, 0) for array in own_weights]
        else:
            arrays = own_parts[r] if s == 0 else None
            if s:
                early = item_sent[s][:1] if width == model else item_sent[s]
                arrays = [from_member(array, -r) for array in after(early, packed[s])]
                arrays += item_sent[s][len(early) :]
            part_weights[s, r] = [(arrays[n], row) for n, row in views]

    def part_bias(part):
        if part == (0, 0):
            return inner_bias.reshape(1, -1)
        array, row = part_weights[part][3]
        terms = full(array[row : row + 3])
        return (terms[0] + terms[1] + terms[2]).reshape(1, -1)

    groups = [
        [(0, 0)],
        [part for part in order if part[0] > 0],
        [(0, r) for r in range(1, members)],
    ]
    groups = [group for group in groups if group]
    out_full = [part_weights[part][0] for part in order]
    acts, inner_grads, bias_sums = {}, {}, {}

    def outer_product(part):
        return contract_rows(acts[part], cotangent)

    def inner_product(part):
        return contract_rows(second_own, inner_grads[part])

    def output_product(part):
        at = order.index(part) * lanes
        return output_grads[at : at + lanes]

    def send_members(product, s):
        return [from_member(low(product((s, r))), r) for r in range(members - 1, 0, -1)]

    def add_members(product, s, others):
        total = product((s, 0))
        for other in others:
            total = total + full(other)
        return low(total)

    totals = {}
    carried, waits = None, ()
    for n, group in enumerate(groups):
        head = tail = None
        if n == 0:
            lines = [row.reshape(1, -1) for row in (outer_bias, second_gain, second_shift)]
            head = (inputs, lines, merged)
        if n == len(groups) - 1:
            tail = [middle, second_gain.reshape(1, -1)]
        inner_parts = [part_weights[part][1] for part in group]
        if n == 1 and width == model:
            late = after([item_sent[s][1] for s in range(items)], acts[0, 0])
            inner_parts = [(from_member(late[s], -r), 0) for s, r in group]
        plain, group_bias, group_acts, group_grads = run_middle(
            cotangent,
            jnp.concatenate([part_bias(part) for part in group], axis=1),
            inner_parts,
            [part_weights[part][2] for part in group],
            out_full,
            head,
            after(carried, waits) if carried else None,
            tail,
        )
        for i, part in enumerate(group):
            acts[part], inner_grads[part] = group_acts[i], group_grads[i]
            bias_sums[part] = group_bias[:, i * width : (i + 1) * width]
        if n == 0:
            second_own, middle, joined = plain[:3]
            plain = plain[3:]
        if n < len(groups) - 1:
            carried = [second_own, *plain]
        waits = []
        for s in sorted({s for s, _ in group if s > 0}, reverse=True):
            for name, product in (("outer", outer_product), ("inner", inner_product)):
                totals[name, s] = add_members(product, s, send_members(product, s))
                waits.append(totals[name, s])
    outputs, middle_grad, branch, second_gain_sum, second_shift_sum, cot_sum = plain[:6]
    tops = plain[6:]
    output_grads = contract_rows(joined, branch)

    top_rows = [[None] * members for _ in range(items)]
    for i, (s, r) in enumerate(order):
        top_rows[s][r] = from_member(tops[i], r)
    products = {"outer": outer_product, "inner": inner_product, "output": output_product}
    item_sent = {
        name: [from_item(totals[name, s], -s) for s in away] for name in ("outer", "inner")
    }
    member_sent = {name: send_members(product, 0) for name, product in products.items()}
    totals["outer", 0] = add_members(outer_product, 0, member_sent["outer"])
    for s in range(items - 1, -1, -1):
        others = send_members(output_product, s) if s else member_sent["output"]
        totals["output", s] = add_members(output_product, s, others)
    item_sent["output"] = [from_item(totals["output", s], -s) for s in away]

    def add_items(total, others):
        total = full(total)
        for other in others:
            total = total + full(other)
        return low(total)

    packed_grad, joint_totals = [None] * items, [None] * items
    outer_sum = GroupSum(
        add_items(totals["outer", 0], after(item_sent["outer"], branch)), (0,), False
    )
    waits = (outer_sum.start(), member_sent, totals["output", 0])
    inner_sum = None
    back, joint_sent = {}, []
    for s in range(items - 1, -1, -1):
        grads = ()
        for part in range(BACK_PARTS):
            if part:
                waits = outer_sum.step(grads[0])
                if inner_sum is None:
                    others, second_own = after((item_sent, second_own), grads[0], waits)
                    totals["inner", 0] = add_members(inner_product, 0, member_sent["inner"])
                    inner_terms = [totals["inner", 0], *others["inner"]]
                    output_terms = [totals["output", 0], *others["output"]]
                    if width == model:
                        inner_total = run_add(inner_terms, output_terms)
                    else:
                        inner_total = add_items(inner_terms[0], inner_terms[1:])
                        output_sum = GroupSum(add_items(output_terms[0], output_terms[1:]), (0,))
                    inner_sum = GroupSum(inner_total, (1,))
                    waits = (waits, inner_sum.start(), outer_sum.step(inner_total))
                else:
                    waits = (waits, inner_sum.step(grads[0]), joint_sent)
            grads = attend_backward(
                sh,
                packed[s],
                after(top_rows[s], waits),
                made[s],
                logs[s],
                lists[s],
                (part, BACK_PARTS),
                grads,
                0 if s == items - 1 and part == 0 else 32,
            )
        packed_grad[s] = grads
        if s:
            rows = after(grads, outer_sum.step(grads[0]))
        else:
            rows = after(grads, inner_sum.step(grads[0]), outer_sum.step(grads[0]))
        total = contract_rows(rows[0], first_all[0])
        for r in range(1, members):
            total = total + contract_rows(rows[r], first_all[r])
        joint_totals[s] = low(total) if s else total
        waits = joint_totals[s]
        if s:
            waits = (waits, outer_sum.step(total), inner_sum.step(total))
            rows = after(grads, waits)
            joint_sent.append(from_item(joint_totals[s], -s))
        grads = rows
        for r in range(members):
            back[s, r] = from_member(grads[r], -r)

    back = [back[part] for part in order]
    joint_full = [from_member(joint_item[s], -r) for s, r in order]
    end_sum = GroupSum(add_items(joint_totals[0], joint_sent), (0,))
    waits = end_sum.start()
    pieces = []
    cut = local_rows // LAST_PARTS
    for n in range(LAST_PARTS):
        outs = run_last(
            n,
            cut,
            inputs,
            middle_grad,
            first_gain.reshape(1, -1),
            after(back, waits),
            joint_full,
            pieces[-1][0] if pieces else None,
        )
        pieces.append(outs)
        if n == 0:
            waits = end_sum.step(outs[1])
    input_grad = pieces[-1][0]
    vectors = [
        sum(piece[1] for piece in pieces),
        sum(piece[2] for piece in pieces),
        second_gain_sum,
        second_shift_sum,
        cot_sum,
    ]
    bias_rows = jnp.zeros((tensor, width), jnp.float32)
    for s, r in order:
        spot = (item + s) % items * members + (member - r) % members
        bias_rows = lax.dynamic_update_slice(bias_rows, bias_sums[s, r], (spot, 0))
    vectors.append(bias_rows)
    vectors = after(vectors, end_sum.step(), inner_sum.step(pieces[-1][1]))
    small = sum_all(jnp.concatenate([vector.reshape(-1) for vector in vectors]))
    bias_grad = lax.dynamic_slice_in_dim(small, 5 * model + place * width, width, 0)
    small = small[: 5 * model].reshape(5, model)
    end_grad = end_sum.result((lanes, 2 * lanes))
    outer_grad, inner_grad = outer_sum.result(), inner_sum.result()
    if width == model:
        inner_grad, output_grad = inner_grad[:model], inner_grad[model:]
    else:
        output_grad = output_sum.result()
    return (
        outputs,
        input_grad,
        *end_grad,
        output_grad,
        inner_grad,
        bias_grad,
        outer_grad,
        small[4],
        small[0],
        small[1],
        small[2],
        small[3],
    )


def solution(mesh):
    placed = (
        P(("dp", "tensor"), None),
        P("tensor", None),
        P("tensor", None),
        P("tensor", None),
        P("tensor", None),
        P(None, "tensor"),
        P("tensor"),
        P("tensor", None),
        P(),
        P(),
        P(),
        P(),
        P(),
        P("dp"),
        P("dp"),
        P("dp", "tensor", None, None),
        P(("dp", "tensor"), None),
    )
    return jax.shard_map(
        per_device,
        mesh=mesh,
        in_specs=placed,
        out_specs=(
            P(("dp", "tensor"), None),
            P(("dp", "tensor"), None),
            P("tensor", None),
            P("tensor", None),
            P("tensor", None),
            P("tensor", None),
            P(None, "tensor"),
            P("tensor"),
            P("tensor", None),
            P(),
            P(),
            P(),
            P(),
            P(),
        ),
        check_vma=False,
    )
```

```python
import functools

import jax
import jax.numpy as jnp
from jax import lax
from jax.experimental import pallas as pl
from jax.experimental.pallas import tpu as pltpu
from jax.sharding import PartitionSpec as P

EPSILON = 1e-05
MASKED = -1e30
LOG2E = 1.4426950408889634
SHARED = 5
KEY_CHUNK = 512
MEGA = 2**20
ROW_TILE = 256
LAST_PARTS = 2
BACK_PARTS = 2


def contract_rows(left, right):
    return lax.dot_general(
        left, right, (((0,), (0,)), ((), ())), preferred_element_type=jnp.float32
    )


def contract_cols(left, right):
    return lax.dot_general(
        left, right, (((1,), (1,)), ((), ())), preferred_element_type=jnp.float32
    )


def matmul(left, right):
    return lax.dot_general(
        left, right, (((1,), (0,)), ((), ())), preferred_element_type=jnp.float32
    )


def block_lists(blocks_used, random_pick):
    block_count = random_pick.shape[0]
    places = jnp.arange(block_count, dtype=jnp.int32)[:, None]
    fixed_cols = jnp.zeros_like(places)
    chosen = jnp.concatenate(
        [
            places - 1,
            places,
            places + 1,
            fixed_cols,
            fixed_cols + blocks_used - 1,
            random_pick % blocks_used,
        ],
        axis=1,
    )
    inside = (chosen >= 0) & (chosen < blocks_used)
    slot_count = chosen.shape[1]
    before = jnp.arange(slot_count)[:, None] < jnp.arange(slot_count)[None, :]
    repeated = jnp.any(
        (chosen[:, :, None] == chosen[:, None, :]) & inside[:, :, None] & before[None], axis=1
    )
    return (jnp.clip(chosen, 0, block_count - 1), inside & jnp.logical_not(repeated))


def low(values):
    return values.astype(jnp.bfloat16)


def full(values):
    return values.astype(jnp.float32)


class Shape:
    def __init__(self, span, heads, head_size, blocks, slots):
        self.span, self.heads, self.head_size, self.blocks, self.slots = (
            span,
            heads,
            head_size,
            blocks,
            slots,
        )
        self.length = span // blocks
        self.lanes = heads * head_size
        self.columns = heads * self.length
        self.wide = max(1, min(heads, 128 // head_size))
        self.tile = self.wide * head_size
        self.chunk = min(KEY_CHUNK, span)
        self.bias_lanes = min(128, self.columns)


def rows_of(index, length):
    return pl.ds(pl.multiple_of(index * length, length), length)


def spread_heads(block, sh):
    lane = lax.broadcasted_iota(jnp.int32, block.shape, 1) // sh.head_size
    zero = jnp.zeros_like(block)
    return jnp.concatenate([jnp.where(lane == h, block, zero) for h in range(sh.heads)], axis=0)


def pick_heads(stacked, sh):
    lane = lax.broadcasted_iota(jnp.int32, (sh.length, sh.lanes), 1) // sh.head_size
    out = stacked[: sh.length]
    for h in range(1, sh.heads):
        out = jnp.where(lane == h, stacked[h * sh.length : (h + 1) * sh.length], out)
    return out


def mixed_slot(load, idx, j, s, sh):
    cols = []
    for t in range(sh.heads // sh.wide):
        out = None
        for i in range(sh.wide):
            at = idx[((t * sh.wide + i) * sh.blocks + j) * sh.slots + s]
            piece = load(rows_of(at, sh.length), t)
            if i == 0:
                out = piece
            else:
                lane = lax.broadcasted_iota(jnp.int32, piece.shape, 1) // sh.head_size
                out = jnp.where(lane == i, piece, out)
        cols.append(out)
    return cols[0] if len(cols) == 1 else jnp.concatenate(cols, axis=1)


def gather_rows(ref, first, idx, j, sh):
    parts = [
        ref[rows_of(idx[j * sh.slots + s], sh.length), first : first + sh.lanes]
        for s in range(SHARED)
    ]

    def load(rows, t):
        return ref[rows, first + t * sh.tile : first + (t + 1) * sh.tile]

    for s in range(SHARED, sh.slots):
        parts.append(mixed_slot(load, idx, j, s, sh))
    return jnp.concatenate(parts, axis=0)


def widen(bias, sh):
    reps = sh.columns // sh.bias_lanes
    return bias if reps == 1 else jnp.concatenate([bias] * reps, axis=1)


def gather_bias(ref, idx, j, sh):
    parts = [
        widen(ref[rows_of(idx[j * sh.slots + s], sh.length), : sh.bias_lanes], sh)
        for s in range(SHARED)
    ]

    def load(rows, t):
        return ref[rows, : sh.bias_lanes]

    for s in range(SHARED, sh.slots):
        parts.append(mixed_slot(load, idx, j, s, sh))
    return jnp.concatenate(parts, axis=0)


def split_rows(dot, left, right, cuts):
    edges = [0, *cuts, left.shape[0]]
    return jnp.concatenate([dot(left[a:b], right) for a, b in zip(edges, edges[1:])], axis=0)


def each_block(first, count, unroll, blocks_from):
    def many(i, carry):
        blocks_from(first + i * unroll, unroll)
        return carry

    lax.fori_loop(0, count // unroll, many, 0)

    def one(j, carry):
        blocks_from(j, 1)
        return carry

    lax.fori_loop(first + count // unroll * unroll, first + count, one, 0)


def forward_kernel(sh, pieces, unroll, used, member, idx, bidx, *refs):
    packed, bias_ref = refs[:pieces], refs[pieces]
    outs, log_ref = refs[pieces + 1 : 2 * pieces + 1], refs[2 * pieces + 1]
    rows, o_scr, s_scr, sems = refs[2 * pieces + 2 :]
    c = used[0]
    scale = sh.head_size ** (-0.5) * LOG2E
    rows_each = sh.span // pieces
    query, key, value = 0, sh.lanes, 2 * sh.lanes

    def place(r):
        return rows_of(lax.rem(member[0] + r, pieces), rows_each)

    loads = [pltpu.make_async_copy(packed[r], rows.at[place(r)], sems.at[r]) for r in range(pieces)]
    for copy in loads:
        copy.start()
    o_scr[...] = jnp.zeros_like(o_scr)
    log_ref[...] = jnp.zeros_like(log_ref)
    for copy in loads:
        copy.wait()

    def block(j):
        at = rows_of(j, sh.length)
        q_all = spread_heads(rows[at, query : query + sh.lanes], sh)
        scores = contract_cols(gather_rows(rows, key, idx, j, sh), q_all) * scale
        scores = scores + gather_bias(bias_ref, bidx, j, sh)
        top = jnp.max(scores, axis=0, keepdims=True)
        shifted = jnp.exp2(scores - top)
        total = jnp.sum(shifted, axis=0, keepdims=True)
        log_ref[pl.ds(j, 1), :] = top + jnp.log2(total)
        probs = low(shifted * (1.0 / total))
        out = pick_heads(contract_rows(probs, gather_rows(rows, value, idx, j, sh)), sh)
        o_scr[at, :] = low(out)

    def blocks_from(j, count):
        for u in range(count):
            block(j + u)

    each_block(1, c - 2, unroll, blocks_from)

    row = (1, sh.columns)
    ends = [rows_of(j, sh.length) for j in (0, c - 1)]
    q_ends = [spread_heads(rows[at, query : query + sh.lanes], sh) for at in ends]
    chunks = sh.span // sh.chunk

    def first(i, tops):
        keys = rows_of(i, sh.chunk)
        k_rows = rows[keys, key : key + sh.lanes]
        mask = widen(bias_ref[keys, : sh.bias_lanes], sh)
        highest = []
        for n in range(2):
            scores = contract_cols(k_rows, q_ends[n]) * scale + mask
            s_scr[n, keys, :] = scores
            highest.append(jnp.maximum(tops[n], jnp.max(scores, axis=0, keepdims=True)))
        return tuple(highest)

    lowest = jnp.full(row, MASKED, jnp.float32)
    tops = lax.fori_loop(0, chunks, first, (lowest, lowest), unroll=2 - chunks % 2)

    def second(i, carry):
        keys = rows_of(i, sh.chunk)
        v_rows = rows[keys, value : value + sh.lanes]
        found = []
        for n in range(2):
            total, out = carry[n]
            shifted = jnp.exp2(s_scr[n, keys, :] - tops[n])
            total = total + jnp.sum(shifted, axis=0, keepdims=True)
            found.append((total, out + contract_rows(low(shifted), v_rows)))
        return tuple(found)

    empty = (jnp.zeros(row, jnp.float32), jnp.zeros((sh.columns, sh.lanes), jnp.float32))
    found = lax.fori_loop(0, chunks, second, (empty, empty), unroll=2 - chunks % 2)
    square = (sh.columns, sh.columns)
    diagonal = lax.broadcasted_iota(jnp.int32, square, 0) == lax.broadcasted_iota(
        jnp.int32, square, 1
    )
    for n, j in enumerate((0, c - 1)):
        total, out = found[n]
        log_ref[pl.ds(j, 1), :] = tops[n] + jnp.log2(total)
        inverse = jnp.broadcast_to(1.0 / total, square)
        inverse = jnp.sum(jnp.where(diagonal, inverse, 0.0), axis=1, keepdims=True)
        o_scr[ends[n], :] = low(pick_heads(out * inverse, sh))

    stores = [
        pltpu.make_async_copy(o_scr.at[place(r)], outs[r], sems.at[pieces + r])
        for r in range(pieces)
    ]
    for copy in stores:
        copy.start()
    for copy in stores:
        copy.wait()


def backward_kernel(sh, pieces, unroll, part, used, member, idx, bidx, *refs):
    part, parts = part
    packed, tops, made = refs[:pieces], refs[pieces : 2 * pieces], refs[2 * pieces : 3 * pieces]
    refs = refs[3 * pieces :]
    (bias_ref, log_ref), refs = refs[:2], refs[2:]
    carried, refs = refs[: pieces * (part > 0)], refs[pieces * (part > 0) :]
    outs, refs = refs[:pieces], refs[pieces:]
    rows, grads, merged, d_scr, ka_scr, va_scr, sems = refs[:7]
    c = used[0]
    factor = sh.head_size ** (-0.5)
    scale = factor * LOG2E
    rows_each = sh.span // pieces
    query, key, value = 0, sh.lanes, 2 * sh.lanes
    length, slots = sh.length, sh.slots
    keys_each = slots * length

    def place(r):
        return rows_of(lax.rem(member[0] + r, pieces), rows_each)

    loads = []
    for n, (sources, target) in enumerate(((packed, rows), (tops, grads), (made, merged))):
        for r in range(pieces):
            copy = pltpu.make_async_copy(
                sources[r], target.at[place(r)], sems.at[n * pieces + r]
            )
            loads.append(copy)
            copy.start()
    carries = []
    for r in range(pieces if part else 0):
        copy = pltpu.make_async_copy(carried[r], refs[7].at[place(r)], sems.at[4 * pieces + r])
        carries.append(copy)
        copy.start()
    d_scr[:, : sh.lanes] = jnp.zeros((sh.span, sh.lanes), d_scr.dtype)
    ka_scr[...] = jnp.zeros_like(ka_scr)
    va_scr[...] = jnp.zeros_like(va_scr)
    for copy in loads:
        copy.wait()

    def equal_rows(products):
        row = lax.broadcasted_iota(jnp.int32, products.shape, 0)
        column = lax.broadcasted_iota(jnp.int32, products.shape, 1)
        return jnp.sum(
            jnp.where(column % length == row, products, 0.0), axis=0, keepdims=True
        )

    def block(j):
        at = rows_of(j, length)
        q_all = spread_heads(rows[at, query : query + sh.lanes], sh)
        g_all = spread_heads(grads[at, :], sh)
        k_all = gather_rows(rows, key, idx, j, sh)
        v_all = jnp.concatenate([gather_rows(rows, value, idx, j, sh), merged[at, :]], axis=0)
        cuts = [keys_each // 2]
        scores = split_rows(contract_cols, k_all, q_all, cuts) * scale
        prob_grad = split_rows(contract_cols, v_all, g_all, cuts)
        delta = equal_rows(prob_grad[keys_each:])
        scores = scores + gather_bias(bias_ref, bidx, j, sh)
        probs = jnp.exp2(scores - log_ref[pl.ds(j, 1), :])
        score_grad = low(probs * (prob_grad[:keys_each] - delta))
        query_grad = pick_heads(contract_rows(score_grad, k_all), sh) * factor
        d_scr[at, : sh.lanes] = low(query_grad)
        return (
            split_rows(matmul, score_grad, q_all, cuts),
            split_rows(matmul, low(probs), g_all, cuts),
        )

    def random_add(ref, j, value):
        tile = sh.tile
        for s in range(SHARED, slots):
            for h in range(sh.heads):
                t, i = h // sh.wide, h % sh.wide
                at = rows_of(idx[(h * sh.blocks + j) * slots + s], length)
                piece = value[s * length : (s + 1) * length, t * tile : (t + 1) * tile]
                if sh.wide > 1:
                    lane = lax.broadcasted_iota(jnp.int32, piece.shape, 1) // sh.head_size
                    piece = jnp.where(lane == i, piece, 0.0)
                ref[at, t * tile : (t + 1) * tile] += piece

    def blocks_from(j, count):
        gained = [block(j + u) for u in range(count)]
        for which, ref in ((0, ka_scr), (1, va_scr)):

            def slot(u, s):
                return gained[u][which][s * length : (s + 1) * length]

            for n in range(count + 2):
                total = None
                for u in range(count):
                    if 0 <= n - u <= 2:
                        total = slot(u, n - u) if total is None else total + slot(u, n - u)
                ref[rows_of(j - 1 + n, length), :] += total
            for s, target in ((3, 0), (4, c - 1)):
                total = slot(0, s)
                for u in range(1, count):
                    total = total + slot(u, s)
                ref[rows_of(target, length), :] += total
            for u in range(count):
                random_add(ref, j + u, gained[u][which])

    steps = (c - 2) // unroll
    shares = [-(-steps * n // parts) * unroll for n in (part, part + 1)]
    begin, end = shares
    if part == parts - 1:
        end = c - 2
    each_block(1 + begin, end - begin, unroll, blocks_from)

    chunks = sh.span // sh.chunk
    for j in (0, c - 1)[2 * part // parts : 2 * (part + 1) // parts]:
        at = rows_of(j, length)
        q_all = spread_heads(rows[at, query : query + sh.lanes], sh)
        g_all = spread_heads(grads[at, :], sh)
        delta = equal_rows(contract_cols(merged[at, :], g_all))
        log_row = log_ref[pl.ds(j, 1), :]

        def chunk(i, total):
            keys = rows_of(i, sh.chunk)
            k_all = rows[keys, key : key + sh.lanes]
            scores = contract_cols(k_all, q_all) * scale
            scores = scores + widen(bias_ref[keys, : sh.bias_lanes], sh)
            probs = jnp.exp2(scores - log_row)
            prob_grad = contract_cols(rows[keys, value : value + sh.lanes], g_all)
            score_grad = low(probs * (prob_grad - delta))
            ka_scr[keys, :] += matmul(score_grad, q_all)
            va_scr[keys, :] += matmul(low(probs), g_all)
            return total + contract_rows(score_grad, k_all)

        total = jnp.zeros((sh.columns, sh.lanes), jnp.float32)
        total = lax.fori_loop(0, chunks, chunk, total, unroll=2 - chunks % 2)
        d_scr[at, : sh.lanes] = low(pick_heads(total, sh) * factor)

    for copy in carries:
        copy.wait()

    def with_carried(first, values):
        return values + full(refs[7][:, first : first + sh.lanes]) if part else values

    if part:
        d_scr[:, : sh.lanes] = d_scr[:, : sh.lanes] + refs[7][:, : sh.lanes]
    d_scr[:, key : key + sh.lanes] = low(with_carried(key, ka_scr[...] * factor))
    d_scr[:, value : value + sh.lanes] = low(with_carried(value, va_scr[...]))
    stores = [
        pltpu.make_async_copy(d_scr.at[place(r)], outs[r], sems.at[3 * pieces + r])
        for r in range(pieces)
    ]
    for copy in stores:
        copy.start()
    for copy in stores:
        copy.wait()


ANYWHERE = pl.BlockSpec(memory_space=pl.ANY)
ON_CHIP = pl.BlockSpec(memory_space=pltpu.VMEM)
SCALARS = pl.BlockSpec(memory_space=pltpu.SMEM)


def cost(flops, accessed=10**6):
    return pl.CostEstimate(flops=int(flops), bytes_accessed=int(accessed), transcendentals=0)


def attend_cost(sh, weight):
    return cost(weight * sh.blocks * sh.slots * sh.length * sh.columns * sh.lanes)


def attend_forward(sh, packed, lists, weight=16, unroll=15):
    pieces = len(packed)
    used, member, idx, bidx, bias = lists
    rows_each = sh.span // pieces
    outs = pl.pallas_call(
        functools.partial(forward_kernel, sh, pieces, unroll),
        in_specs=[SCALARS] * 4 + [ANYWHERE] * pieces + [ON_CHIP],
        out_specs=[ANYWHERE] * pieces + [ON_CHIP],
        out_shape=[jax.ShapeDtypeStruct((rows_each, sh.lanes), jnp.bfloat16)] * pieces
        + [jax.ShapeDtypeStruct((sh.blocks, sh.columns), jnp.float32)],
        scratch_shapes=[
            pltpu.VMEM((sh.span, 3 * sh.lanes), jnp.bfloat16),
            pltpu.VMEM((sh.span, sh.lanes), jnp.bfloat16),
            pltpu.VMEM((2, sh.span, sh.columns), jnp.float32),
            pltpu.SemaphoreType.DMA((2 * pieces,)),
        ],
        compiler_params=pltpu.CompilerParams(vmem_limit_bytes=34 * MEGA),
        cost_estimate=attend_cost(sh, weight),
        name="attend_forward",
    )(used, member, idx, bidx, *packed, bias)
    return outs[:pieces], outs[pieces]


def attend_backward(sh, packed, tops, made, log_rows, lists, part=(0, 1), carried=(), weight=32, unroll=4):
    pieces = len(packed)
    used, member, idx, bidx, bias = lists
    rows_each = sh.span // pieces
    return pl.pallas_call(
        functools.partial(backward_kernel, sh, pieces, unroll, part),
        in_specs=[SCALARS] * 4
        + [ANYWHERE] * (3 * pieces)
        + [ON_CHIP] * 2
        + [ANYWHERE] * len(carried),
        out_specs=[ANYWHERE] * pieces,
        out_shape=[jax.ShapeDtypeStruct((rows_each, 3 * sh.lanes), jnp.bfloat16)] * pieces,
        scratch_shapes=[
            pltpu.VMEM((sh.span, 3 * sh.lanes), jnp.bfloat16),
            pltpu.VMEM((sh.span, sh.lanes), jnp.bfloat16),
            pltpu.VMEM((sh.span, sh.lanes), jnp.bfloat16),
            pltpu.VMEM((sh.span, 3 * sh.lanes), jnp.bfloat16),
            pltpu.VMEM((sh.span, sh.lanes), jnp.float32),
            pltpu.VMEM((sh.span, sh.lanes), jnp.float32),
            pltpu.SemaphoreType.DMA((5 * pieces,)),
        ]
        + [pltpu.VMEM((sh.span, 3 * sh.lanes), jnp.bfloat16)] * (len(carried) > 0),
        compiler_params=pltpu.CompilerParams(
            vmem_limit_bytes=(40 if carried else 34) * MEGA
        ),
        cost_estimate=attend_cost(sh, weight // part[1]),
        name="attend_backward",
    )(used, member, idx, bidx, *packed, *tops, *made, bias, log_rows, *carried)


GELU_A = (2 / 3.141592653589793) ** 0.5
GELU_B = GELU_A * 0.044715


def gelu_both(pre):
    square = pre * pre
    turn = jnp.tanh(pre * (GELU_A + GELU_B * square))
    half = 0.5 + 0.5 * turn
    act = pre * half
    slope = half + act * (1.0 - turn) * (GELU_A + 3.0 * GELU_B * square)
    return act, slope


def unit_of(rows):
    center = jnp.mean(rows, axis=1, keepdims=True)
    deviation = rows - center
    inverse = lax.rsqrt(jnp.mean(deviation * deviation, axis=1, keepdims=True) + EPSILON)
    return deviation * inverse, inverse


def norm_grad(grad_normed, unit, inverse, gain):
    scaled = grad_normed * gain
    plain_mean = jnp.mean(scaled, axis=1, keepdims=True)
    cross_mean = jnp.mean(scaled * unit, axis=1, keepdims=True)
    return inverse * (scaled - plain_mean - unit * cross_mean)


def column_sum(values):
    return jnp.sum(values, axis=0, keepdims=True)


def take(refs, count):
    return refs[:count], refs[count:]


def tiled(tile, cols, first=0):
    return pl.BlockSpec((tile, cols), lambda i: (first + i, 0))


def line(cols):
    return pl.BlockSpec((1, cols), lambda i: (0, 0))


def line_out(cols):
    return jax.ShapeDtypeStruct((1, cols), jnp.float32)


def rows_out(rows, cols, dtype=jnp.bfloat16):
    return jax.ShapeDtypeStruct((rows, cols), dtype)


def middle_kernel(count, outs_count, head, tail, offsets, *refs):
    (cot_ref, bias_ref), refs = take(refs, 2)
    if head:
        (resid_ref, outer_bias_ref, gain_ref, shift_ref), refs = take(refs, 4)
        merged, refs = take(refs, outs_count)
    else:
        (second_in, total_in, back_in), refs = take(refs, 3)
    if tail:
        (middle_in, gain_in), refs = take(refs, 2)
    out_w, refs = take(refs, outs_count if head or tail else 0)
    inner_w, refs = take(refs, count)
    outer_w, refs = take(refs, count)
    if head:
        (second_ref, middle_ref, joined_ref), refs = take(refs, 3)
    if tail:
        (outputs_ref, grad_ref, branch_ref, gain_sum, shift_sum, cot_sum), refs = take(refs, 6)
        tops, refs = take(refs, outs_count)
    else:
        (total_ref, back_ref), refs = take(refs, 2)
    (bias_sum,), refs = take(refs, 1)
    acts, refs = take(refs, count)
    inner_grads, refs = take(refs, count)
    out_scr, inner_scr, outer_scr, total_scr, back_scr, sems = refs
    step = pl.program_id(0)
    model, width = inner_scr.shape[1:]
    out_copies = []
    for i, ref in enumerate(out_w):
        lanes = out_scr.shape[0] // outs_count
        out_copies.append(
            pltpu.make_async_copy(
                ref.at[pl.ds(offsets[0][i], lanes)], out_scr.at[pl.ds(i * lanes, lanes)], sems.at[i]
            )
        )
    copies = []
    for i in range(count):
        n = outs_count + 2 * i
        inner = inner_w[i].at[pl.ds(offsets[1][i], model)]
        outer = outer_w[i].at[pl.ds(offsets[2][i], width)]
        copies.append(
            [
                pltpu.make_async_copy(inner, inner_scr.at[i], sems.at[n]),
                pltpu.make_async_copy(outer, outer_scr.at[i], sems.at[n + 1]),
            ]
        )

    @pl.when(step == 0)
    def _():
        for copy in out_copies if head else []:
            copy.start()
        for pair in copies:
            for copy in pair:
                copy.start()
        for copy in [] if head else out_copies:
            copy.start()
        for ref in (bias_sum, gain_sum, shift_sum, cot_sum) if tail else (bias_sum,):
            ref[...] = jnp.zeros_like(ref)

    def body(first_step):
        def ready(group):
            if first_step:
                for copy in group:
                    copy.wait()

        cot = cot_ref[...]
        if head:
            ready(out_copies)
            joined = jnp.concatenate([ref[...] for ref in merged], axis=1)
            joined_ref[...] = joined
            middle = full(resid_ref[...]) + matmul(joined, out_scr[...])
            middle_ref[...] = middle
            unit, _ = unit_of(middle)
            second = low(unit * gain_ref[...] + shift_ref[...])
            second_ref[...] = second
            total_scr[...] = middle + outer_bias_ref[...]
        else:
            second = second_in[...]
            total_scr[...] = total_in[...]
            back_scr[...] = back_in[...]
        for i in range(count):
            ready(copies[i])
            pre = matmul(second, inner_scr[i]) + bias_ref[:, i * width : (i + 1) * width]
            grad = contract_cols(cot, outer_scr[i])
            act, slope = gelu_both(pre)
            act = low(act)
            acts[i][...] = act
            grad = grad * slope
            bias_sum[:, i * width : (i + 1) * width] += column_sum(grad)
            grad = low(grad)
            inner_grads[i][...] = grad
            total_scr[...] += matmul(act, outer_scr[i])
            back = contract_cols(grad, inner_scr[i])
            if head and i == 0:
                back_scr[...] = back
            else:
                back_scr[...] += back
        if not tail:
            total_ref[...] = total_scr[...]
            back_ref[...] = back_scr[...]
            return
        outputs_ref[...] = low(total_scr[...])
        second_grad = back_scr[...]
        unit, inverse = unit_of(middle_in[...])
        cot_wide = full(cot)
        middle_grad = cot_wide + norm_grad(second_grad, unit, inverse, gain_in[...])
        gain_sum[...] += column_sum(second_grad * unit)
        shift_sum[...] += column_sum(second_grad)
        cot_sum[...] += column_sum(cot_wide)
        grad_ref[...] = middle_grad
        branch = low(middle_grad)
        branch_ref[...] = branch
        ready([] if head else out_copies)
        top = low(contract_cols(branch, out_scr[...]))
        at = 0
        for ref in tops:
            ref[...] = top[:, at : at + ref.shape[1]]
            at += ref.shape[1]

    @pl.when(step == 0)
    def _():
        body(True)

    @pl.when(step > 0)
    def _():
        body(False)


def run_middle(cot, bias, inner_w, outer_w, out_w, head=None, carried=None, tail=None):
    rows, model = cot.shape
    count, outs_count = len(inner_w), len(out_w)
    tile = min(ROW_TILE, rows)
    width = bias.shape[1] // count
    lanes = model // outs_count
    args, in_specs = [cot, bias], [tiled(tile, model), line(count * width)]
    if head is not None:
        resid, lines, merged = head
        args += [resid, *lines, *merged]
        in_specs += [tiled(tile, model)] + [line(model)] * 3 + [tiled(tile, lanes)] * outs_count
    else:
        args += carried
        in_specs += [tiled(tile, model)] * 3
    if tail is not None:
        args += tail
        in_specs += [tiled(tile, model), line(model)]
    used_out = out_w if head is not None or tail is not None else []
    weights = [*used_out, *inner_w, *outer_w]
    args += [array for array, _ in weights]
    in_specs += [ANYWHERE] * len(weights)
    offsets = [[first for _, first in group] for group in (used_out, inner_w, outer_w)]
    out_specs, out_shape = [], []

    def result(cols, dtype=jnp.bfloat16):
        out_specs.append(tiled(tile, cols))
        out_shape.append(rows_out(rows, cols, dtype))

    if head is not None:
        result(model)
        result(model, jnp.float32)
        result(model)
    if tail is not None:
        result(model)
        result(model, jnp.float32)
        result(model)
        for _ in range(3):
            out_specs.append(line(model))
            out_shape.append(line_out(model))
        for _ in range(outs_count):
            result(lanes)
    else:
        result(model, jnp.float32)
        result(model, jnp.float32)
    out_specs.append(line(count * width))
    out_shape.append(line_out(count * width))
    for _ in range(2 * count):
        result(width)
    outs = pl.pallas_call(
        functools.partial(
            middle_kernel, count, outs_count, head is not None, tail is not None, offsets
        ),
        grid=(rows // tile,),
        in_specs=in_specs,
        out_specs=out_specs,
        out_shape=out_shape,
        scratch_shapes=[
            pltpu.VMEM((model, model), jnp.bfloat16),
            pltpu.VMEM((count, model, width), jnp.bfloat16),
            pltpu.VMEM((count, width, model), jnp.bfloat16),
            pltpu.VMEM((tile, model), jnp.float32),
            pltpu.VMEM((tile, model), jnp.float32),
            pltpu.SemaphoreType.DMA((outs_count + 2 * count,)),
        ],
        compiler_params=pltpu.CompilerParams(vmem_limit_bytes=31 * MEGA),
        cost_estimate=cost(rows * model),
        name="middle",
    )(*args)
    plain, bias_sums = outs[: -2 * count - 1], outs[-2 * count - 1]
    return plain, bias_sums, outs[-2 * count : -count], outs[-count:]


def bundle_kernel(count, *refs):
    sources, target, (held, sems) = refs[:count], refs[count], refs[count + 1 :]
    loads, stores, at = [], [], 0
    for i, source in enumerate(sources):
        rows = pl.ds(at, source.shape[0])
        at += source.shape[0]
        loads.append(pltpu.make_async_copy(source, held.at[rows], sems.at[i]))
        stores.append(pltpu.make_async_copy(held.at[rows], target.at[rows], sems.at[count + i]))
    for copy in loads:
        copy.start()
    for load, store in zip(loads, stores):
        load.wait()
        store.start()
    for copy in stores:
        copy.wait()


def run_bundle(arrays):
    rows, cols = sum(array.shape[0] for array in arrays), arrays[0].shape[1]
    return pl.pallas_call(
        functools.partial(bundle_kernel, len(arrays)),
        in_specs=[ANYWHERE] * len(arrays),
        out_specs=ANYWHERE,
        out_shape=rows_out(rows, cols),
        scratch_shapes=[
            pltpu.VMEM((rows, cols), jnp.bfloat16),
            pltpu.SemaphoreType.DMA((2 * len(arrays),)),
        ],
        compiler_params=pltpu.CompilerParams(vmem_limit_bytes=58 * MEGA),
        cost_estimate=cost(rows * cols),
        name="bundle",
    )(*arrays)


def add_kernel(count, *refs):
    at = 0
    for group in (refs[:count], refs[count : 2 * count]):
        total = full(group[0][...])
        for ref in group[1:]:
            total = total + full(ref[...])
        refs[-1][at : at + total.shape[0], :] = low(total)
        at += total.shape[0]


def run_add(firsts, seconds):
    count, cols = len(firsts), firsts[0].shape[1]
    return pl.pallas_call(
        functools.partial(add_kernel, count),
        in_specs=[ON_CHIP] * (2 * count),
        out_specs=ON_CHIP,
        out_shape=rows_out(firsts[0].shape[0] + seconds[0].shape[0], cols),
        compiler_params=pltpu.CompilerParams(vmem_limit_bytes=14 * MEGA),
        cost_estimate=cost(10**6, 8 * firsts[0].shape[0] * cols),
        name="add",
    )(*firsts, *seconds)


def first_kernel(resid_ref, gain_ref, shift_ref, weight_ref, normed_ref, packed_ref):
    unit, _ = unit_of(full(resid_ref[...]))
    normed = low(unit * gain_ref[...] + shift_ref[...])
    normed_ref[...] = normed
    packed_ref[...] = low(contract_cols(normed, weight_ref[...]))


def run_first(resid, gain, shift, weight):
    rows, model = resid.shape
    tile = min(ROW_TILE, rows)
    cols = weight.shape[0]
    return pl.pallas_call(
        first_kernel,
        grid=(rows // tile,),
        in_specs=[
            tiled(tile, model),
            line(model),
            line(model),
            pl.BlockSpec((cols, model), lambda i: (0, 0), pipeline_mode=pl.Buffered(1)),
        ],
        out_specs=[tiled(tile, model), tiled(tile, cols)],
        out_shape=[rows_out(rows, model), rows_out(rows, cols)],
        compiler_params=pltpu.CompilerParams(vmem_limit_bytes=14 * MEGA),
        cost_estimate=cost(rows * model),
        name="first",
    )(resid, gain, shift, weight)


def project_kernel(rows_ref, weight_ref, packed_ref):
    packed_ref[...] = low(contract_cols(rows_ref[...], weight_ref[...]))


def run_project(rows_in, weight):
    rows, model = rows_in.shape
    tile = min(2 * ROW_TILE, rows)
    cols = weight.shape[0]
    return pl.pallas_call(
        project_kernel,
        grid=(rows // tile,),
        in_specs=[
            tiled(tile, model),
            pl.BlockSpec((cols, model), lambda i: (0, 0), pipeline_mode=pl.Buffered(1)),
        ],
        out_specs=tiled(tile, cols),
        out_shape=rows_out(rows, cols),
        compiler_params=pltpu.CompilerParams(vmem_limit_bytes=12 * MEGA),
        cost_estimate=cost(rows * model),
        name="project",
    )(rows_in, weight)


def last_kernel(parts, *refs):
    (resid_ref, grad_ref, gain_ref), refs = take(refs, 3)
    packed, refs = take(refs, parts)
    joint_w, refs = take(refs, parts)
    out_ref, gain_sum, shift_sum, joint_scr, sems = refs[-5:]
    step = pl.program_id(0)
    copies = [
        pltpu.make_async_copy(joint_w[i], joint_scr.at[i], sems.at[i]) for i in range(parts)
    ]

    @pl.when(step == 0)
    def _():
        for copy in copies:
            copy.start()
        gain_sum[...] = jnp.zeros_like(gain_sum)
        shift_sum[...] = jnp.zeros_like(shift_sum)
        for copy in copies:
            copy.wait()

    unit, inverse = unit_of(full(resid_ref[...]))
    joined = jnp.concatenate([ref[...] for ref in packed], axis=1)
    first_grad = matmul(joined, joint_scr[...].reshape(joined.shape[1], joint_scr.shape[2]))
    out_ref[...] = grad_ref[...] + norm_grad(first_grad, unit, inverse, gain_ref[...])
    gain_sum[...] += column_sum(first_grad * unit)
    shift_sum[...] += column_sum(first_grad)


def run_last(part, part_rows, resid, middle_grad, gain, packed, joint_w, made):
    parts = len(packed)
    rows, model = resid.shape
    tile = min(ROW_TILE, part_rows)
    depth = packed[0].shape[1]
    first = part * part_rows // tile
    return pl.pallas_call(
        functools.partial(last_kernel, parts),
        grid=(part_rows // tile,),
        in_specs=[tiled(tile, model, first)] * 2
        + [line(model)]
        + [tiled(tile, depth, first)] * parts
        + [ANYWHERE] * parts
        + [ANYWHERE] * (made is not None),
        out_specs=[tiled(tile, model, first)] + [line(model)] * 2,
        out_shape=[rows_out(rows, model, jnp.float32)] + [line_out(model)] * 2,
        scratch_shapes=[
            pltpu.VMEM((parts, depth, model), jnp.bfloat16),
            pltpu.SemaphoreType.DMA((parts,)),
        ],
        input_output_aliases={} if made is None else {3 + 2 * parts: 0},
        compiler_params=pltpu.CompilerParams(vmem_limit_bytes=20 * MEGA),
        cost_estimate=cost(2 * part_rows * model * parts * depth, part_rows * model * 20),
        name="last",
    )(resid, middle_grad, gain, *packed, *joint_w, *([] if made is None else [made]))


def swap(values, axis, bit):
    size = lax.axis_size(axis)
    return lax.ppermute(values, axis, [(i, i ^ bit) for i in range(size)])


def after(values, *earlier):
    return lax.optimization_barrier((values, earlier))[0]


def put_halves(upper, mine, other):
    return jnp.where(
        upper == 0,
        jnp.concatenate([mine, other], axis=0),
        jnp.concatenate([other, mine], axis=0),
    )


def half(values, upper):
    rows = values.shape[0] // 2
    return lax.dynamic_slice_in_dim(values, upper * rows, rows, 0)


class GroupSum:
    def __init__(self, values, which=(0, 1), pairs=True):
        bits = [1 << i for i in range(lax.axis_size("dp").bit_length() - 1)]
        orders = []
        for order in (bits, bits[1:2] + bits[:1] + bits[2:]):
            if not pairs:
                orders.append([(bit,) for bit in order])
                continue
            odd = len(order) % 2
            groups = [order[:odd]] + [order[i : i + 2] for i in range(odd, len(order), 2)]
            orders.append([tuple(group) for group in groups if group])
        orders = [orders[n] for n in which]
        part = values.shape[0] // len(orders)
        self.parts = [values[n * part : (n + 1) * part] for n in range(len(orders))]
        self.steps = [
            [(True, group) for group in order] + [(False, group) for group in order[::-1]]
            for order in orders
        ]
        self.pending = None

    def start(self):
        self.pending, sent = [], []
        if not self.steps[0]:
            return tuple(self.parts)
        for values, steps in zip(self.parts, self.steps):
            halving, group = steps.pop(0)
            uppers = [(lax.axis_index("dp") // bit) % 2 for bit in group]
            others = []
            for k in range(1, 1 << len(group)):
                flips = [k >> i & 1 for i in range(len(group))]
                leaving = values
                if halving:
                    for upper, flip in zip(uppers[::-1], flips[::-1]):
                        leaving = half(leaving, 1 - upper if flip else upper)
                sent.append(leaving)
                bit = sum(bit for bit, flip in zip(group, flips) if flip)
                others.append(swap(leaving, "dp", bit))
            if halving:
                for upper in uppers[::-1]:
                    values = half(values, upper)
            self.pending.append((halving, uppers, values, others))
        return tuple(sent)

    def finish(self, *earlier):
        if not self.pending:
            return
        self.parts = []
        for halving, uppers, mine, others in self.pending:
            if earlier:
                others = after(others, *earlier)
            if halving:
                total = full(mine)
                for other in others:
                    total = total + full(other)
                self.parts.append(low(total))
            else:
                pieces = [mine, *others]
                for upper in uppers:
                    pieces = [
                        put_halves(upper, pieces[n], pieces[n + 1])
                        for n in range(0, len(pieces), 2)
                    ]
                self.parts += pieces
        self.pending = None

    def step(self, *earlier):
        self.finish(*earlier)
        return self.start()

    def result(self, cuts=()):
        while self.steps[0] or (self.pending and not cuts):
            self.step()
        if not cuts:
            return full(jnp.concatenate(self.parts, axis=0))
        ((_, uppers, mine, others),) = self.pending
        if len(uppers) > 1:
            self.finish()
            halves = self.parts
        else:
            halves = [
                jnp.where(uppers[0] == 0, mine, others[0]),
                jnp.where(uppers[0] == 0, others[0], mine),
            ]
        edges, outs = [0, *cuts, sum(half.shape[0] for half in halves)], []
        for low_at, high_at in zip(edges, edges[1:]):
            pieces, first = [], 0
            for rows in halves:
                a, b = max(low_at - first, 0), min(high_at - first, rows.shape[0])
                if a < b:
                    pieces.append(rows[a:b])
                first += rows.shape[0]
            outs.append(full(jnp.concatenate(pieces, axis=0)))
        return outs


def sum_all(values):
    for axis in ("tensor", "dp"):
        bits = [1 << i for i in range(lax.axis_size(axis).bit_length() - 1)]
        bits = bits[len(bits) % 2 :] + bits[: len(bits) % 2]
        for i in range(0, len(bits) - 1, 2):
            others = [
                swap(values, axis, bit) for bit in (bits[i], bits[i + 1], bits[i] ^ bits[i + 1])
            ]
            values = (values + others[0]) + (others[1] + others[2])
        if len(bits) % 2:
            values = values + swap(values, axis, bits[-1])
    return values


def split_exact(values):
    terms = []
    for _ in range(3):
        term = lax.reduce_precision(values, 8, 7)
        terms.append(low(term))
        values = values - term
    return terms


def per_device(
    inputs,
    query_weight,
    key_weight,
    value_weight,
    output_weight,
    inner_weight,
    inner_bias,
    outer_weight,
    outer_bias,
    first_gain,
    first_shift,
    second_gain,
    second_shift,
    item_lengths,
    key_mask,
    random_blocks,
    cotangent,
):
    tensor = lax.axis_size("tensor")
    items = item_lengths.shape[0]
    local_rows, model = inputs.shape
    span = local_rows * tensor // items
    members = tensor // items
    place = lax.axis_index("tensor")
    item, member = place // members, place % members
    heads, blocks = random_blocks.shape[1], random_blocks.shape[2]
    lanes = query_weight.shape[0]
    length = span // blocks
    sh = Shape(span, heads, lanes // heads, blocks, SHARED + random_blocks.shape[3])

    def from_item(values, step):
        if step % items == 0:
            return values
        pairs = [
            (t, (t // members - step) % items * members + t % members) for t in range(tensor)
        ]
        return lax.ppermute(values, "tensor", pairs)

    def from_member(values, step):
        if step % members == 0:
            return values
        pairs = [
            (t, t // members * members + (t % members - step) % members) for t in range(tensor)
        ]
        return lax.ppermute(values, "tensor", pairs)

    order = [(s, r) for s in range(items) for r in range(members)]
    away = range(1, items)
    joint = run_bundle([query_weight, key_weight, value_weight])
    upper = lax.axis_index("dp") % 2
    joint_halves = [from_item(half(joint, upper), s) for s in away]

    lines = (first_gain.reshape(1, -1), first_shift.reshape(1, -1))
    firsts = [run_first(from_member(inputs, r), *lines, joint) for r in range(members)]
    first_all = [normed for normed, _ in firsts]

    width = inner_weight.shape[1]
    bias_rows = jnp.stack(split_exact(inner_bias))
    bias_rows = jnp.concatenate([bias_rows, jnp.zeros((13, width), jnp.bfloat16)], axis=0)
    own_weights = [output_weight, inner_weight, outer_weight, bias_rows]
    if width == model:
        sent = [run_bundle([output_weight, outer_weight, bias_rows]), inner_weight]
        views = [(0, 0), (1, 0), (0, lanes), (0, lanes + width)]
    else:
        sent = own_weights
        views = [(n, 0) for n in range(len(own_weights))]

    used = lax.dynamic_index_in_dim(item_lengths, item, 0, False) // length
    flags = lax.dynamic_index_in_dim(key_mask.reshape(items, span), item, 0, False)
    key_ok = (jnp.arange(span, dtype=jnp.int32) < used * length) & (flags == 1)
    bias = jnp.where(jnp.concatenate([key_ok, jnp.zeros((length,), bool)]), 0.0, MASKED)
    bias = jnp.broadcast_to(full(bias)[:, None], (span + length, 128))
    picks = [
        from_item(lax.dynamic_index_in_dim(random_blocks, (item - s) % items, 0, False), s)
        for s in range(items)
    ]
    chosen, usable = jax.vmap(lambda pick: block_lists(used, pick))(jnp.concatenate(picks))
    marked = jnp.where(usable, chosen, blocks)
    chosen, marked = chosen.reshape(items, -1), marked.reshape(items, -1)
    lists = [
        (used.reshape(1), member.reshape(1), chosen[s], marked[s], bias) for s in range(items)
    ]

    packed, made, merged, logs, joint_item = [], [], [], [], [joint]
    rows_in = first_all
    for s in range(items):
        if s == 0:
            group = [packed_rows for _, packed_rows in firsts]
            sent = after(sent, joint_halves)
            joint_others = [swap(rows, "dp", 1) for rows in joint_halves]
            own_sent = after(sent, group[-1])
            own_parts = {
                r: [from_member(array, -r) for array in own_sent] for r in range(1, members)
            }
            item_sent = [own_sent] + [[from_item(array, t) for array in sent] for t in away]
        else:
            halves = after((joint_halves[s - 1], joint_others[s - 1]), made[s - 1][0])
            weight = put_halves(upper, *halves)
            joint_item.append(weight)
            group = [run_project(rows, weight) for rows in rows_in]
        packed.append(group)
        outs, log_rows = attend_forward(sh, after(group, sent, joint_halves), lists[s], 0 if s else 64)
        made.append(outs)
        logs.append(log_rows)
        merged += [from_member(outs[r], -r) for r in range(members)]
        rows_in = after(first_all, outs[0], [arrays[0] for arrays in own_parts.values()])

    part_weights = {}
    for s, r in order:
        if (s, r) == (0, 0):
            part_weights[s, r] = [(array, 0) for array in own_weights]
        else:
            arrays = own_parts[r] if s == 0 else None
            if s:
                early = item_sent[s][:1] if width == model else item_sent[s]
                arrays = [from_member(array, -r) for array in after(early, made[-1][0])]
                arrays += item_sent[s][len(early) :]
            part_weights[s, r] = [(arrays[n], row) for n, row in views]

    def part_bias(part):
        if part == (0, 0):
            return inner_bias.reshape(1, -1)
        array, row = part_weights[part][3]
        terms = full(array[row : row + 3])
        return (terms[0] + terms[1] + terms[2]).reshape(1, -1)

    groups = [
        [(0, 0)],
        [part for part in order if part[0] > 0],
        [(0, r) for r in range(1, members)],
    ]
    groups = [group for group in groups if group]
    out_full = [part_weights[part][0] for part in order]
    acts, inner_grads, bias_sums = {}, {}, {}

    def outer_product(part):
        return contract_rows(acts[part], cotangent)

    def inner_product(part):
        return contract_rows(second_own, inner_grads[part])

    def output_product(part):
        at = order.index(part) * lanes
        return output_grads[at : at + lanes]

    def send_members(product, s):
        return [from_member(low(product((s, r))), r) for r in range(members - 1, 0, -1)]

    def add_members(product, s, others):
        total = product((s, 0))
        for other in others:
            total = total + full(other)
        return low(total)

    totals = {}
    carried, waits = None, ()
    for n, group in enumerate(groups):
        head = tail = None
        if n == 0:
            lines = [row.reshape(1, -1) for row in (outer_bias, second_gain, second_shift)]
            head = (inputs, lines, merged)
        if n == len(groups) - 1:
            tail = [middle, second_gain.reshape(1, -1)]
        inner_parts = [part_weights[part][1] for part in group]
        if n == 1 and width == model:
            late = after([item_sent[s][1] for s in range(items)], acts[0, 0])
            inner_parts = [(from_member(late[s], -r), 0) for s, r in group]
        plain, group_bias, group_acts, group_grads = run_middle(
            cotangent,
            jnp.concatenate([part_bias(part) for part in group], axis=1),
            inner_parts,
            [part_weights[part][2] for part in group],
            out_full,
            head,
            after(carried, waits) if carried else None,
            tail,
        )
        for i, part in enumerate(group):
            acts[part], inner_grads[part] = group_acts[i], group_grads[i]
            bias_sums[part] = group_bias[:, i * width : (i + 1) * width]
        if n == 0:
            second_own, middle, joined = plain[:3]
            plain = plain[3:]
        if n < len(groups) - 1:
            carried = [second_own, *plain]
        waits = []
        for s in sorted({s for s, _ in group if s > 0}, reverse=True):
            for name, product in (("outer", outer_product), ("inner", inner_product)):
                totals[name, s] = add_members(product, s, send_members(product, s))
                waits.append(totals[name, s])
    outputs, middle_grad, branch, second_gain_sum, second_shift_sum, cot_sum = plain[:6]
    tops = plain[6:]
    output_grads = contract_rows(joined, branch)

    top_rows = [[None] * members for _ in range(items)]
    for i, (s, r) in enumerate(order):
        top_rows[s][r] = from_member(tops[i], r)
    products = {"outer": outer_product, "inner": inner_product, "output": output_product}
    item_sent = {
        name: [from_item(totals[name, s], -s) for s in away] for name in ("outer", "inner")
    }
    member_sent = {name: send_members(product, 0) for name, product in products.items()}
    totals["outer", 0] = add_members(outer_product, 0, member_sent["outer"])
    for s in range(items - 1, -1, -1):
        others = send_members(output_product, s) if s else member_sent["output"]
        totals["output", s] = add_members(output_product, s, others)
    item_sent["output"] = [from_item(totals["output", s], -s) for s in away]

    def add_items(total, others):
        total = full(total)
        for other in others:
            total = total + full(other)
        return low(total)

    packed_grad, joint_totals = [None] * items, [None] * items
    outer_sum = GroupSum(
        add_items(totals["outer", 0], after(item_sent["outer"], branch)), (0,), False
    )
    waits = (outer_sum.start(), member_sent, totals["output", 0])
    inner_sum = None
    back, joint_sent = {}, []
    for s in range(items - 1, -1, -1):
        grads = ()
        for part in range(BACK_PARTS):
            if part:
                waits = outer_sum.step(grads[0])
                if inner_sum is None:
                    others, second_own = after((item_sent, second_own), grads[0], waits)
                    totals["inner", 0] = add_members(inner_product, 0, member_sent["inner"])
                    inner_terms = [totals["inner", 0], *others["inner"]]
                    output_terms = [totals["output", 0], *others["output"]]
                    if width == model:
                        inner_total = run_add(inner_terms, output_terms)
                    else:
                        inner_total = add_items(inner_terms[0], inner_terms[1:])
                        output_sum = GroupSum(add_items(output_terms[0], output_terms[1:]), (0,))
                    inner_sum = GroupSum(inner_total, (1,))
                    waits = (waits, inner_sum.start(), outer_sum.step(inner_total))
                else:
                    waits = (waits, inner_sum.step(grads[0]), joint_sent)
            grads = attend_backward(
                sh,
                packed[s],
                after(top_rows[s], waits),
                made[s],
                logs[s],
                lists[s],
                (part, BACK_PARTS),
                grads,
                0 if s == items - 1 and part == 0 else 32,
            )
        packed_grad[s] = grads
        if s:
            rows = after(grads, outer_sum.step(grads[0]))
        else:
            rows = after(grads, inner_sum.step(grads[0]), outer_sum.step(grads[0]))
        total = contract_rows(rows[0], first_all[0])
        for r in range(1, members):
            total = total + contract_rows(rows[r], first_all[r])
        joint_totals[s] = low(total) if s else total
        waits = joint_totals[s]
        if s:
            waits = (waits, outer_sum.step(total), inner_sum.step(total))
            rows = after(grads, waits)
            joint_sent.append(from_item(joint_totals[s], -s))
        grads = rows
        for r in range(members):
            back[s, r] = from_member(grads[r], -r)

    back = [back[part] for part in order]
    joint_full = [from_member(joint_item[s], -r) for s, r in order]
    end_sum = GroupSum(add_items(joint_totals[0], joint_sent), (0,))
    waits = end_sum.start()
    pieces = []
    cut = local_rows // LAST_PARTS
    for n in range(LAST_PARTS):
        outs = run_last(
            n,
            cut,
            inputs,
            middle_grad,
            first_gain.reshape(1, -1),
            after(back, waits),
            joint_full,
            pieces[-1][0] if pieces else None,
        )
        pieces.append(outs)
        if n == 0:
            waits = end_sum.step(outs[1])
    input_grad = pieces[-1][0]
    vectors = [
        sum(piece[1] for piece in pieces),
        sum(piece[2] for piece in pieces),
        second_gain_sum,
        second_shift_sum,
        cot_sum,
    ]
    bias_rows = jnp.zeros((tensor, width), jnp.float32)
    for s, r in order:
        spot = (item + s) % items * members + (member - r) % members
        bias_rows = lax.dynamic_update_slice(bias_rows, bias_sums[s, r], (spot, 0))
    vectors.append(bias_rows)
    vectors = after(vectors, end_sum.step())
    arriving = [others for *_, others in inner_sum.pending]
    vectors = after(vectors, arriving)
    small = sum_all(jnp.concatenate([vector.reshape(-1) for vector in vectors]))
    bias_grad = lax.dynamic_slice_in_dim(small, 5 * model + place * width, width, 0)
    small = small[: 5 * model].reshape(5, model)
    end_grad = end_sum.result((lanes, 2 * lanes))
    outer_grad, inner_grad = outer_sum.result(), inner_sum.result()
    if width == model:
        inner_grad, output_grad = inner_grad[:model], inner_grad[model:]
    else:
        output_grad = output_sum.result()
    return (
        outputs,
        input_grad,
        *end_grad,
        output_grad,
        inner_grad,
        bias_grad,
        outer_grad,
        small[4],
        small[0],
        small[1],
        small[2],
        small[3],
    )


def solution(mesh):
    placed = (
        P(("dp", "tensor"), None),
        P("tensor", None),
        P("tensor", None),
        P("tensor", None),
        P("tensor", None),
        P(None, "tensor"),
        P("tensor"),
        P("tensor", None),
        P(),
        P(),
        P(),
        P(),
        P(),
        P("dp"),
        P("dp"),
        P("dp", "tensor", None, None),
        P(("dp", "tensor"), None),
    )
    return jax.shard_map(
        per_device,
        mesh=mesh,
        in_specs=placed,
        out_specs=(
            P(("dp", "tensor"), None),
            P(("dp", "tensor"), None),
            P("tensor", None),
            P("tensor", None),
            P("tensor", None),
            P("tensor", None),
            P(None, "tensor"),
            P("tensor"),
            P("tensor", None),
            P(),
            P(),
            P(),
            P(),
            P(),
        ),
        check_vma=False,
    )
```

```python
import functools

import jax
import jax.numpy as jnp
from jax import lax
from jax.experimental import pallas as pl
from jax.experimental.pallas import tpu as pltpu
from jax.sharding import PartitionSpec as P

EPSILON = 1e-05
MASKED = -1e30
LOG2E = 1.4426950408889634
SHARED = 5
KEY_CHUNK = 512
MEGA = 2**20
ROW_TILE = 256
LAST_PARTS = 2
BACK_PARTS = 2


def contract_rows(left, right):
    return lax.dot_general(
        left, right, (((0,), (0,)), ((), ())), preferred_element_type=jnp.float32
    )


def contract_cols(left, right):
    return lax.dot_general(
        left, right, (((1,), (1,)), ((), ())), preferred_element_type=jnp.float32
    )


def matmul(left, right):
    return lax.dot_general(
        left, right, (((1,), (0,)), ((), ())), preferred_element_type=jnp.float32
    )


def block_lists(blocks_used, random_pick):
    block_count = random_pick.shape[0]
    places = jnp.arange(block_count, dtype=jnp.int32)[:, None]
    fixed_cols = jnp.zeros_like(places)
    chosen = jnp.concatenate(
        [
            places - 1,
            places,
            places + 1,
            fixed_cols,
            fixed_cols + blocks_used - 1,
            random_pick % blocks_used,
        ],
        axis=1,
    )
    inside = (chosen >= 0) & (chosen < blocks_used)
    slot_count = chosen.shape[1]
    before = jnp.arange(slot_count)[:, None] < jnp.arange(slot_count)[None, :]
    repeated = jnp.any(
        (chosen[:, :, None] == chosen[:, None, :]) & inside[:, :, None] & before[None], axis=1
    )
    return (jnp.clip(chosen, 0, block_count - 1), inside & jnp.logical_not(repeated))


def low(values):
    return values.astype(jnp.bfloat16)


def full(values):
    return values.astype(jnp.float32)


class Shape:
    def __init__(self, span, heads, head_size, blocks, slots):
        self.span, self.heads, self.head_size, self.blocks, self.slots = (
            span,
            heads,
            head_size,
            blocks,
            slots,
        )
        self.length = span // blocks
        self.lanes = heads * head_size
        self.columns = heads * self.length
        self.wide = max(1, min(heads, 128 // head_size))
        self.tile = self.wide * head_size
        self.chunk = min(KEY_CHUNK, span)
        self.bias_lanes = min(128, self.columns)


def rows_of(index, length):
    return pl.ds(pl.multiple_of(index * length, length), length)


def spread_heads(block, sh):
    lane = lax.broadcasted_iota(jnp.int32, block.shape, 1) // sh.head_size
    zero = jnp.zeros_like(block)
    return jnp.concatenate([jnp.where(lane == h, block, zero) for h in range(sh.heads)], axis=0)


def pick_heads(stacked, sh):
    lane = lax.broadcasted_iota(jnp.int32, (sh.length, sh.lanes), 1) // sh.head_size
    out = stacked[: sh.length]
    for h in range(1, sh.heads):
        out = jnp.where(lane == h, stacked[h * sh.length : (h + 1) * sh.length], out)
    return out


def mixed_slot(load, idx, j, s, sh):
    cols = []
    for t in range(sh.heads // sh.wide):
        out = None
        for i in range(sh.wide):
            at = idx[((t * sh.wide + i) * sh.blocks + j) * sh.slots + s]
            piece = load(rows_of(at, sh.length), t)
            if i == 0:
                out = piece
            else:
                lane = lax.broadcasted_iota(jnp.int32, piece.shape, 1) // sh.head_size
                out = jnp.where(lane == i, piece, out)
        cols.append(out)
    return cols[0] if len(cols) == 1 else jnp.concatenate(cols, axis=1)


def gather_rows(ref, first, idx, j, sh):
    parts = [
        ref[rows_of(idx[j * sh.slots + s], sh.length), first : first + sh.lanes]
        for s in range(SHARED)
    ]

    def load(rows, t):
        return ref[rows, first + t * sh.tile : first + (t + 1) * sh.tile]

    for s in range(SHARED, sh.slots):
        parts.append(mixed_slot(load, idx, j, s, sh))
    return jnp.concatenate(parts, axis=0)


def widen(bias, sh):
    reps = sh.columns // sh.bias_lanes
    return bias if reps == 1 else jnp.concatenate([bias] * reps, axis=1)


def gather_bias(ref, idx, j, sh):
    parts = [
        widen(ref[rows_of(idx[j * sh.slots + s], sh.length), : sh.bias_lanes], sh)
        for s in range(SHARED)
    ]

    def load(rows, t):
        return ref[rows, : sh.bias_lanes]

    for s in range(SHARED, sh.slots):
        parts.append(mixed_slot(load, idx, j, s, sh))
    return jnp.concatenate(parts, axis=0)


def split_rows(dot, left, right, cuts):
    edges = [0, *cuts, left.shape[0]]
    return jnp.concatenate([dot(left[a:b], right) for a, b in zip(edges, edges[1:])], axis=0)


def each_block(first, count, unroll, blocks_from):
    def many(i, carry):
        blocks_from(first + i * unroll, unroll)
        return carry

    lax.fori_loop(0, count // unroll, many, 0)

    def one(j, carry):
        blocks_from(j, 1)
        return carry

    lax.fori_loop(first + count // unroll * unroll, first + count, one, 0)


def forward_kernel(sh, pieces, unroll, used, member, idx, bidx, *refs):
    packed, bias_ref = refs[:pieces], refs[pieces]
    outs, log_ref = refs[pieces + 1 : 2 * pieces + 1], refs[2 * pieces + 1]
    rows, o_scr, s_scr, sems = refs[2 * pieces + 2 :]
    c = used[0]
    scale = sh.head_size ** (-0.5) * LOG2E
    rows_each = sh.span // pieces
    query, key, value = 0, sh.lanes, 2 * sh.lanes

    def place(r):
        return rows_of(lax.rem(member[0] + r, pieces), rows_each)

    loads = [pltpu.make_async_copy(packed[r], rows.at[place(r)], sems.at[r]) for r in range(pieces)]
    for copy in loads:
        copy.start()
    o_scr[...] = jnp.zeros_like(o_scr)
    log_ref[...] = jnp.zeros_like(log_ref)
    for copy in loads:
        copy.wait()

    def block(j):
        at = rows_of(j, sh.length)
        q_all = spread_heads(rows[at, query : query + sh.lanes], sh)
        scores = contract_cols(gather_rows(rows, key, idx, j, sh), q_all) * scale
        scores = scores + gather_bias(bias_ref, bidx, j, sh)
        top = jnp.max(scores, axis=0, keepdims=True)
        shifted = jnp.exp2(scores - top)
        total = jnp.sum(shifted, axis=0, keepdims=True)
        log_ref[pl.ds(j, 1), :] = top + jnp.log2(total)
        probs = low(shifted * (1.0 / total))
        out = pick_heads(contract_rows(probs, gather_rows(rows, value, idx, j, sh)), sh)
        o_scr[at, :] = low(out)

    def blocks_from(j, count):
        for u in range(count):
            block(j + u)

    each_block(1, c - 2, unroll, blocks_from)

    row = (1, sh.columns)
    ends = [rows_of(j, sh.length) for j in (0, c - 1)]
    q_ends = [spread_heads(rows[at, query : query + sh.lanes], sh) for at in ends]
    chunks = sh.span // sh.chunk

    def first(i, tops):
        keys = rows_of(i, sh.chunk)
        k_rows = rows[keys, key : key + sh.lanes]
        mask = widen(bias_ref[keys, : sh.bias_lanes], sh)
        highest = []
        for n in range(2):
            scores = contract_cols(k_rows, q_ends[n]) * scale + mask
            s_scr[n, keys, :] = scores
            highest.append(jnp.maximum(tops[n], jnp.max(scores, axis=0, keepdims=True)))
        return tuple(highest)

    lowest = jnp.full(row, MASKED, jnp.float32)
    tops = lax.fori_loop(0, chunks, first, (lowest, lowest), unroll=2 - chunks % 2)

    def second(i, carry):
        keys = rows_of(i, sh.chunk)
        v_rows = rows[keys, value : value + sh.lanes]
        found = []
        for n in range(2):
            total, out = carry[n]
            shifted = jnp.exp2(s_scr[n, keys, :] - tops[n])
            total = total + jnp.sum(shifted, axis=0, keepdims=True)
            found.append((total, out + contract_rows(low(shifted), v_rows)))
        return tuple(found)

    empty = (jnp.zeros(row, jnp.float32), jnp.zeros((sh.columns, sh.lanes), jnp.float32))
    found = lax.fori_loop(0, chunks, second, (empty, empty), unroll=2 - chunks % 2)
    square = (sh.columns, sh.columns)
    diagonal = lax.broadcasted_iota(jnp.int32, square, 0) == lax.broadcasted_iota(
        jnp.int32, square, 1
    )
    for n, j in enumerate((0, c - 1)):
        total, out = found[n]
        log_ref[pl.ds(j, 1), :] = tops[n] + jnp.log2(total)
        inverse = jnp.broadcast_to(1.0 / total, square)
        inverse = jnp.sum(jnp.where(diagonal, inverse, 0.0), axis=1, keepdims=True)
        o_scr[ends[n], :] = low(pick_heads(out * inverse, sh))

    stores = [
        pltpu.make_async_copy(o_scr.at[place(r)], outs[r], sems.at[pieces + r])
        for r in range(pieces)
    ]
    for copy in stores:
        copy.start()
    for copy in stores:
        copy.wait()


def backward_kernel(sh, pieces, unroll, part, used, member, idx, bidx, *refs):
    part, parts = part
    packed, tops = refs[:pieces], refs[pieces : 2 * pieces]
    refs = refs[2 * pieces :]
    (bias_ref, log_ref), refs = refs[:2], refs[2:]
    carried, refs = refs[: pieces * (part > 0)], refs[pieces * (part > 0) :]
    outs, refs = refs[:pieces], refs[pieces:]
    rows, grads, d_scr, ka_scr, va_scr, p_scr, sems = refs[:7]
    c = used[0]
    factor = sh.head_size ** (-0.5)
    scale = factor * LOG2E
    rows_each = sh.span // pieces
    query, key, value = 0, sh.lanes, 2 * sh.lanes
    length, slots = sh.length, sh.slots
    keys_each = slots * length

    def place(r):
        return rows_of(lax.rem(member[0] + r, pieces), rows_each)

    loads = []
    for n, (sources, target) in enumerate(((packed, rows), (tops, grads))):
        for r in range(pieces):
            copy = pltpu.make_async_copy(
                sources[r], target.at[place(r)], sems.at[n * pieces + r]
            )
            loads.append(copy)
            copy.start()
    carries = []
    for r in range(pieces if part else 0):
        copy = pltpu.make_async_copy(carried[r], refs[7].at[place(r)], sems.at[3 * pieces + r])
        carries.append(copy)
        copy.start()
    d_scr[:, : sh.lanes] = jnp.zeros((sh.span, sh.lanes), d_scr.dtype)
    ka_scr[...] = jnp.zeros_like(ka_scr)
    va_scr[...] = jnp.zeros_like(va_scr)
    for copy in loads:
        copy.wait()

    def block(j):
        at = rows_of(j, length)
        q_all = spread_heads(rows[at, query : query + sh.lanes], sh)
        g_all = spread_heads(grads[at, :], sh)
        k_all = gather_rows(rows, key, idx, j, sh)
        v_all = gather_rows(rows, value, idx, j, sh)
        cuts = [keys_each // 2]
        scores = split_rows(contract_cols, k_all, q_all, cuts) * scale
        prob_grad = split_rows(contract_cols, v_all, g_all, cuts)
        scores = scores + gather_bias(bias_ref, bidx, j, sh)
        probs = jnp.exp2(scores - log_ref[pl.ds(j, 1), :])
        delta = jnp.sum(probs * prob_grad, axis=0, keepdims=True)
        score_grad = low(probs * (prob_grad - delta))
        query_grad = pick_heads(contract_rows(score_grad, k_all), sh) * factor
        d_scr[at, : sh.lanes] = low(query_grad)
        return (
            split_rows(matmul, score_grad, q_all, cuts),
            split_rows(matmul, low(probs), g_all, cuts),
        )

    def random_add(ref, j, value):
        tile = sh.tile
        for s in range(SHARED, slots):
            for h in range(sh.heads):
                t, i = h // sh.wide, h % sh.wide
                at = rows_of(idx[(h * sh.blocks + j) * slots + s], length)
                piece = value[s * length : (s + 1) * length, t * tile : (t + 1) * tile]
                if sh.wide > 1:
                    lane = lax.broadcasted_iota(jnp.int32, piece.shape, 1) // sh.head_size
                    piece = jnp.where(lane == i, piece, 0.0)
                ref[at, t * tile : (t + 1) * tile] += piece

    def blocks_from(j, count):
        gained = [block(j + u) for u in range(count)]
        for which, ref in ((0, ka_scr), (1, va_scr)):

            def slot(u, s):
                return gained[u][which][s * length : (s + 1) * length]

            for n in range(count + 2):
                total = None
                for u in range(count):
                    if 0 <= n - u <= 2:
                        total = slot(u, n - u) if total is None else total + slot(u, n - u)
                ref[rows_of(j - 1 + n, length), :] += total
            for s, target in ((3, 0), (4, c - 1)):
                total = slot(0, s)
                for u in range(1, count):
                    total = total + slot(u, s)
                ref[rows_of(target, length), :] += total
            for u in range(count):
                random_add(ref, j + u, gained[u][which])

    steps = (c - 2) // unroll
    shares = [-(-steps * n // parts) * unroll for n in (part, part + 1)]
    begin, end = shares
    if part == parts - 1:
        end = c - 2
    each_block(1 + begin, end - begin, unroll, blocks_from)

    chunks = sh.span // sh.chunk
    for j in (0, c - 1)[2 * part // parts : 2 * (part + 1) // parts]:
        at = rows_of(j, length)
        q_all = spread_heads(rows[at, query : query + sh.lanes], sh)
        g_all = spread_heads(grads[at, :], sh)
        log_row = log_ref[pl.ds(j, 1), :]

        def probs_of(keys):
            scores = contract_cols(rows[keys, key : key + sh.lanes], q_all) * scale
            return jnp.exp2(scores + widen(bias_ref[keys, : sh.bias_lanes], sh) - log_row)

        def scan(i, delta):
            keys = rows_of(i, sh.chunk)
            prob_grad = contract_cols(rows[keys, value : value + sh.lanes], g_all)
            p_scr[keys, :] = prob_grad
            return delta + jnp.sum(probs_of(keys) * prob_grad, axis=0, keepdims=True)

        delta = jnp.zeros((1, sh.columns), jnp.float32)
        delta = lax.fori_loop(0, chunks, scan, delta, unroll=2 - chunks % 2)

        def chunk(i, total):
            keys = rows_of(i, sh.chunk)
            probs = probs_of(keys)
            score_grad = low(probs * (p_scr[keys, :] - delta))
            ka_scr[keys, :] += matmul(score_grad, q_all)
            va_scr[keys, :] += matmul(low(probs), g_all)
            return total + contract_rows(score_grad, rows[keys, key : key + sh.lanes])

        total = jnp.zeros((sh.columns, sh.lanes), jnp.float32)
        total = lax.fori_loop(0, chunks, chunk, total, unroll=2 - chunks % 2)
        d_scr[at, : sh.lanes] = low(pick_heads(total, sh) * factor)

    for copy in carries:
        copy.wait()

    def with_carried(first, values):
        return values + full(refs[7][:, first : first + sh.lanes]) if part else values

    if part:
        d_scr[:, : sh.lanes] = d_scr[:, : sh.lanes] + refs[7][:, : sh.lanes]
    d_scr[:, key : key + sh.lanes] = low(with_carried(key, ka_scr[...] * factor))
    d_scr[:, value : value + sh.lanes] = low(with_carried(value, va_scr[...]))
    stores = [
        pltpu.make_async_copy(d_scr.at[place(r)], outs[r], sems.at[2 * pieces + r])
        for r in range(pieces)
    ]
    for copy in stores:
        copy.start()
    for copy in stores:
        copy.wait()


ANYWHERE = pl.BlockSpec(memory_space=pl.ANY)
ON_CHIP = pl.BlockSpec(memory_space=pltpu.VMEM)
SCALARS = pl.BlockSpec(memory_space=pltpu.SMEM)


def cost(flops, accessed=10**6):
    return pl.CostEstimate(flops=int(flops), bytes_accessed=int(accessed), transcendentals=0)


def attend_cost(sh, weight):
    return cost(weight * sh.blocks * sh.slots * sh.length * sh.columns * sh.lanes)


def attend_forward(sh, packed, lists, weight=16, unroll=15):
    pieces = len(packed)
    used, member, idx, bidx, bias = lists
    rows_each = sh.span // pieces
    outs = pl.pallas_call(
        functools.partial(forward_kernel, sh, pieces, unroll),
        in_specs=[SCALARS] * 4 + [ANYWHERE] * pieces + [ON_CHIP],
        out_specs=[ANYWHERE] * pieces + [ON_CHIP],
        out_shape=[jax.ShapeDtypeStruct((rows_each, sh.lanes), jnp.bfloat16)] * pieces
        + [jax.ShapeDtypeStruct((sh.blocks, sh.columns), jnp.float32)],
        scratch_shapes=[
            pltpu.VMEM((sh.span, 3 * sh.lanes), jnp.bfloat16),
            pltpu.VMEM((sh.span, sh.lanes), jnp.bfloat16),
            pltpu.VMEM((2, sh.span, sh.columns), jnp.float32),
            pltpu.SemaphoreType.DMA((2 * pieces,)),
        ],
        compiler_params=pltpu.CompilerParams(vmem_limit_bytes=34 * MEGA),
        cost_estimate=attend_cost(sh, weight),
        name="attend_forward",
    )(used, member, idx, bidx, *packed, bias)
    return outs[:pieces], outs[pieces]


def attend_backward(sh, packed, tops, log_rows, lists, part=(0, 1), carried=(), weight=32, unroll=4):
    pieces = len(packed)
    used, member, idx, bidx, bias = lists
    rows_each = sh.span // pieces
    return pl.pallas_call(
        functools.partial(backward_kernel, sh, pieces, unroll, part),
        in_specs=[SCALARS] * 4
        + [ANYWHERE] * (2 * pieces)
        + [ON_CHIP] * 2
        + [ANYWHERE] * len(carried),
        out_specs=[ANYWHERE] * pieces,
        out_shape=[jax.ShapeDtypeStruct((rows_each, 3 * sh.lanes), jnp.bfloat16)] * pieces,
        scratch_shapes=[
            pltpu.VMEM((sh.span, 3 * sh.lanes), jnp.bfloat16),
            pltpu.VMEM((sh.span, sh.lanes), jnp.bfloat16),
            pltpu.VMEM((sh.span, 3 * sh.lanes), jnp.bfloat16),
            pltpu.VMEM((sh.span, sh.lanes), jnp.float32),
            pltpu.VMEM((sh.span, sh.lanes), jnp.float32),
            pltpu.VMEM((sh.span, sh.columns), jnp.float32),
            pltpu.SemaphoreType.DMA((4 * pieces,)),
        ]
        + [pltpu.VMEM((sh.span, 3 * sh.lanes), jnp.bfloat16)] * (len(carried) > 0),
        compiler_params=pltpu.CompilerParams(
            vmem_limit_bytes=(42 if carried else 36) * MEGA
        ),
        cost_estimate=attend_cost(sh, weight // part[1]),
        name="attend_backward",
    )(used, member, idx, bidx, *packed, *tops, bias, log_rows, *carried)


GELU_A = (2 / 3.141592653589793) ** 0.5
GELU_B = GELU_A * 0.044715


def gelu_both(pre):
    square = pre * pre
    turn = jnp.tanh(pre * (GELU_A + GELU_B * square))
    half = 0.5 + 0.5 * turn
    act = pre * half
    slope = half + act * (1.0 - turn) * (GELU_A + 3.0 * GELU_B * square)
    return act, slope


def unit_of(rows):
    center = jnp.mean(rows, axis=1, keepdims=True)
    deviation = rows - center
    inverse = lax.rsqrt(jnp.mean(deviation * deviation, axis=1, keepdims=True) + EPSILON)
    return deviation * inverse, inverse


def norm_grad(grad_normed, unit, inverse, gain):
    scaled = grad_normed * gain
    plain_mean = jnp.mean(scaled, axis=1, keepdims=True)
    cross_mean = jnp.mean(scaled * unit, axis=1, keepdims=True)
    return inverse * (scaled - plain_mean - unit * cross_mean)


def column_sum(values):
    return jnp.sum(values, axis=0, keepdims=True)


def take(refs, count):
    return refs[:count], refs[count:]


def tiled(tile, cols, first=0):
    return pl.BlockSpec((tile, cols), lambda i: (first + i, 0))


def line(cols):
    return pl.BlockSpec((1, cols), lambda i: (0, 0))


def line_out(cols):
    return jax.ShapeDtypeStruct((1, cols), jnp.float32)


def rows_out(rows, cols, dtype=jnp.bfloat16):
    return jax.ShapeDtypeStruct((rows, cols), dtype)


def middle_kernel(count, outs_count, head, tail, offsets, *refs):
    (cot_ref, bias_ref), refs = take(refs, 2)
    if head:
        (resid_ref, outer_bias_ref, gain_ref, shift_ref), refs = take(refs, 4)
        merged, refs = take(refs, outs_count)
    else:
        (second_in, total_in, back_in), refs = take(refs, 3)
    if tail:
        (middle_in, gain_in), refs = take(refs, 2)
    out_w, refs = take(refs, outs_count if head or tail else 0)
    inner_w, refs = take(refs, count)
    outer_w, refs = take(refs, count)
    if head:
        (second_ref, middle_ref, joined_ref), refs = take(refs, 3)
    if tail:
        (outputs_ref, grad_ref, branch_ref, gain_sum, shift_sum, cot_sum), refs = take(refs, 6)
        tops, refs = take(refs, outs_count)
    else:
        (total_ref, back_ref), refs = take(refs, 2)
    (bias_sum,), refs = take(refs, 1)
    acts, refs = take(refs, count)
    inner_grads, refs = take(refs, count)
    out_scr, inner_scr, outer_scr, total_scr, back_scr, sems = refs
    step = pl.program_id(0)
    model, width = inner_scr.shape[1:]
    out_copies = []
    for i, ref in enumerate(out_w):
        lanes = out_scr.shape[0] // outs_count
        out_copies.append(
            pltpu.make_async_copy(
                ref.at[pl.ds(offsets[0][i], lanes)], out_scr.at[pl.ds(i * lanes, lanes)], sems.at[i]
            )
        )
    copies = []
    for i in range(count):
        n = outs_count + 2 * i
        inner = inner_w[i].at[pl.ds(offsets[1][i], model)]
        outer = outer_w[i].at[pl.ds(offsets[2][i], width)]
        copies.append(
            [
                pltpu.make_async_copy(inner, inner_scr.at[i], sems.at[n]),
                pltpu.make_async_copy(outer, outer_scr.at[i], sems.at[n + 1]),
            ]
        )

    @pl.when(step == 0)
    def _():
        for copy in out_copies if head else []:
            copy.start()
        for pair in copies:
            for copy in pair:
                copy.start()
        for copy in [] if head else out_copies:
            copy.start()
        for ref in (bias_sum, gain_sum, shift_sum, cot_sum) if tail else (bias_sum,):
            ref[...] = jnp.zeros_like(ref)

    def body(first_step):
        def ready(group):
            if first_step:
                for copy in group:
                    copy.wait()

        cot = cot_ref[...]
        if head:
            ready(out_copies)
            joined = jnp.concatenate([ref[...] for ref in merged], axis=1)
            joined_ref[...] = joined
            middle = full(resid_ref[...]) + matmul(joined, out_scr[...])
            middle_ref[...] = middle
            unit, _ = unit_of(middle)
            second = low(unit * gain_ref[...] + shift_ref[...])
            second_ref[...] = second
            total_scr[...] = middle + outer_bias_ref[...]
        else:
            second = second_in[...]
            total_scr[...] = total_in[...]
            back_scr[...] = back_in[...]
        for i in range(count):
            ready(copies[i])
            pre = matmul(second, inner_scr[i]) + bias_ref[:, i * width : (i + 1) * width]
            grad = contract_cols(cot, outer_scr[i])
            act, slope = gelu_both(pre)
            act = low(act)
            acts[i][...] = act
            grad = grad * slope
            bias_sum[:, i * width : (i + 1) * width] += column_sum(grad)
            grad = low(grad)
            inner_grads[i][...] = grad
            total_scr[...] += matmul(act, outer_scr[i])
            back = contract_cols(grad, inner_scr[i])
            if head and i == 0:
                back_scr[...] = back
            else:
                back_scr[...] += back
        if not tail:
            total_ref[...] = total_scr[...]
            back_ref[...] = back_scr[...]
            return
        outputs_ref[...] = low(total_scr[...])
        second_grad = back_scr[...]
        unit, inverse = unit_of(middle_in[...])
        cot_wide = full(cot)
        middle_grad = cot_wide + norm_grad(second_grad, unit, inverse, gain_in[...])
        gain_sum[...] += column_sum(second_grad * unit)
        shift_sum[...] += column_sum(second_grad)
        cot_sum[...] += column_sum(cot_wide)
        grad_ref[...] = middle_grad
        branch = low(middle_grad)
        branch_ref[...] = branch
        ready([] if head else out_copies)
        top = low(contract_cols(branch, out_scr[...]))
        at = 0
        for ref in tops:
            ref[...] = top[:, at : at + ref.shape[1]]
            at += ref.shape[1]

    @pl.when(step == 0)
    def _():
        body(True)

    @pl.when(step > 0)
    def _():
        body(False)


def run_middle(cot, bias, inner_w, outer_w, out_w, head=None, carried=None, tail=None):
    rows, model = cot.shape
    count, outs_count = len(inner_w), len(out_w)
    tile = min(ROW_TILE, rows)
    width = bias.shape[1] // count
    lanes = model // outs_count
    args, in_specs = [cot, bias], [tiled(tile, model), line(count * width)]
    if head is not None:
        resid, lines, merged = head
        args += [resid, *lines, *merged]
        in_specs += [tiled(tile, model)] + [line(model)] * 3 + [tiled(tile, lanes)] * outs_count
    else:
        args += carried
        in_specs += [tiled(tile, model)] * 3
    if tail is not None:
        args += tail
        in_specs += [tiled(tile, model), line(model)]
    used_out = out_w if head is not None or tail is not None else []
    weights = [*used_out, *inner_w, *outer_w]
    args += [array for array, _ in weights]
    in_specs += [ANYWHERE] * len(weights)
    offsets = [[first for _, first in group] for group in (used_out, inner_w, outer_w)]
    out_specs, out_shape = [], []

    def result(cols, dtype=jnp.bfloat16):
        out_specs.append(tiled(tile, cols))
        out_shape.append(rows_out(rows, cols, dtype))

    if head is not None:
        result(model)
        result(model, jnp.float32)
        result(model)
    if tail is not None:
        result(model)
        result(model, jnp.float32)
        result(model)
        for _ in range(3):
            out_specs.append(line(model))
            out_shape.append(line_out(model))
        for _ in range(outs_count):
            result(lanes)
    else:
        result(model, jnp.float32)
        result(model, jnp.float32)
    out_specs.append(line(count * width))
    out_shape.append(line_out(count * width))
    for _ in range(2 * count):
        result(width)
    outs = pl.pallas_call(
        functools.partial(
            middle_kernel, count, outs_count, head is not None, tail is not None, offsets
        ),
        grid=(rows // tile,),
        in_specs=in_specs,
        out_specs=out_specs,
        out_shape=out_shape,
        scratch_shapes=[
            pltpu.VMEM((model, model), jnp.bfloat16),
            pltpu.VMEM((count, model, width), jnp.bfloat16),
            pltpu.VMEM((count, width, model), jnp.bfloat16),
            pltpu.VMEM((tile, model), jnp.float32),
            pltpu.VMEM((tile, model), jnp.float32),
            pltpu.SemaphoreType.DMA((outs_count + 2 * count,)),
        ],
        compiler_params=pltpu.CompilerParams(vmem_limit_bytes=31 * MEGA),
        cost_estimate=cost(rows * model),
        name="middle",
    )(*args)
    plain, bias_sums = outs[: -2 * count - 1], outs[-2 * count - 1]
    return plain, bias_sums, outs[-2 * count : -count], outs[-count:]


def bundle_kernel(count, *refs):
    sources, target, (held, sems) = refs[:count], refs[count], refs[count + 1 :]
    loads, stores, at = [], [], 0
    for i, source in enumerate(sources):
        rows = pl.ds(at, source.shape[0])
        at += source.shape[0]
        loads.append(pltpu.make_async_copy(source, held.at[rows], sems.at[i]))
        stores.append(pltpu.make_async_copy(held.at[rows], target.at[rows], sems.at[count + i]))
    for copy in loads:
        copy.start()
    for load, store in zip(loads, stores):
        load.wait()
        store.start()
    for copy in stores:
        copy.wait()


def run_bundle(arrays):
    rows, cols = sum(array.shape[0] for array in arrays), arrays[0].shape[1]
    return pl.pallas_call(
        functools.partial(bundle_kernel, len(arrays)),
        in_specs=[ANYWHERE] * len(arrays),
        out_specs=ANYWHERE,
        out_shape=rows_out(rows, cols),
        scratch_shapes=[
            pltpu.VMEM((rows, cols), jnp.bfloat16),
            pltpu.SemaphoreType.DMA((2 * len(arrays),)),
        ],
        compiler_params=pltpu.CompilerParams(vmem_limit_bytes=58 * MEGA),
        cost_estimate=cost(rows * cols),
        name="bundle",
    )(*arrays)


def add_kernel(count, *refs):
    at = 0
    for group in (refs[:count], refs[count : 2 * count]):
        total = full(group[0][...])
        for ref in group[1:]:
            total = total + full(ref[...])
        refs[-1][at : at + total.shape[0], :] = low(total)
        at += total.shape[0]


def run_add(firsts, seconds):
    count, cols = len(firsts), firsts[0].shape[1]
    return pl.pallas_call(
        functools.partial(add_kernel, count),
        in_specs=[ON_CHIP] * (2 * count),
        out_specs=ON_CHIP,
        out_shape=rows_out(firsts[0].shape[0] + seconds[0].shape[0], cols),
        compiler_params=pltpu.CompilerParams(vmem_limit_bytes=14 * MEGA),
        cost_estimate=cost(10**6, 8 * firsts[0].shape[0] * cols),
        name="add",
    )(*firsts, *seconds)


def first_kernel(resid_ref, gain_ref, shift_ref, weight_ref, normed_ref, packed_ref):
    unit, _ = unit_of(full(resid_ref[...]))
    normed = low(unit * gain_ref[...] + shift_ref[...])
    normed_ref[...] = normed
    packed_ref[...] = low(contract_cols(normed, weight_ref[...]))


def run_first(resid, gain, shift, weight):
    rows, model = resid.shape
    tile = min(ROW_TILE, rows)
    cols = weight.shape[0]
    return pl.pallas_call(
        first_kernel,
        grid=(rows // tile,),
        in_specs=[
            tiled(tile, model),
            line(model),
            line(model),
            pl.BlockSpec((cols, model), lambda i: (0, 0), pipeline_mode=pl.Buffered(1)),
        ],
        out_specs=[tiled(tile, model), tiled(tile, cols)],
        out_shape=[rows_out(rows, model), rows_out(rows, cols)],
        compiler_params=pltpu.CompilerParams(vmem_limit_bytes=14 * MEGA),
        cost_estimate=cost(rows * model),
        name="first",
    )(resid, gain, shift, weight)


def project_kernel(rows_ref, weight_ref, packed_ref):
    packed_ref[...] = low(contract_cols(rows_ref[...], weight_ref[...]))


def run_project(rows_in, weight):
    rows, model = rows_in.shape
    tile = min(2 * ROW_TILE, rows)
    cols = weight.shape[0]
    return pl.pallas_call(
        project_kernel,
        grid=(rows // tile,),
        in_specs=[
            tiled(tile, model),
            pl.BlockSpec((cols, model), lambda i: (0, 0), pipeline_mode=pl.Buffered(1)),
        ],
        out_specs=tiled(tile, cols),
        out_shape=rows_out(rows, cols),
        compiler_params=pltpu.CompilerParams(vmem_limit_bytes=12 * MEGA),
        cost_estimate=cost(rows * model),
        name="project",
    )(rows_in, weight)


def last_kernel(parts, *refs):
    (resid_ref, grad_ref, gain_ref), refs = take(refs, 3)
    packed, refs = take(refs, parts)
    joint_w, refs = take(refs, parts)
    out_ref, gain_sum, shift_sum, joint_scr, sems = refs[-5:]
    step = pl.program_id(0)
    copies = [
        pltpu.make_async_copy(joint_w[i], joint_scr.at[i], sems.at[i]) for i in range(parts)
    ]

    @pl.when(step == 0)
    def _():
        for copy in copies:
            copy.start()
        gain_sum[...] = jnp.zeros_like(gain_sum)
        shift_sum[...] = jnp.zeros_like(shift_sum)
        for copy in copies:
            copy.wait()

    unit, inverse = unit_of(full(resid_ref[...]))
    joined = jnp.concatenate([ref[...] for ref in packed], axis=1)
    first_grad = matmul(joined, joint_scr[...].reshape(joined.shape[1], joint_scr.shape[2]))
    out_ref[...] = grad_ref[...] + norm_grad(first_grad, unit, inverse, gain_ref[...])
    gain_sum[...] += column_sum(first_grad * unit)
    shift_sum[...] += column_sum(first_grad)


def run_last(part, part_rows, resid, middle_grad, gain, packed, joint_w, made):
    parts = len(packed)
    rows, model = resid.shape
    tile = min(ROW_TILE, part_rows)
    depth = packed[0].shape[1]
    first = part * part_rows // tile
    return pl.pallas_call(
        functools.partial(last_kernel, parts),
        grid=(part_rows // tile,),
        in_specs=[tiled(tile, model, first)] * 2
        + [line(model)]
        + [tiled(tile, depth, first)] * parts
        + [ANYWHERE] * parts
        + [ANYWHERE] * (made is not None),
        out_specs=[tiled(tile, model, first)] + [line(model)] * 2,
        out_shape=[rows_out(rows, model, jnp.float32)] + [line_out(model)] * 2,
        scratch_shapes=[
            pltpu.VMEM((parts, depth, model), jnp.bfloat16),
            pltpu.SemaphoreType.DMA((parts,)),
        ],
        input_output_aliases={} if made is None else {3 + 2 * parts: 0},
        compiler_params=pltpu.CompilerParams(vmem_limit_bytes=20 * MEGA),
        cost_estimate=cost(2 * part_rows * model * parts * depth, part_rows * model * 20),
        name="last",
    )(resid, middle_grad, gain, *packed, *joint_w, *([] if made is None else [made]))


def swap(values, axis, bit):
    size = lax.axis_size(axis)
    return lax.ppermute(values, axis, [(i, i ^ bit) for i in range(size)])


def after(values, *earlier):
    return lax.optimization_barrier((values, earlier))[0]


def put_halves(upper, mine, other):
    return jnp.where(
        upper == 0,
        jnp.concatenate([mine, other], axis=0),
        jnp.concatenate([other, mine], axis=0),
    )


def half(values, upper):
    rows = values.shape[0] // 2
    return lax.dynamic_slice_in_dim(values, upper * rows, rows, 0)


class GroupSum:
    def __init__(self, values, which=(0, 1), pairs=True):
        bits = [1 << i for i in range(lax.axis_size("dp").bit_length() - 1)]
        orders = []
        for order in (bits, bits[1:2] + bits[:1] + bits[2:]):
            if not pairs:
                orders.append([(bit,) for bit in order])
                continue
            odd = len(order) % 2
            groups = [order[:odd]] + [order[i : i + 2] for i in range(odd, len(order), 2)]
            orders.append([tuple(group) for group in groups if group])
        orders = [orders[n] for n in which]
        part = values.shape[0] // len(orders)
        self.parts = [values[n * part : (n + 1) * part] for n in range(len(orders))]
        self.steps = [
            [(True, group) for group in order] + [(False, group) for group in order[::-1]]
            for order in orders
        ]
        self.pending = None

    def start(self):
        self.pending, sent = [], []
        if not self.steps[0]:
            return tuple(self.parts)
        for values, steps in zip(self.parts, self.steps):
            halving, group = steps.pop(0)
            uppers = [(lax.axis_index("dp") // bit) % 2 for bit in group]
            others = []
            for k in range(1, 1 << len(group)):
                flips = [k >> i & 1 for i in range(len(group))]
                leaving = values
                if halving:
                    for upper, flip in zip(uppers[::-1], flips[::-1]):
                        leaving = half(leaving, 1 - upper if flip else upper)
                sent.append(leaving)
                bit = sum(bit for bit, flip in zip(group, flips) if flip)
                others.append(swap(leaving, "dp", bit))
            if halving:
                for upper in uppers[::-1]:
                    values = half(values, upper)
            self.pending.append((halving, uppers, values, others))
        return tuple(sent)

    def finish(self, *earlier):
        if not self.pending:
            return
        self.parts = []
        for halving, uppers, mine, others in self.pending:
            if earlier:
                others = after(others, *earlier)
            if halving:
                total = full(mine)
                for other in others:
                    total = total + full(other)
                self.parts.append(low(total))
            else:
                pieces = [mine, *others]
                for upper in uppers:
                    pieces = [
                        put_halves(upper, pieces[n], pieces[n + 1])
                        for n in range(0, len(pieces), 2)
                    ]
                self.parts += pieces
        self.pending = None

    def step(self, *earlier):
        self.finish(*earlier)
        return self.start()

    def result(self, cuts=()):
        while self.steps[0] or (self.pending and not cuts):
            self.step()
        if not cuts:
            return full(jnp.concatenate(self.parts, axis=0))
        ((_, uppers, mine, others),) = self.pending
        if len(uppers) > 1:
            self.finish()
            halves = self.parts
        else:
            halves = [
                jnp.where(uppers[0] == 0, mine, others[0]),
                jnp.where(uppers[0] == 0, others[0], mine),
            ]
        edges, outs = [0, *cuts, sum(half.shape[0] for half in halves)], []
        for low_at, high_at in zip(edges, edges[1:]):
            pieces, first = [], 0
            for rows in halves:
                a, b = max(low_at - first, 0), min(high_at - first, rows.shape[0])
                if a < b:
                    pieces.append(rows[a:b])
                first += rows.shape[0]
            outs.append(full(jnp.concatenate(pieces, axis=0)))
        return outs


def sum_all(values):
    for axis in ("tensor", "dp"):
        bits = [1 << i for i in range(lax.axis_size(axis).bit_length() - 1)]
        bits = bits[len(bits) % 2 :] + bits[: len(bits) % 2]
        for i in range(0, len(bits) - 1, 2):
            others = [
                swap(values, axis, bit) for bit in (bits[i], bits[i + 1], bits[i] ^ bits[i + 1])
            ]
            values = (values + others[0]) + (others[1] + others[2])
        if len(bits) % 2:
            values = values + swap(values, axis, bits[-1])
    return values


def split_exact(values):
    terms = []
    for _ in range(3):
        term = lax.reduce_precision(values, 8, 7)
        terms.append(low(term))
        values = values - term
    return terms


def per_device(
    inputs,
    query_weight,
    key_weight,
    value_weight,
    output_weight,
    inner_weight,
    inner_bias,
    outer_weight,
    outer_bias,
    first_gain,
    first_shift,
    second_gain,
    second_shift,
    item_lengths,
    key_mask,
    random_blocks,
    cotangent,
):
    tensor = lax.axis_size("tensor")
    items = item_lengths.shape[0]
    local_rows, model = inputs.shape
    span = local_rows * tensor // items
    members = tensor // items
    place = lax.axis_index("tensor")
    item, member = place // members, place % members
    heads, blocks = random_blocks.shape[1], random_blocks.shape[2]
    lanes = query_weight.shape[0]
    length = span // blocks
    sh = Shape(span, heads, lanes // heads, blocks, SHARED + random_blocks.shape[3])

    def from_item(values, step):
        if step % items == 0:
            return values
        pairs = [
            (t, (t // members - step) % items * members + t % members) for t in range(tensor)
        ]
        return lax.ppermute(values, "tensor", pairs)

    def from_member(values, step):
        if step % members == 0:
            return values
        pairs = [
            (t, t // members * members + (t % members - step) % members) for t in range(tensor)
        ]
        return lax.ppermute(values, "tensor", pairs)

    order = [(s, r) for s in range(items) for r in range(members)]
    away = range(1, items)
    joint = run_bundle([query_weight, key_weight, value_weight])
    upper = lax.axis_index("dp") % 2
    joint_halves = [from_item(half(joint, upper), s) for s in away]

    lines = (first_gain.reshape(1, -1), first_shift.reshape(1, -1))
    firsts = [run_first(from_member(inputs, r), *lines, joint) for r in range(members)]
    first_all = [normed for normed, _ in firsts]

    width = inner_weight.shape[1]
    bias_rows = jnp.stack(split_exact(inner_bias))
    bias_rows = jnp.concatenate([bias_rows, jnp.zeros((13, width), jnp.bfloat16)], axis=0)
    own_weights = [output_weight, inner_weight, outer_weight, bias_rows]
    if width == model:
        sent = [run_bundle([output_weight, outer_weight, bias_rows]), inner_weight]
        views = [(0, 0), (1, 0), (0, lanes), (0, lanes + width)]
    else:
        sent = own_weights
        views = [(n, 0) for n in range(len(own_weights))]

    used = lax.dynamic_index_in_dim(item_lengths, item, 0, False) // length
    flags = lax.dynamic_index_in_dim(key_mask.reshape(items, span), item, 0, False)
    key_ok = (jnp.arange(span, dtype=jnp.int32) < used * length) & (flags == 1)
    bias = jnp.where(jnp.concatenate([key_ok, jnp.zeros((length,), bool)]), 0.0, MASKED)
    bias = jnp.broadcast_to(full(bias)[:, None], (span + length, 128))
    picks = [
        from_item(lax.dynamic_index_in_dim(random_blocks, (item - s) % items, 0, False), s)
        for s in range(items)
    ]
    chosen, usable = jax.vmap(lambda pick: block_lists(used, pick))(jnp.concatenate(picks))
    marked = jnp.where(usable, chosen, blocks)
    chosen, marked = chosen.reshape(items, -1), marked.reshape(items, -1)
    lists = [
        (used.reshape(1), member.reshape(1), chosen[s], marked[s], bias) for s in range(items)
    ]

    packed, made, merged, logs, joint_item = [], [], [], [], [joint]
    rows_in = first_all
    for s in range(items):
        if s == 0:
            group = [packed_rows for _, packed_rows in firsts]
            sent = after(sent, joint_halves)
            joint_others = [swap(rows, "dp", 1) for rows in joint_halves]
            own_sent = after(sent, group[-1])
            own_parts = {
                r: [from_member(array, -r) for array in own_sent] for r in range(1, members)
            }
            item_sent = [own_sent] + [[from_item(array, t) for array in sent] for t in away]
        else:
            halves = after((joint_halves[s - 1], joint_others[s - 1]), made[s - 1][0])
            weight = put_halves(upper, *halves)
            joint_item.append(weight)
            group = [run_project(rows, weight) for rows in rows_in]
        packed.append(group)
        outs, log_rows = attend_forward(sh, after(group, sent, joint_halves), lists[s], 0 if s else 64)
        made.append(outs)
        logs.append(log_rows)
        merged += [from_member(outs[r], -r) for r in range(members)]
        rows_in = after(first_all, outs[0], [arrays[0] for arrays in own_parts.values()])

    part_weights = {}
    for s, r in order:
        if (s, r) == (0, 0):
            part_weights[s, r] = [(array, 0) for array in own_weights]
        else:
            arrays = own_parts[r] if s == 0 else None
            if s:
                early = item_sent[s][:1] if width == model else item_sent[s]
                arrays = [from_member(array, -r) for array in after(early, made[-1][0])]
                arrays += item_sent[s][len(early) :]
            part_weights[s, r] = [(arrays[n], row) for n, row in views]

    def part_bias(part):
        if part == (0, 0):
            return inner_bias.reshape(1, -1)
        array, row = part_weights[part][3]
        terms = full(array[row : row + 3])
        return (terms[0] + terms[1] + terms[2]).reshape(1, -1)

    groups = [
        [(0, 0)],
        [part for part in order if part[0] > 0],
        [(0, r) for r in range(1, members)],
    ]
    groups = [group for group in groups if group]
    out_full = [part_weights[part][0] for part in order]
    acts, inner_grads, bias_sums = {}, {}, {}

    def outer_product(part):
        return contract_rows(acts[part], cotangent)

    def inner_product(part):
        return contract_rows(second_own, inner_grads[part])

    def output_product(part):
        at = order.index(part) * lanes
        return output_grads[at : at + lanes]

    def send_members(product, s):
        return [from_member(low(product((s, r))), r) for r in range(members - 1, 0, -1)]

    def add_members(product, s, others):
        total = product((s, 0))
        for other in others:
            total = total + full(other)
        return low(total)

    totals = {}
    carried, waits = None, ()
    for n, group in enumerate(groups):
        head = tail = None
        if n == 0:
            lines = [row.reshape(1, -1) for row in (outer_bias, second_gain, second_shift)]
            head = (inputs, lines, merged)
        if n == len(groups) - 1:
            tail = [middle, second_gain.reshape(1, -1)]
        inner_parts = [part_weights[part][1] for part in group]
        if n == 1 and width == model:
            late = after([item_sent[s][1] for s in range(items)], acts[0, 0])
            inner_parts = [(from_member(late[s], -r), 0) for s, r in group]
        plain, group_bias, group_acts, group_grads = run_middle(
            cotangent,
            jnp.concatenate([part_bias(part) for part in group], axis=1),
            inner_parts,
            [part_weights[part][2] for part in group],
            out_full,
            head,
            after(carried, waits) if carried else None,
            tail,
        )
        for i, part in enumerate(group):
            acts[part], inner_grads[part] = group_acts[i], group_grads[i]
            bias_sums[part] = group_bias[:, i * width : (i + 1) * width]
        if n == 0:
            second_own, middle, joined = plain[:3]
            plain = plain[3:]
        if n < len(groups) - 1:
            carried = [second_own, *plain]
        waits = []
        for s in sorted({s for s, _ in group if s > 0}, reverse=True):
            for name, product in (("outer", outer_product), ("inner", inner_product)):
                totals[name, s] = add_members(product, s, send_members(product, s))
                waits.append(totals[name, s])
    outputs, middle_grad, branch, second_gain_sum, second_shift_sum, cot_sum = plain[:6]
    tops = plain[6:]
    output_grads = contract_rows(joined, branch)

    top_rows = [[None] * members for _ in range(items)]
    for i, (s, r) in enumerate(order):
        top_rows[s][r] = from_member(tops[i], r)
    products = {"outer": outer_product, "inner": inner_product, "output": output_product}
    item_sent = {
        name: [from_item(totals[name, s], -s) for s in away] for name in ("outer", "inner")
    }
    member_sent = {name: send_members(product, 0) for name, product in products.items()}
    totals["outer", 0] = add_members(outer_product, 0, member_sent["outer"])
    for s in range(items - 1, -1, -1):
        others = send_members(output_product, s) if s else member_sent["output"]
        totals["output", s] = add_members(output_product, s, others)
    item_sent["output"] = [from_item(totals["output", s], -s) for s in away]

    def add_items(total, others):
        total = full(total)
        for other in others:
            total = total + full(other)
        return low(total)

    packed_grad, joint_totals = [None] * items, [None] * items
    outer_sum = GroupSum(
        add_items(totals["outer", 0], after(item_sent["outer"], branch)), (0,), False
    )
    waits = (outer_sum.start(), member_sent, totals["output", 0])
    inner_sum = None
    back, joint_sent = {}, []
    for s in range(items - 1, -1, -1):
        grads = ()
        for part in range(BACK_PARTS):
            if part:
                waits = outer_sum.step(grads[0])
                if inner_sum is None:
                    others, second_own = after((item_sent, second_own), grads[0], waits)
                    totals["inner", 0] = add_members(inner_product, 0, member_sent["inner"])
                    inner_terms = [totals["inner", 0], *others["inner"]]
                    output_terms = [totals["output", 0], *others["output"]]
                    if width == model:
                        inner_total = run_add(inner_terms, output_terms)
                    else:
                        inner_total = add_items(inner_terms[0], inner_terms[1:])
                        output_sum = GroupSum(add_items(output_terms[0], output_terms[1:]), (0,))
                    inner_sum = GroupSum(inner_total, (1,))
                    waits = (waits, inner_sum.start(), outer_sum.step(inner_total))
                else:
                    waits = (waits, inner_sum.step(grads[0]), joint_sent)
            grads = attend_backward(
                sh,
                packed[s],
                after(top_rows[s], waits),
                logs[s],
                lists[s],
                (part, BACK_PARTS),
                grads,
                0 if s == items - 1 and part == 0 else 32,
            )
        packed_grad[s] = grads
        if s:
            rows = after(grads, outer_sum.step(grads[0]))
        else:
            rows = after(grads, inner_sum.step(grads[0]), outer_sum.step(grads[0]))
        total = contract_rows(rows[0], first_all[0])
        for r in range(1, members):
            total = total + contract_rows(rows[r], first_all[r])
        joint_totals[s] = low(total) if s else total
        waits = joint_totals[s]
        if s:
            waits = (waits, outer_sum.step(total), inner_sum.step(total))
            rows = after(grads, waits)
            joint_sent.append(from_item(joint_totals[s], -s))
        grads = rows
        for r in range(members):
            back[s, r] = from_member(grads[r], -r)

    back = [back[part] for part in order]
    joint_full = [from_member(joint_item[s], -r) for s, r in order]
    end_sum = GroupSum(add_items(joint_totals[0], joint_sent), (0,))
    waits = end_sum.start()
    pieces = []
    cut = local_rows // LAST_PARTS
    for n in range(LAST_PARTS):
        outs = run_last(
            n,
            cut,
            inputs,
            middle_grad,
            first_gain.reshape(1, -1),
            after(back, waits),
            joint_full,
            pieces[-1][0] if pieces else None,
        )
        pieces.append(outs)
        if n == 0:
            waits = end_sum.step(outs[1])
    input_grad = pieces[-1][0]
    vectors = [
        sum(piece[1] for piece in pieces),
        sum(piece[2] for piece in pieces),
        second_gain_sum,
        second_shift_sum,
        cot_sum,
    ]
    bias_rows = jnp.zeros((tensor, width), jnp.float32)
    for s, r in order:
        spot = (item + s) % items * members + (member - r) % members
        bias_rows = lax.dynamic_update_slice(bias_rows, bias_sums[s, r], (spot, 0))
    vectors.append(bias_rows)
    vectors = after(vectors, end_sum.step())
    arriving = [others for *_, others in inner_sum.pending]
    vectors = after(vectors, arriving)
    small = sum_all(jnp.concatenate([vector.reshape(-1) for vector in vectors]))
    bias_grad = lax.dynamic_slice_in_dim(small, 5 * model + place * width, width, 0)
    small = small[: 5 * model].reshape(5, model)
    end_grad = end_sum.result((lanes, 2 * lanes))
    outer_grad, inner_grad = outer_sum.result(), inner_sum.result()
    if width == model:
        inner_grad, output_grad = inner_grad[:model], inner_grad[model:]
    else:
        output_grad = output_sum.result()
    return (
        outputs,
        input_grad,
        *end_grad,
        output_grad,
        inner_grad,
        bias_grad,
        outer_grad,
        small[4],
        small[0],
        small[1],
        small[2],
        small[3],
    )


def solution(mesh):
    placed = (
        P(("dp", "tensor"), None),
        P("tensor", None),
        P("tensor", None),
        P("tensor", None),
        P("tensor", None),
        P(None, "tensor"),
        P("tensor"),
        P("tensor", None),
        P(),
        P(),
        P(),
        P(),
        P(),
        P("dp"),
        P("dp"),
        P("dp", "tensor", None, None),
        P(("dp", "tensor"), None),
    )
    return jax.shard_map(
        per_device,
        mesh=mesh,
        in_specs=placed,
        out_specs=(
            P(("dp", "tensor"), None),
            P(("dp", "tensor"), None),
            P("tensor", None),
            P("tensor", None),
            P("tensor", None),
            P("tensor", None),
            P(None, "tensor"),
            P("tensor"),
            P("tensor", None),
            P(),
            P(),
            P(),
            P(),
            P(),
        ),
        check_vma=False,
    )
```
